32 devices in a mesh: rep: 4 (over z), fsdp: 8 (over y, x, core).
Axes of the slice: x: 2, y: 2, z: 4, core: 2. Of those that a mesh axis runs over, the one named last changes fastest.
Arguments:
- tokens: bfloat16 [64, 512, 768], P(('rep', 'fsdp')), may hold values from -6 to 6
- segment_ids: int32 [64, 512], P(('rep', 'fsdp')), may hold values from 0 to 7, never falling along the last dimension, each value on 1 to 128 neighbouring positions
- pairing: int32 [512], replicated, may hold values from 0 to 511, each once
- query_weight: bfloat16 [768, 768], P('fsdp'), may hold values from -0.21875 to 0.21875
- key_weight: bfloat16 [768, 768], P('fsdp'), may hold values from -0.21875 to 0.21875
- value_weight: bfloat16 [768, 768], P('fsdp'), may hold values from -0.21875 to 0.21875
- out_weight: bfloat16 [768, 768], P('fsdp'), may hold values from -0.625 to 0.625
- up_weight: bfloat16 [768, 3072], P('fsdp'), may hold values from -0.21875 to 0.21875
- down_weight: bfloat16 [3072, 768], P('fsdp'), may hold values from -0.109375 to 0.109375
- query_bias: bfloat16 [768], P('fsdp'), may hold values from -3 to 3
- value_bias: bfloat16 [768], P('fsdp'), may hold values from -3 to 3
- out_bias: bfloat16 [768], P('fsdp'), may hold values from -3 to 3
- up_bias: bfloat16 [3072], P('fsdp'), may hold values from -3 to 3
- down_bias: bfloat16 [768], P('fsdp'), may hold values from -3 to 3
- first_gain: bfloat16 [768], P('fsdp'), may hold values from 0.5 to 1.5
- first_shift: bfloat16 [768], P('fsdp'), may hold values from -1 to 1
- second_gain: bfloat16 [768], P('fsdp'), may hold values from 0.5 to 1.5
- second_shift: bfloat16 [768], P('fsdp'), may hold values from -0.5 to 0.5
Outputs:
- layer_output: bfloat16 [64, 512, 768], P(('rep', 'fsdp'))
- grad_tokens: bfloat16 [64, 512, 768], P(('rep', 'fsdp'))
- grad_query_weight: float32 [768, 768], P('fsdp')
- grad_key_weight: float32 [768, 768], P('fsdp')
- grad_value_weight: float32 [768, 768], P('fsdp')
- grad_out_weight: float32 [768, 768], P('fsdp')
- grad_up_weight: float32 [768, 3072], P('fsdp')
- grad_down_weight: float32 [3072, 768], P('fsdp')
- grad_query_bias: float32 [768], P('fsdp')
- grad_value_bias: float32 [768], P('fsdp')
- grad_out_bias: float32 [768], P('fsdp')
- grad_up_bias: float32 [3072], P('fsdp')
- grad_down_bias: float32 [768], P('fsdp')
- grad_first_gain: float32 [768], P('fsdp')
- grad_first_shift: float32 [768], P('fsdp')
- grad_second_gain: float32 [768], P('fsdp')
- grad_second_shift: float32 [768], P('fsdp')
The draws below stay inside these ranges and needn't reach their ends.
Inputs may be any that keep to these rules, and one draw needn't show every extreme that they name: `segment_ids`: within each row the ids never fall, and each of 0 to 7 occurs on 1 to 128 positions. `pairing`: every text number occurs once.
All inputs are finite; a program needn't handle non-finite values.
Results may differ from the reference program's by a relative error of at most 0.015.
Values may be sent and summed in bfloat16 or wider, within the bound.
A program may use at most 192 MiB of HBM per device.

```python
import math
import jax
import jax.numpy as jnp
import numpy as np
from jax import lax

D = 768
H = 12
HD = 64
FF = 3072
LEN = 512
SEGS = 8
MOST = 128
ROWS = 64
NTEXTS = 512


def shard_levels(key, shape, cuts, least, largest):
    factor_of, own = 1.0, jax.random.fold_in(key, 6)
    for position, parts in cuts:
        heights = jnp.exp(jax.random.uniform(jax.random.fold_in(own, position), (parts,), jnp.float32, least / len(cuts), largest / len(cuts)))
        factor_of = factor_of * jnp.repeat(heights, shape[position] // parts).reshape([-1 if axis == position else 1 for axis in range(len(shape))])
    return factor_of


def length_profile(number_of, total, reach, lean):
    loads = [(1 << 20) // math.isqrt(grade ** lean) + 1 for grade in range(2, number_of + 1)]
    spare, given = total - reach - (number_of - 1), [1] * (number_of - 1)
    while spare > 0:
        free = [i for i in range(number_of - 1) if given[i] < reach]
        whole, remaining = sum([loads[i] for i in free]), spare
        for i in free:
            addition = min(reach - given[i], max(1, remaining * loads[i] // whole), spare)
            given[i] = given[i] + addition
            spare = spare - addition
    return np.array([reach] + given)


def uneven(own_key, amount, total, reach, slope):
    if amount == 2:
        one = jax.random.randint(own_key, (), max(1, total - reach), min(reach, total - 1) + 1)
        return jnp.stack([one, total - one])
    tallies = jnp.asarray(length_profile(amount, total, reach, slope), jnp.int32)
    twos = (amount - 1) // 2
    giver, receiver = tallies[1:1 + 2 * twos:2], tallies[2:2 + 2 * twos:2]
    margin = jnp.minimum(giver - 1, reach - receiver)
    moved = jax.random.randint(jax.random.fold_in(own_key, 1), (twos,), 0, 1 << 20) % (margin + 1)
    tallies = tallies.at[1:1 + 2 * twos:2].set(giver - moved).at[2:2 + 2 * twos:2].set(receiver + moved)
    return tallies[jax.random.permutation(jax.random.fold_in(own_key, 2), amount)]


def noise(own_key, dims, scale, reach, split=(), held_as=jnp.bfloat16):
    level = shard_levels(own_key, dims, split, -0.22, 0.18) if split else 1.0
    values = jax.random.normal(own_key, dims, jnp.float32) * scale * level
    return jnp.minimum(jnp.maximum(values, -reach), reach).astype(held_as)


def setup_inputs(seed: int = 0) -> dict:
    arg_keys = jax.random.split(jax.random.key(seed), 19)
    tokens = noise(arg_keys[0], (ROWS, LEN, D), 1.0, 6.0, ((0, 32),))
    segment_ids = jax.vmap(lambda own: jnp.searchsorted(jnp.cumsum(uneven(own, SEGS, LEN, MOST, 2)), jnp.arange(LEN), side="right"))(jax.random.split(arg_keys[1], ROWS)).reshape((ROWS, LEN)).astype(jnp.int32)
    pairing = jax.random.permutation(arg_keys[2], NTEXTS).astype(jnp.int32)
    query_weight = noise(arg_keys[3], (D, D), D ** -0.5, 0.21875, ((0, 8),))
    key_weight = noise(arg_keys[4], (D, D), D ** -0.5, 0.21875, ((0, 8),))
    value_weight = noise(arg_keys[5], (D, D), D ** -0.5, 0.21875, ((0, 8),))
    out_weight = noise(arg_keys[6], (D, D), (D // 8) ** -0.5, 0.625, ((0, 8),))
    up_weight = noise(arg_keys[7], (D, FF), D ** -0.5, 0.21875, ((0, 8),))
    down_weight = noise(arg_keys[8], (FF, D), FF ** -0.5, 0.109375, ((0, 8),))
    query_bias = noise(arg_keys[9], (D,), 0.5, 3.0, ((0, 8),))
    value_bias = noise(arg_keys[10], (D,), 0.5, 3.0, ((0, 8),))
    out_bias = noise(arg_keys[11], (D,), 0.5, 3.0, ((0, 8),))
    up_bias = noise(arg_keys[12], (FF,), 0.5, 3.0, ((0, 8),))
    down_bias = noise(arg_keys[13], (D,), 0.5, 3.0, ((0, 8),))
    first_gain = jnp.clip(1.0 + 0.1 * jax.random.normal(arg_keys[14], (D,), jnp.float32), 0.5, 1.5).astype(jnp.bfloat16)
    first_shift = noise(arg_keys[15], (D,), 0.2, 1.0, ((0, 8),))
    second_gain = jnp.clip(1.0 + 0.1 * jax.random.normal(arg_keys[16], (D,), jnp.float32), 0.5, 1.5).astype(jnp.bfloat16)
    second_shift = noise(arg_keys[17], (D,), 0.1, 0.5, ((0, 8),))
    return {"tokens": tokens, "segment_ids": segment_ids, "pairing": pairing, "query_weight": query_weight, "key_weight": key_weight, "value_weight": value_weight, "out_weight": out_weight, "up_weight": up_weight, "down_weight": down_weight, "query_bias": query_bias, "value_bias": value_bias, "out_bias": out_bias, "up_bias": up_bias, "down_bias": down_bias, "first_gain": first_gain, "first_shift": first_shift, "second_gain": second_gain, "second_shift": second_shift}


@jax.custom_vjp
def low(v):
    return lax.optimization_barrier(v.astype(jnp.bfloat16)).astype(jnp.float32)

@jax.custom_vjp
def low_back(v):
    return v

def low_keep(v):
    return (low(v), None)

def low_pass(kept, grad):
    return (grad,)

def back_keep(v):
    return (v, None)

def back_low(kept, grad):
    return (low(grad),)
low.defvjp(low_keep, low_pass)
low_back.defvjp(back_keep, back_low)

def matmul(left, right):
    return jnp.dot(left, right, precision=lax.Precision.HIGHEST)

def round_both(values_in):
    return low_back(low(values_in))

def norm_piece(residual, gain_vector, shift_vector):
    centre = lax.optimization_barrier(jnp.mean(residual, -1, keepdims=True))
    offset = residual - centre
    spread = lax.optimization_barrier(jnp.mean(offset * offset, -1, keepdims=True))
    return offset * lax.rsqrt(spread + 1e-12) * gain_vector + shift_vector

def gelu_exact(argument):
    return jax.nn.gelu(argument, approximate=False)

def pool_texts(layer_out, segments):
    member = (segments[:, None] == jnp.arange(SEGS)[None, :]).astype(layer_out.dtype)
    totals = jnp.dot(member.T, layer_out, precision=lax.Precision.HIGHEST)
    counts = lax.optimization_barrier(jnp.sum(member, 0))
    pooled = totals / counts[:, None]
    return pooled * lax.rsqrt(lax.optimization_barrier(jnp.sum(pooled * pooled, -1, keepdims=True)) + 1e-06)

@jax.checkpoint
def attend_row(query_states, key_states, value_states, segments):
    row_length = query_states.shape[0]
    query_heads = query_states.reshape(row_length, H, HD)
    key_heads = key_states.reshape(row_length, H, HD)
    value_heads = value_states.reshape(row_length, H, HD)
    scores = jnp.einsum('qhd,khd->hqk', query_heads, key_heads, precision=lax.Precision.HIGHEST) * HD ** (-0.5)
    scores = low_back(scores)
    same_text = segments[:, None] == segments[None, :]
    scores = jnp.where(same_text[None], scores, -1e+30)
    probability = low(jax.nn.softmax(scores, axis=-1))
    mixture = jnp.einsum('hqk,khd->qhd', probability, value_heads, precision=lax.Precision.HIGHEST)
    return mixture.reshape(row_length, H * HD)

def block_embed(block_tokens, params, block_segments):
    query_weight, key_weight, value_weight, out_weight, up_weight, down_weight, query_bias, value_bias, out_bias, up_bias, down_bias, first_gain, first_shift, second_gain, second_shift = params
    row_count = block_tokens.shape[0]
    flat_tokens = block_tokens.reshape(row_count * LEN, D)
    query_states = round_both(matmul(flat_tokens, query_weight) + query_bias)
    key_states = round_both(matmul(flat_tokens, key_weight))
    value_states = round_both(matmul(flat_tokens, value_weight) + value_bias)

    def attend_piece(pieces):
        return attend_row(pieces[0], pieces[1], pieces[2], pieces[3])
    joined = lax.map(attend_piece, (query_states.reshape(row_count, LEN, D), key_states.reshape(row_count, LEN, D), value_states.reshape(row_count, LEN, D), block_segments))
    joined = round_both(joined.reshape(row_count * LEN, D))
    branch = low_back(matmul(joined, out_weight) + out_bias)
    hidden = norm_piece(flat_tokens + branch, first_gain, first_shift)
    expanded = low_back(matmul(low(hidden), up_weight) + up_bias)
    active = low(gelu_exact(expanded))
    feed = low_back(matmul(active, down_weight) + down_bias)
    output = norm_piece(hidden + feed, second_gain, second_shift)
    embedded = jax.vmap(pool_texts)(output.reshape(row_count, LEN, D), block_segments)
    return (output, embedded.reshape(row_count * SEGS, D))

def contrast(embeddings, pairing):
    queries = embeddings[pairing[0::2]]
    passages = embeddings[pairing[1::2]]
    similar = low_back(matmul(queries, passages.T))
    logits = similar * 100.0
    return jnp.sum(jax.nn.logsumexp(logits, axis=1) - jnp.diagonal(logits))

def reference(tokens, segment_ids, pairing, query_weight, key_weight, value_weight, out_weight, up_weight, down_weight, query_bias, value_bias, out_bias, up_bias, down_bias, first_gain, first_shift, second_gain, second_shift):
    params = tuple((piece.astype(jnp.float32) for piece in (query_weight, key_weight, value_weight, out_weight, up_weight, down_weight, query_bias, value_bias, out_bias, up_bias, down_bias, first_gain, first_shift, second_gain, second_shift)))
    block_count = ROWS // 8
    token_blocks = tokens.astype(jnp.float32).reshape(block_count, 8, LEN, D)
    segment_blocks = segment_ids.reshape(block_count, 8, LEN)

    def forward_block(pieces):
        return block_embed(pieces[0], params, pieces[1])
    outputs, embedded = lax.map(forward_block, (token_blocks, segment_blocks))
    rounded = low(embedded.reshape(NTEXTS, D))

    def loss_of(embeddings):
        return contrast(embeddings, pairing)
    loss_value, loss_pullback = jax.vjp(loss_of, rounded)
    grad_embed, = loss_pullback(jnp.ones_like(loss_value))
    grad_blocks = grad_embed.reshape(block_count, 8 * SEGS, D)

    def backward_block(carry, pieces):
        block_tokens, block_segments, block_grad = pieces

        def embed_only(inputs, weights):
            return block_embed(inputs, weights, block_segments)[1]
        unused, pullback = jax.vjp(embed_only, block_tokens, params)
        grad_inputs, grad_params = pullback(block_grad)
        return (jax.tree.map(jnp.add, carry, grad_params), grad_inputs)
    zero_grads = jax.tree.map(jnp.zeros_like, params)
    grad_sums, grad_inputs = lax.scan(backward_block, zero_grads, (token_blocks, segment_blocks, grad_blocks))
    return (outputs.reshape(ROWS, LEN, D).astype(jnp.bfloat16), grad_inputs.reshape(ROWS, LEN, D).astype(jnp.bfloat16), grad_sums[0], grad_sums[1], grad_sums[2], grad_sums[3], grad_sums[4], grad_sums[5], grad_sums[6], grad_sums[7], grad_sums[8], grad_sums[9], grad_sums[10], grad_sums[11], grad_sums[12], grad_sums[13], grad_sums[14])
```

```python
import jax
import jax.numpy as jnp
from jax import lax
from jax.sharding import PartitionSpec as P

H = 12
HD = 64
SEGS = 8


def norm_piece(residual, gain_vector, shift_vector):
    centre = jnp.mean(residual, -1, keepdims=True)
    offset = residual - centre
    spread = jnp.mean(offset * offset, -1, keepdims=True)
    return offset * lax.rsqrt(spread + 1e-12) * gain_vector + shift_vector


def gelu_exact(argument):
    return jax.nn.gelu(argument, approximate=False)


def pool_texts(layer_out, segments):
    member = (segments[:, None] == jnp.arange(SEGS)[None, :]).astype(jnp.float32)
    totals = jnp.dot(member.T, layer_out, precision=lax.Precision.HIGHEST)
    counts = jnp.sum(member, 0)
    pooled = totals / counts[:, None]
    return pooled * lax.rsqrt(jnp.sum(pooled * pooled, -1, keepdims=True) + 1e-06)


def project(inputs, weight, bias_vector):
    return jnp.dot(inputs, weight, preferred_element_type=jnp.float32) + bias_vector.astype(
        jnp.float32
    )


def head_scores(query_states, key_states, segments):
    row_length = query_states.shape[0]
    scores = jnp.einsum(
        "qhd,khd->hqk",
        query_states.reshape(row_length, H, HD),
        key_states.reshape(row_length, H, HD),
        preferred_element_type=jnp.float32,
    ) * HD ** (-0.5)
    same_text = segments[:, None] == segments[None, :]
    return jnp.where(same_text[None], scores, -1e30)


def attend_forward(pieces):
    query_states, key_states, value_states, segments = pieces
    row_length = query_states.shape[0]
    scores = head_scores(query_states, key_states, segments)
    row_peak = jnp.max(scores, -1, keepdims=True)
    exponent = jnp.exp(scores - row_peak)
    row_total = jnp.sum(exponent, -1, keepdims=True)
    probability = (exponent / row_total).astype(jnp.bfloat16)
    mixture = jnp.einsum(
        "hqk,khd->qhd",
        probability,
        value_states.reshape(row_length, H, HD),
        preferred_element_type=jnp.float32,
    )
    return (mixture.reshape(row_length, H * HD).astype(jnp.bfloat16), row_peak + jnp.log(row_total))


def attend_backward(pieces):
    query_states, key_states, value_states, segments, grad_mixture, log_total = pieces
    row_length = query_states.shape[0]
    query_heads = query_states.reshape(row_length, H, HD)
    key_heads = key_states.reshape(row_length, H, HD)
    value_heads = value_states.reshape(row_length, H, HD)
    grad_heads = grad_mixture.reshape(row_length, H, HD)
    probability = jnp.exp(head_scores(query_states, key_states, segments) - log_total)
    grad_probability = jnp.einsum(
        "qhd,khd->hqk", grad_heads, value_heads, preferred_element_type=jnp.float32
    )
    grad_values = jnp.einsum(
        "hqk,qhd->khd",
        probability.astype(jnp.bfloat16),
        grad_heads,
        preferred_element_type=jnp.float32,
    )
    grad_scores = probability * (
        grad_probability - jnp.sum(probability * grad_probability, -1, keepdims=True)
    )
    grad_scores = grad_scores.astype(jnp.bfloat16)
    score_scale = HD ** (-0.5)
    grad_queries = (
        jnp.einsum("hqk,khd->qhd", grad_scores, key_heads, preferred_element_type=jnp.float32)
        * score_scale
    )
    grad_keys = (
        jnp.einsum("hqk,qhd->khd", grad_scores, query_heads, preferred_element_type=jnp.float32)
        * score_scale
    )
    return (
        grad_queries.reshape(row_length, H * HD).astype(jnp.bfloat16),
        grad_keys.reshape(row_length, H * HD).astype(jnp.bfloat16),
        grad_values.reshape(row_length, H * HD).astype(jnp.bfloat16),
    )


def run_layer(tokens, params, segment_ids):
    (
        query_weight,
        key_weight,
        value_weight,
        out_weight,
        up_weight,
        down_weight,
        query_bias,
        value_bias,
        out_bias,
        up_bias,
        down_bias,
        first_gain,
        first_shift,
        second_gain,
        second_shift,
    ) = params
    row_count, row_length, feature_width = tokens.shape
    flat_tokens = tokens.reshape(row_count * row_length, feature_width)
    query_states = project(flat_tokens, query_weight, query_bias).astype(jnp.bfloat16)
    key_states = jnp.dot(flat_tokens, key_weight, preferred_element_type=jnp.float32).astype(
        jnp.bfloat16
    )
    value_states = project(flat_tokens, value_weight, value_bias).astype(jnp.bfloat16)
    row_shape = (row_count, row_length, feature_width)
    joined, log_total = lax.map(
        attend_forward,
        (
            query_states.reshape(row_shape),
            key_states.reshape(row_shape),
            value_states.reshape(row_shape),
            segment_ids,
        ),
    )
    joined = joined.reshape(row_count * row_length, feature_width)
    resid_one = flat_tokens.astype(jnp.float32) + project(joined, out_weight, out_bias)
    hidden = norm_piece(resid_one, first_gain.astype(jnp.float32), first_shift.astype(jnp.float32))
    expanded = project(hidden.astype(jnp.bfloat16), up_weight, up_bias)
    active = gelu_exact(expanded).astype(jnp.bfloat16)
    resid_two = hidden + project(active, down_weight, down_bias)
    output = norm_piece(
        resid_two, second_gain.astype(jnp.float32), second_shift.astype(jnp.float32)
    )
    return (
        flat_tokens,
        query_states,
        key_states,
        value_states,
        joined,
        log_total,
        resid_one,
        hidden,
        expanded,
        active,
        resid_two,
        output,
    )


def gather_all(shards):
    packed = jnp.concatenate([piece.reshape(-1) for piece in shards])
    gathered = lax.all_gather(packed, "fsdp", axis=0, tiled=True)
    gathered = gathered.reshape(-1, packed.size)
    params, at = [], 0
    for piece in shards:
        part = gathered[:, at : at + piece.size]
        params.append(part.reshape((-1,) + piece.shape[1:]))
        at += piece.size
    return tuple(params)


def reduce_all(grad_params):
    group = lax.axis_size("fsdp")
    packed = jnp.concatenate(
        [piece.astype(jnp.bfloat16).reshape(group, -1) for piece in grad_params], 1
    )
    share = lax.psum_scatter(packed.reshape(-1), "fsdp", scatter_dimension=0, tiled=True)
    total = lax.psum(share, "rep").astype(jnp.float32)
    totals, at = [], 0
    for piece in grad_params:
        count = piece.size // group
        shape = (piece.shape[0] // group,) + piece.shape[1:]
        totals.append(total[at : at + count].reshape(shape))
        at += count
    return tuple(totals)


def local(
    tokens,
    segment_ids,
    pairing,
    query_weight,
    key_weight,
    value_weight,
    out_weight,
    up_weight,
    down_weight,
    query_bias,
    value_bias,
    out_bias,
    up_bias,
    down_bias,
    first_gain,
    first_shift,
    second_gain,
    second_shift,
):
    shards = (
        query_weight,
        key_weight,
        value_weight,
        out_weight,
        up_weight,
        down_weight,
        query_bias,
        value_bias,
        out_bias,
        up_bias,
        down_bias,
        first_gain,
        first_shift,
        second_gain,
        second_shift,
    )
    params = gather_all(shards)
    row_count, row_length, feature_width = tokens.shape
    states = run_layer(tokens, params, segment_ids)
    output = states[11].reshape(row_count, row_length, feature_width)

    def embed_rows(layer_out):
        return jax.vmap(pool_texts)(layer_out, segment_ids)

    embedded, embed_pullback = jax.vjp(embed_rows, output)
    local_count = row_count * SEGS
    local_embed = embedded.reshape(local_count, feature_width).astype(jnp.bfloat16)
    everything = lax.all_gather(local_embed, ("rep", "fsdp"), axis=0, tiled=True)
    text_count = everything.shape[0]
    pair_count = text_count // 2
    local_ids = lax.axis_index(("rep", "fsdp")) * local_count + jnp.arange(
        local_count, dtype=jnp.int32
    )
    matches = pairing[None, :] == local_ids[:, None]
    position = jnp.sum(jnp.where(matches, jnp.arange(text_count, dtype=jnp.int32)[None, :], 0), 1)
    pair_index = position // 2
    query_flag = position % 2 == 0
    passages = everything[pairing[1::2]]
    logits = (
        jnp.einsum("td,pd->tp", local_embed, passages, preferred_element_type=jnp.float32) * 100.0
    )
    row_peak = jnp.max(logits, 1, keepdims=True)
    exponent = jnp.exp(logits - row_peak)
    softmax_rows = exponent / jnp.sum(exponent, 1, keepdims=True)
    pairs = jnp.arange(pair_count, dtype=jnp.int32)[None, :]
    target = (pairs == pair_index[:, None]).astype(jnp.float32)
    queries = everything[pairing[0::2]]
    whole = jnp.einsum("qd,pd->qp", queries, passages, preferred_element_type=jnp.float32) * 100.0
    peak_all = jnp.max(whole, 1)
    total_all = jnp.sum(jnp.exp(whole - peak_all[:, None]), 1)
    cross = jnp.einsum("td,qd->tq", local_embed, queries, preferred_element_type=jnp.float32) * 100.0
    softmax_columns = jnp.exp(cross - peak_all[None, :]) / total_all[None, :]
    scaled_rows = ((softmax_rows - target) * 100.0).astype(jnp.bfloat16)
    scaled_columns = ((softmax_columns - target) * 100.0).astype(jnp.bfloat16)
    grad_query = jnp.einsum("tp,pd->td", scaled_rows, passages, preferred_element_type=jnp.float32)
    grad_passage = jnp.einsum(
        "tq,qd->td", scaled_columns, queries, preferred_element_type=jnp.float32
    )
    grad_embed = jnp.where(query_flag[:, None], grad_query, grad_passage)
    (grad_output,) = embed_pullback(grad_embed.reshape(row_count, SEGS, feature_width))
    flat_tokens, query_states, key_states, value_states, joined, log_total = states[:6]
    resid_one, hidden, expanded, active, resid_two = states[6:11]
    w_query_full, w_key_full, w_value_full, w_out_full, w_up_full, w_down_full = params[:6]
    first_gain_f = params[11].astype(jnp.float32)
    first_shift_f = params[12].astype(jnp.float32)
    second_gain_f = params[13].astype(jnp.float32)
    second_shift_f = params[14].astype(jnp.float32)
    token_total = row_count * row_length
    norm_out, second_pullback = jax.vjp(norm_piece, resid_two, second_gain_f, second_shift_f)
    grad_resid_two, grad_second_gain, grad_second_shift = second_pullback(
        grad_output.reshape(token_total, feature_width)
    )
    grad_feed = grad_resid_two.astype(jnp.bfloat16)
    grad_down_weight = jnp.einsum(
        "nf,nd->fd", active, grad_feed, preferred_element_type=jnp.float32
    )
    grad_down_bias = jnp.sum(grad_feed.astype(jnp.float32), 0)
    grad_active = jnp.einsum(
        "nd,fd->nf", grad_feed, w_down_full, preferred_element_type=jnp.float32
    )
    gelu_out, gelu_pullback = jax.vjp(gelu_exact, expanded)
    grad_expanded = gelu_pullback(grad_active)[0].astype(jnp.bfloat16)
    grad_up_weight = jnp.einsum(
        "nd,nf->df", hidden.astype(jnp.bfloat16), grad_expanded, preferred_element_type=jnp.float32
    )
    grad_up_bias = jnp.sum(grad_expanded.astype(jnp.float32), 0)
    grad_hidden = grad_resid_two + jnp.einsum(
        "nf,df->nd", grad_expanded, w_up_full, preferred_element_type=jnp.float32
    )
    hidden_out, first_pullback = jax.vjp(norm_piece, resid_one, first_gain_f, first_shift_f)
    grad_resid_one, grad_first_gain, grad_first_shift = first_pullback(grad_hidden)
    grad_branch = grad_resid_one.astype(jnp.bfloat16)
    grad_out_weight = jnp.einsum(
        "nd,ne->de", joined, grad_branch, preferred_element_type=jnp.float32
    )
    grad_out_bias = jnp.sum(grad_branch.astype(jnp.float32), 0)
    grad_joined = jnp.einsum(
        "ne,de->nd", grad_branch, w_out_full, preferred_element_type=jnp.float32
    ).astype(jnp.bfloat16)
    row_shape = (row_count, row_length, feature_width)
    grad_queries, grad_keys, grad_values = lax.map(
        attend_backward,
        (
            query_states.reshape(row_shape),
            key_states.reshape(row_shape),
            value_states.reshape(row_shape),
            segment_ids,
            grad_joined.reshape(row_shape),
            log_total,
        ),
    )
    grad_queries = grad_queries.reshape(token_total, feature_width)
    grad_keys = grad_keys.reshape(token_total, feature_width)
    grad_values = grad_values.reshape(token_total, feature_width)
    grad_query_weight = jnp.einsum(
        "nd,ne->de", flat_tokens, grad_queries, preferred_element_type=jnp.float32
    )
    grad_key_weight = jnp.einsum(
        "nd,ne->de", flat_tokens, grad_keys, preferred_element_type=jnp.float32
    )
    grad_value_weight = jnp.einsum(
        "nd,ne->de", flat_tokens, grad_values, preferred_element_type=jnp.float32
    )
    grad_query_bias = jnp.sum(grad_queries.astype(jnp.float32), 0)
    grad_value_bias = jnp.sum(grad_values.astype(jnp.float32), 0)
    grad_inputs = grad_resid_one
    grad_inputs = grad_inputs + jnp.einsum(
        "ne,de->nd", grad_queries, w_query_full, preferred_element_type=jnp.float32
    )
    grad_inputs = grad_inputs + jnp.einsum(
        "ne,de->nd", grad_keys, w_key_full, preferred_element_type=jnp.float32
    )
    grad_inputs = grad_inputs + jnp.einsum(
        "ne,de->nd", grad_values, w_value_full, preferred_element_type=jnp.float32
    )
    grad_params = (
        grad_query_weight,
        grad_key_weight,
        grad_value_weight,
        grad_out_weight,
        grad_up_weight,
        grad_down_weight,
        grad_query_bias,
        grad_value_bias,
        grad_out_bias,
        grad_up_bias,
        grad_down_bias,
        grad_first_gain,
        grad_first_shift,
        grad_second_gain,
        grad_second_shift,
    )
    totals = reduce_all(grad_params)
    return (
        output.astype(jnp.bfloat16),
        grad_inputs.reshape(row_shape).astype(jnp.bfloat16),
    ) + tuple(totals)


def solution(mesh):
    in_specs = (
        P(("rep", "fsdp"), None, None),
        P(("rep", "fsdp"), None),
        P(),
        P("fsdp", None),
        P("fsdp", None),
        P("fsdp", None),
        P("fsdp", None),
        P("fsdp", None),
        P("fsdp", None),
        P("fsdp"),
        P("fsdp"),
        P("fsdp"),
        P("fsdp"),
        P("fsdp"),
        P("fsdp"),
        P("fsdp"),
        P("fsdp"),
        P("fsdp"),
    )
    out_specs = (
        P(("rep", "fsdp"), None, None),
        P(("rep", "fsdp"), None, None),
        P("fsdp", None),
        P("fsdp", None),
        P("fsdp", None),
        P("fsdp", None),
        P("fsdp", None),
        P("fsdp", None),
        P("fsdp"),
        P("fsdp"),
        P("fsdp"),
        P("fsdp"),
        P("fsdp"),
        P("fsdp"),
        P("fsdp"),
        P("fsdp"),
        P("fsdp"),
    )
    return jax.shard_map(local, mesh=mesh, in_specs=in_specs, out_specs=out_specs, check_vma=False)
```

```python
import functools

import jax
import jax.numpy as jnp
from jax import lax
from jax.experimental import pallas as pl
from jax.experimental.pallas import tpu as pltpu
from jax.sharding import PartitionSpec as P

H = 12
HD = 64
SEGS = 8
MESH = pl.DeviceIdType.MESH
BF = jnp.bfloat16
F32 = jnp.float32


T = 1024
D = 768
FF = 3072
ROW = 512
NEG = -1e30
GROUPS = 4
UNITS = (96, 96, 96, 384)
(XW, YW, S0, ZX, D2, SX, ZY, D1, SY, ZD, SD, SZX, SZY, SZD) = range(14)
NCHUNK = 11
ACCS = 6


def dg(left, right, left_axis, right_axis):
    return lax.dot_general(
        left, right, (((left_axis,), (right_axis,)), ((), ())), preferred_element_type=F32
    )


def split_two(value):
    high = value.astype(BF)
    return high, (value - high.astype(F32)).astype(BF)


def aligned(start, size, step):
    return pl.ds(pl.multiple_of(start, step), size)


def gelu_pair(z):
    size = jnp.abs(z)
    t = 1.0 / (1.0 + 0.23164188814 * size)
    bell = jnp.exp(-0.5 * (z * z))
    poly = t * (
        0.127414796
        + t * (-0.142248368 + t * (0.7107068705 + t * (-0.7265760135 + t * 0.5307027145)))
    )
    tail = poly * bell
    phi = jnp.where(z >= 0, 1.0 - tail, tail)
    return z * phi, phi + z * (bell * 0.3989422804014327)


def normalize(residual):
    centre = jnp.mean(residual, -1, keepdims=True)
    offset = residual - centre
    spread = jnp.mean(offset * offset, -1, keepdims=True)
    scale = lax.rsqrt(spread + 1e-12)
    return offset * scale, scale


def fused_kernel(
    tokens,
    seg,
    meta,
    small,
    wq_in,
    wk_in,
    wv_in,
    wo_in,
    wup_in,
    wdn_in,
    out_y,
    out_dx,
    out_gq,
    out_gk,
    out_gv,
    out_go,
    out_gup,
    out_gdn,
    out_vec,
    x_s,
    wqkv,
    wo,
    wup,
    wdn,
    sb,
    vecs,
    upb,
    qkv,
    mb,
    colseg,
    lse,
    ao,
    n1,
    rs1,
    h1b,
    g_s,
    gp,
    n2,
    rs2,
    df,
    npool,
    e4,
    poscol,
    c_s,
    rsib,
    acc,
    rx,
    ry,
    rx2,
    ry2,
    rz1,
    rz2,
    fin,
    vg,
    vr,
    gsend,
    grecv,
    lsem,
    bsend,
    brecv,
    esend,
    erecv,
    xsend,
    xrecv,
    vsend,
    vrecv,
    osem,
):
    rep = lax.axis_index("rep")
    f = lax.axis_index("fsdp")
    core = f & 1
    chip = f >> 1
    pz = rep & 1
    dev_s, dev_x, dev_y, dev_d = (rep, f ^ 1), (rep, f ^ 2), (rep, f ^ 4), (rep, f ^ 6)
    dev_z1, dev_z2, dev_z3 = (rep ^ 1, f), (rep ^ 2, f), (rep ^ 3, f)
    weights = (wqkv, wo, wup, wdn)

    def remote(src, dst, ssem, rsem, dev):
        return pltpu.make_async_remote_copy(
            src_ref=src, dst_ref=dst, send_sem=ssem, recv_sem=rsem, device_id=dev, device_id_type=MESH
        )

    def local_pairs():
        own = [aligned(f * u, u, 16) for u in UNITS]
        return [
            (wq_in, wqkv.at[own[0], pl.ds(0, D)]),
            (wk_in, wqkv.at[own[0], pl.ds(D, D)]),
            (wv_in, wqkv.at[own[0], pl.ds(2 * D, D)]),
            (wo_in, wo.at[own[1], :]),
            (wup_in, wup.at[own[2], :]),
            (wdn_in, wdn.at[own[3], :]),
            (tokens, x_s),
        ]

    locals_ = [
        pltpu.make_async_copy(src, dst, lsem.at[i]) for i, (src, dst) in enumerate(local_pairs())
    ]
    for copy in locals_:
        copy.start()
    sb[pl.ds(f, 1)] = small[...].reshape(1, 8, 512)

    barrier = pltpu.get_barrier_semaphore()
    peers = [(rep, f ^ k) for k in range(1, 8)] + [dev_z1, dev_z2, dev_z3]
    for peer in peers:
        pl.semaphore_signal(barrier, inc=1, device_id=peer, device_id_type=MESH)
    pl.semaphore_wait(barrier, len(peers))

    def full(g, who):
        return who * UNITS[g], UNITS[g]

    def wide(g, who):
        return who * UNITS[g] + (UNITS[g] // 3) * pz, 2 * (UNITS[g] // 3)

    def part_m(g, who):
        return who * UNITS[g] + 2 * (UNITS[g] // 3) * pz, UNITS[g] // 3

    def part_a(g, who):
        return who * UNITS[g] + UNITS[g] // 3, UNITS[g] // 3

    def part_o(g, who):
        return who * UNITS[g] + 2 * (UNITS[g] // 3) * (1 - pz), UNITS[g] // 3

    fx, fy, fd, fs = f ^ 2, f ^ 4, f ^ 6, f ^ 1
    fsx, fsy, fsd = fs ^ 2, fs ^ 4, fs ^ 6
    sent_rows = {
        XW: (wide, f, dev_x),
        YW: (wide, f, dev_y),
        S0: (full, f, dev_s),
        ZX: (part_m, fx, dev_z1),
        D2: (part_m, fx, dev_y),
        SX: (wide, fx, dev_s),
        ZY: (part_m, fy, dev_z1),
        D1: (part_a, fy, dev_x),
        SY: (wide, fy, dev_s),
        ZD: (part_m, fd, dev_z1),
        SD: (wide, fd, dev_s),
        SZX: (part_o, fx, dev_s),
        SZY: (part_o, fy, dev_s),
        SZD: (part_o, fd, dev_s),
    }
    got_rows = {
        XW: (wide, fx),
        YW: (wide, fy),
        S0: (full, fs),
        ZX: (part_o, fx),
        D2: (part_m, fd),
        SX: (wide, fsx),
        ZY: (part_o, fy),
        D1: (part_a, fd),
        SY: (wide, fsy),
        ZD: (part_o, fd),
        SD: (wide, fsd),
        SZX: (part_o, fsx),
        SZY: (part_o, fsy),
        SZD: (part_o, fsd),
    }

    def gather_copy(g, piece):
        rows, who, dev = sent_rows[piece]
        start, size = rows(g, who)
        view = weights[g].at[aligned(start, size, 16), :]
        return remote(view, view, gsend.at[g, piece], grecv.at[g, piece], dev)

    def g_send(g, *pieces):
        for piece in pieces:
            gather_copy(g, piece).start()

    def g_recv(g, *pieces):
        for piece in pieces:
            rows, who = got_rows[piece]
            start, size = rows(g, who)
            view = weights[g].at[aligned(start, size, 16), :]
            remote(
                view, view, gsend.at[g, piece], grecv.at[g, piece], sent_rows[piece][2]
            ).wait_recv()

    def g_done(g):
        for piece in range(14):
            gather_copy(g, piece).wait_send()

    def st0(g):
        for i in ((0, 1, 2), (3,), (4,), (5,))[g]:
            locals_[i].wait()
        g_send(g, XW, YW, S0)

    def st1(g):
        g_recv(g, XW)
        g_send(g, ZX, D2, SX)
        g_recv(g, YW)
        g_send(g, D1, ZY, SY)

    def st2(g):
        g_recv(g, D1, D2)
        g_send(g, ZD, SD)
        g_recv(g, ZX)
        g_send(g, SZX)
        g_recv(g, ZY)
        g_send(g, SZY)

    def st3(g):
        g_recv(g, ZD)
        g_send(g, SZD)

    def st4(g):
        g_recv(g, S0, SX, SY, SD, SZX, SZY, SZD)

    def small_copy(k):
        view = sb.at[pl.ds(f, 1)]
        return remote(view, view, bsend.at[k - 1], brecv.at[k - 1], (rep, f ^ k))

    st0(0)
    for k in range(1, 8):
        small_copy(k).start()
    st0(1)

    segf = seg[...].astype(F32)
    for r in range(2):
        colseg[pl.ds(r * ROW, ROW), :] = jnp.broadcast_to(segf[r : r + 1, :], (128, ROW)).T
    for r in range(2):
        for b in range(2):
            key_side = colseg[pl.ds(r * ROW + 128 * b, 384), 0:1]
            query_side = segf[r : r + 1, 256 * b : 256 * b + 256]
            mb[2 * r + b] = jnp.where(key_side == query_side, 0.0, NEG)
    poscol[...] = jnp.broadcast_to(meta[0:1, :], (128, 512)).T

    st1(0)
    st0(2)

    for k in range(1, 8):
        view = sb.at[pl.ds(f ^ k, 1)]
        remote(view, view, bsend.at[k - 1], brecv.at[k - 1], (rep, f ^ k)).wait_recv()
    lane = lax.broadcasted_iota(jnp.int32, (128, D), 0)
    column = lax.broadcasted_iota(jnp.int32, (128, D), 1)
    total = jnp.zeros((8, D), F32)
    for k in range(8):
        upb[:, k * 384 : (k + 1) * 384] = sb[k, :, 0:384]
        place = jnp.where((column == lane + 96 * k) & (lane < 96), 1.0, 0.0).astype(BF)
        total = total + dg(sb[k, :, 384:512].astype(BF), place, 1, 0)
    vecs[...] = total
    bq, bv, bo, bdn = (vecs[i : i + 1, :] for i in range(4))
    g1, s1, g2, s2 = (vecs[i : i + 1, :] for i in range(4, 8))
    locals_[6].wait()

    st2(0)
    st1(1)
    st3(0)
    st4(0)

    def qkv_step(i, carry):
        rows = aligned(i * 512, 512, 512)
        xb = x_s[rows, :]
        qkv[rows, 0:D] = ((dg(xb, wqkv[:, 0:D], 1, 0) + bq).astype(BF).astype(F32) * 0.125).astype(BF)
        qkv[rows, D : 2 * D] = dg(xb, wqkv[:, D : 2 * D], 1, 0).astype(BF)
        qkv[rows, 2 * D : 3 * D] = (dg(xb, wqkv[:, 2 * D : 3 * D], 1, 0) + bv).astype(BF)
        return carry

    lax.fori_loop(0, 2, qkv_step, 0)
    st2(1)
    st3(1)
    st1(2)
    st0(3)

    even = (lax.broadcasted_iota(jnp.int32, (1, 128), 1) < HD).astype(F32).astype(BF)
    odd = (lax.broadcasted_iota(jnp.int32, (1, 128), 1) >= HD).astype(F32).astype(BF)
    lower = lax.broadcasted_iota(jnp.int32, (384, 128), 1) < HD

    def both(value):
        return jnp.concatenate([value * even, value * odd], axis=0)

    def attend(i, carry):
        r = i // 12
        pair = (i // 2) % 6
        b = i % 2
        kq = aligned(r * ROW + 128 * b, 384, 128)
        qq = aligned(r * ROW + 256 * b, 256, 256)
        at = pair * 128
        kk = both(qkv[kq, aligned(D + at, 128, 128)])
        vv = both(qkv[kq, aligned(2 * D + at, 128, 128)])
        scores = dg(kk, qkv[qq, aligned(at, 128, 128)], 1, 1)
        bias = mb[2 * r + b]
        parts, logs = [], []
        for h in range(2):
            s = scores[384 * h : 384 * h + 384] + bias
            peak = jnp.max(s, 0, keepdims=True)
            e = jnp.exp(s - peak)
            tot = jnp.sum(e, 0, keepdims=True)
            parts.append((e * (1.0 / tot)).astype(BF))
            logs.append(peak + jnp.log(tot))
        lse[i] = jnp.concatenate(logs + [jnp.zeros((6, 256), F32)], axis=0)
        ao[qq, aligned(at, 128, 128)] = dg(jnp.concatenate(parts, 0), vv, 0, 0).astype(BF)
        return carry

    lax.fori_loop(0, 6, attend, 0)
    st2(2)
    lax.fori_loop(6, 12, attend, 0)
    st3(2)
    st1(3)
    lax.fori_loop(12, 18, attend, 0)
    st4(1)
    st2(3)
    lax.fori_loop(18, 24, attend, 0)
    st3(3)

    def out_step(i, carry):
        rows = aligned(i * 256, 256, 256)
        r1 = x_s[rows, :].astype(F32) + (dg(ao[rows, :], wo[...], 1, 0) + bo)
        n, scale = normalize(r1)
        n1[rows, :] = n
        rs1[rows, :] = jnp.broadcast_to(scale, (256, 128))
        h1b[rows, :] = (n * g1 + s1).astype(BF)
        return carry

    lax.fori_loop(0, 4, out_step, 0)
    st4(2)

    def up_step(i, carry):
        rows = aligned((i // 6) * 512, 512, 512)
        cols = aligned((i % 6) * 512, 512, 512)
        z = dg(h1b[rows, :], wup[:, cols], 1, 0) + upb[0:1, cols]
        g, slope = gelu_pair(z)
        g_s[rows, cols] = g.astype(BF)
        gp[rows, cols] = slope.astype(BF)
        return carry

    lax.fori_loop(0, 12, up_step, 0)
    st4(3)

    npool[...] = jnp.zeros((16, D), F32)
    text_row = lax.broadcasted_iota(jnp.int32, (16, ROW), 0)

    def member_of(r):
        ids = seg[pl.ds(r, 1), :] + 8 * r
        return (text_row == ids).astype(F32)

    for i in range(4):
        rows = pl.ds(i * 256, 256)
        h1 = n1[rows, :] * g1 + s1
        n, scale = normalize(h1 + (dg(g_s[rows, :], wdn[...], 1, 0) + bdn))
        n2[rows, :] = n
        rs2[rows, :] = jnp.broadcast_to(scale, (256, 128))
        df[rows, :] = (n * g2 + s2).astype(BF)
        member = member_of(i // 2)[:, 256 * (i % 2) : 256 * (i % 2) + 256].astype(BF)
        high, low = split_two(n)
        npool[...] += dg(member, high, 1, 0) + dg(member, low, 1, 0)
    y_copy = pltpu.make_async_copy(df, out_y, osem.at[0])
    y_copy.start()

    members = jnp.concatenate([member_of(0), member_of(1)], axis=1)
    counts = jnp.sum(members, 1, keepdims=True)
    members = members.astype(BF)
    pooled = npool[...] / counts * g2 + s2
    inverse = lax.rsqrt(jnp.sum(pooled * pooled, 1, keepdims=True) + 1e-06)
    embed = pooled * inverse
    e4[pl.ds(rep, 1), pl.ds(f, 1)] = embed.astype(BF).reshape(1, 1, 16, D)

    def e_column(who):
        return e4.at[:, pl.ds(who, 1)]

    def e_own(who):
        return e4.at[pl.ds(who, 1), pl.ds(f, 1)]

    z_sends = [
        remote(e_own(rep), e_own(rep), esend.at[k - 1], erecv.at[k - 1], (rep ^ k, f))
        for k in (1, 2, 3)
    ]
    for copy in z_sends:
        copy.start()
    for k in (1, 2, 3):
        remote(e_own(rep ^ k), e_own(rep ^ k), esend.at[k - 1], erecv.at[k - 1], (rep ^ k, f)).wait_recv()
    plane = ((fx, dev_x, 3), (fy, dev_y, 4), (fd, dev_d, 5))
    plane_sends = [
        remote(e_column(f), e_column(f), esend.at[i], erecv.at[i], dev) for who, dev, i in plane
    ]
    plane_sends.append(remote(e_column(f), e_column(f), esend.at[6], erecv.at[6], dev_s))
    for copy in plane_sends:
        copy.start()
    for n_, (who, dev, i) in enumerate(plane):
        remote(e_column(who), e_column(who), esend.at[i], erecv.at[i], dev).wait_recv()
        copy = remote(e_column(who), e_column(who), esend.at[7 + n_], erecv.at[7 + n_], dev_s)
        copy.start()
        plane_sends.append(copy)
    for n_, who in enumerate((fs, fsx, fsy, fsd)):
        remote(e_column(who), e_column(who), esend.at[6 + n_], erecv.at[6 + n_], dev_s).wait_recv()
    for copy in z_sends + plane_sends:
        copy.wait_send()
    for g in range(GROUPS):
        g_done(g)
    for k in range(1, 8):
        small_copy(k).wait_send()

    every = e4[...].reshape(512, D)
    pos_all = meta[0:1, :]
    pair_all = jnp.floor(pos_all * 0.5)
    second_all = pos_all - 2.0 * pair_all
    pos_col = poscol[:, 0:1]
    second_col = pos_col - 2.0 * jnp.floor(pos_col * 0.5)
    whole = dg(every, every, 1, 1) * 100.0
    whole = jnp.where(second_col > 0.5, whole, NEG)
    peak_all = jnp.max(whole, 0, keepdims=True)
    total_all = jnp.sum(jnp.exp(whole - peak_all), 0, keepdims=True)
    own = embed.astype(BF)
    mine = dg(own, every, 1, 1) * 100.0
    pos_own = poscol[aligned((rep * 8 + f) * 16, 16, 16), 0:1]
    pair_own = jnp.floor(pos_own * 0.5)
    second_own = pos_own - 2.0 * pair_own
    same_pair = jnp.where(pair_own == pair_all, 1.0, 0.0)
    rows_masked = jnp.where(second_all > 0.5, mine, NEG)
    row_peak = jnp.max(rows_masked, 1, keepdims=True)
    row_e = jnp.exp(rows_masked - row_peak)
    soft_rows = row_e / jnp.sum(row_e, 1, keepdims=True)
    soft_cols = jnp.exp(jnp.where(second_all > 0.5, NEG, mine - peak_all)) / total_all
    d_rows = (soft_rows - same_pair) * second_all
    d_cols = (soft_cols - same_pair) * (1.0 - second_all)
    d_logits = (jnp.where(second_own > 0.5, d_cols, d_rows) * 100.0).astype(BF)
    d_embed = dg(d_logits, every, 1, 0)
    d_pooled = (d_embed - embed * jnp.sum(embed * d_embed, 1, keepdims=True)) * inverse
    d_each = d_pooled / counts
    vg[...] = jnp.zeros((16, D), F32)
    vg[6:7, :] = jnp.sum(d_each * npool[...], 0, keepdims=True)
    vg[7:8, :] = jnp.sum(d_pooled, 0, keepdims=True)
    u_text = d_each * g2
    u_text = u_text - jnp.mean(u_text, 1, keepdims=True)
    u_high, u_low = split_two(u_text)
    u_both = jnp.concatenate([u_high, u_low], 0)
    y_copy.wait()

    for i in range(4):
        rows = pl.ds(i * 256, 256)
        part = members[:, 256 * i : 256 * i + 256]
        u = dg(jnp.concatenate([part, part], 0), u_both, 0, 0)
        n = n2[rows, :]
        d = (u - n * jnp.mean(u * n, 1, keepdims=True)) * rs2[rows, 0:1]
        n2[rows, :] = d
        db = d.astype(BF)
        df[rows, :] = db
        vg[3:4, :] += jnp.sum(db.astype(F32), 0, keepdims=True)

    def slab_rows(i):
        return 128 if i < 3 else 96

    ch_x, ch_y, ch_d = chip ^ 1, chip ^ 2, chip ^ 3
    hz, cz = pz, rep >> 1

    def view_s(i):
        u, s = slab_rows(i), i % 2
        src = c_s.at[s, :, pl.ds(1 - core, 1), pl.ds(0, u), :]
        dst = rsib.at[s, :, :, pl.ds(0, u), :]
        return remote(src, dst, xsend.at[s, 0], xrecv.at[s, 0], dev_s)

    def views_x1(i):
        u, s, a = slab_rows(i), i % 2, i % ACCS
        half = u // 2
        low, high = pl.ds(0, half), pl.ds(half, half)
        pieces = (
            (ch_x, low, rx.at[s, 0, pl.ds(0, half), :], dev_x),
            (ch_d, low, rx.at[s, 1, pl.ds(0, half), :], dev_x),
            (ch_y, high, ry.at[s, 0, pl.ds(0, half), :], dev_y),
            (ch_d, high, ry.at[s, 1, pl.ds(0, half), :], dev_y),
        )
        return [
            remote(acc.at[a, who, rows, :], dst, xsend.at[s, 1 + n], xrecv.at[s, 1 + n], dev)
            for n, (who, rows, dst, dev) in enumerate(pieces)
        ]

    def views_x2(i):
        u, s, a = slab_rows(i), i % 2, i % ACCS
        half = u // 2
        low, high = pl.ds(0, half), pl.ds(half, half)
        return [
            remote(acc.at[a, ch_y, low, :], ry2.at[s, low, :], xsend.at[s, 5], xrecv.at[s, 5], dev_y),
            remote(acc.at[a, ch_x, high, :], rx2.at[s, low, :], xsend.at[s, 6], xrecv.at[s, 6], dev_x),
        ]

    def view_z1(i):
        u, s, a = slab_rows(i), i % 2, i % ACCS
        half = u // 2
        src = acc.at[a, chip, aligned((1 - hz) * half, half, 16), :]
        return remote(src, rz1.at[s, pl.ds(0, half), :], xsend.at[s, 7], xrecv.at[s, 7], dev_z1)

    def view_z2(i):
        u, s, a = slab_rows(i), i % 2, i % ACCS
        half = u // 2
        src = acc.at[a, chip, aligned(hz * half, half, 16), aligned((1 - cz) * 384, 384, 128)]
        return remote(src, rz2.at[s, pl.ds(0, half), :], xsend.at[s, 8], xrecv.at[s, 8], dev_z2)

    def quarter(i, who):
        half = slab_rows(i) // 2
        return fin.at[i, aligned((who & 1) * half, half, 16), aligned((who >> 1) * 384, 384, 128)]

    def views_z3(i):
        s = i % 2
        return [
            remote(quarter(i, rep), quarter(i, rep), xsend.at[s, 8 + k], xrecv.at[s, 8 + k], (rep ^ k, f))
            for k in (1, 2, 3)
        ]

    def stage_x1(i):
        u, s, a = slab_rows(i), i % 2, i % ACCS
        copy = view_s(i)
        copy.wait()
        for ch in range(4):
            acc[a, ch, 0:u] = c_s[s, ch, pl.ds(core, 1), 0:u][0] + rsib[s, ch, 0, 0:u]
        for copy in views_x1(i):
            copy.start()

    def stage_x2(i):
        u, s, a = slab_rows(i), i % 2, i % ACCS
        half = u // 2
        for copy in views_x1(i):
            copy.wait()
        acc[a, pl.ds(chip, 1), 0:half] += rx[s, 0:1, 0:half]
        acc[a, pl.ds(ch_y, 1), 0:half] += rx[s, 1:2, 0:half]
        acc[a, pl.ds(chip, 1), half:u] += ry[s, 0:1, 0:half]
        acc[a, pl.ds(ch_x, 1), half:u] += ry[s, 1:2, 0:half]
        for copy in views_x2(i):
            copy.start()

    def stage_z1(i):
        u, s, a = slab_rows(i), i % 2, i % ACCS
        half = u // 2
        for copy in views_x2(i):
            copy.wait()
        acc[a, pl.ds(chip, 1), 0:half] += ry2[s : s + 1, 0:half]
        acc[a, pl.ds(chip, 1), half:u] += rx2[s : s + 1, 0:half]
        view_z1(i).start()

    def stage_z2(i):
        u, s, a = slab_rows(i), i % 2, i % ACCS
        half = u // 2
        view_z1(i).wait()
        rows = aligned(hz * half, half, 16)
        acc[a, pl.ds(chip, 1), rows, :] += rz1[s : s + 1, 0:half]
        view_z2(i).start()

    def stage_z3(i):
        u, s, a = slab_rows(i), i % 2, i % ACCS
        half = u // 2
        view_z2(i).wait()
        rows, cols = aligned(hz * half, half, 16), aligned(cz * 384, 384, 128)
        fin[i, rows, cols] = acc[a, pl.ds(chip, 1), rows, cols][0] + rz2[s, 0:half]
        for copy in views_z3(i):
            copy.start()

    def out_copies(i):
        if i < 3:
            pairs = [(fin.at[i], out_gdn.at[pl.ds(128 * i, 128), :])]
        elif i < 7:
            pairs = [(fin.at[i, pl.ds(0, 96), :], out_gup.at[:, pl.ds(D * (i - 3), D)])]
        elif i == 7:
            pairs = [(fin.at[i, pl.ds(0, 96), :], out_go)]
        else:
            pairs = [
                (
                    fin.at[i, pl.ds(0, 96), pl.ds(256 * n, 256)],
                    ref.at[:, pl.ds(256 * (i - 8), 256)],
                )
                for n, ref in enumerate((out_gq, out_gk, out_gv))
            ]
        return [
            pltpu.make_async_copy(src, dst, osem.at[2 + i + (NCHUNK if n == 1 else 2 * NCHUNK if n == 2 else 0)])
            for n, (src, dst) in enumerate(pairs)
        ]

    def stage_f(i):
        s = i % 2
        for copy in views_z3(i):
            copy.wait_send()
        for k in (1, 2, 3):
            remote(
                quarter(i, rep ^ k), quarter(i, rep ^ k), xsend.at[s, 8 + k], xrecv.at[s, 8 + k], (rep ^ k, f)
            ).wait_recv()
        for copy in out_copies(i):
            copy.start()

    stages = (stage_x1, stage_x2, stage_z1, stage_z2, stage_z3, stage_f)
    flight = {}

    def tick(new=None):
        for i in sorted(flight):
            stages[flight[i]](i)
            flight[i] += 1
            if flight[i] == len(stages):
                del flight[i]
        if new is not None:
            view_s(new).start()
            flight[new] = 0

    def store_slabs(i, hh, result):
        u, s = slab_rows(i), i % 2
        for k in range(4):
            c_s[s, pl.ds(2 * hh + k // 2, 1), k % 2, 0:u] = (
                result[u * k : u * k + u].astype(BF).reshape(1, u, D)
            )

    def chunk(i, left_of, right):
        def half(hh, carry):
            store_slabs(i, hh, dg(left_of(hh), right(), 0, 0))
            return carry

        lax.fori_loop(0, 2, half, 0)

    def down_chunk(j):
        def left_of(hh):
            return jnp.concatenate(
                [g_s[:, aligned((4 * hh + k) * 384 + j * 128, 128, 128)] for k in range(4)], 1
            )

        chunk(j, left_of, lambda: df[...])

    def up_chunk(j):
        cols = pl.ds(D * j, D)

        def slope_step(m, carry):
            rows = aligned(m * 512, 512, 512)
            dz = (dg(df[rows, :], wdn[cols, :], 1, 1) * gp[rows, cols].astype(F32)).astype(BF)
            gp[rows, cols] = dz
            vg[8 + j : 9 + j, :] += jnp.sum(dz.astype(F32), 0, keepdims=True)
            return carry

        lax.fori_loop(0, 2, slope_step, 0)
        chunk(3 + j, lambda hh: h1b[:, aligned(384 * hh, 384, 128)], lambda: gp[:, cols])

    for j in range(3):
        down_chunk(j)
        tick(j)
    for j in range(4):
        up_chunk(j)
        tick(3 + j)

    def first_step(i, carry):
        rows = aligned(i * 256, 256, 256)
        dh = n2[rows, :] + dg(gp[rows, :], wup[...], 1, 1)
        n = n1[rows, :]
        vg[4:5, :] += jnp.sum(dh * n, 0, keepdims=True)
        vg[5:6, :] += jnp.sum(dh, 0, keepdims=True)
        u = dh * g1
        d = (u - jnp.mean(u, 1, keepdims=True) - n * jnp.mean(u * n, 1, keepdims=True)) * rs1[rows, 0:1]
        n2[rows, :] = d
        db = d.astype(BF)
        df[rows, :] = db
        vg[2:3, :] += jnp.sum(db.astype(F32), 0, keepdims=True)
        return carry

    lax.fori_loop(0, 2, first_step, 0)
    tick()
    lax.fori_loop(2, 4, first_step, 0)
    chunk(7, lambda hh: ao[:, aligned(384 * hh, 384, 128)], lambda: df[...])
    tick(7)

    def mix_step(m, carry):
        rows = aligned(m * 512, 512, 512)
        h1b[rows, :] = dg(df[rows, :], wo[...], 1, 1).astype(BF)
        return carry

    lax.fori_loop(0, 2, mix_step, 0)

    def attend_back(r, pair):
        at = pair * 128
        grads_k, grads_v = [], []
        for b in range(2):
            kq = aligned(r * ROW + 128 * b, 384, 128)
            qq = aligned(r * ROW + 256 * b, 256, 256)
            kk = both(qkv[kq, aligned(D + at, 128, 128)])
            vv = both(qkv[kq, aligned(2 * D + at, 128, 128)])
            q = qkv[qq, aligned(at, 128, 128)]
            da = h1b[qq, aligned(at, 128, 128)]
            scores = dg(kk, q, 1, 1)
            dp = dg(vv, da, 1, 1)
            bias = mb[2 * r + b]
            logs = lse[r * 12 + pair * 2 + b]
            probs, dscores = [], []
            for h in range(2):
                rows = slice(384 * h, 384 * h + 384)
                prob = jnp.exp(scores[rows] + bias - logs[h : h + 1])
                term = prob * dp[rows]
                inner = jnp.sum(term, 0, keepdims=True)
                probs.append(prob.astype(BF))
                dscores.append((term - prob * inner).astype(BF))
            probs = jnp.concatenate(probs, 0)
            dscores = jnp.concatenate(dscores, 0)
            gv = dg(probs, da, 1, 0)
            gk = dg(dscores, q, 1, 0)
            grads_v.append(jnp.where(lower, gv[0:384], gv[384:768]))
            grads_k.append(jnp.where(lower, gk[0:384], gk[384:768]))
            g_s[qq, aligned(at, 128, 128)] = (dg(dscores, kk, 0, 0) * 0.125).astype(BF)
        for off, (first, second) in ((D, grads_k), (2 * D, grads_v)):
            cols = aligned(off + at, 128, 128)
            g_s[aligned(r * ROW, 128, 128), cols] = first[0:128].astype(BF)
            g_s[aligned(r * ROW + 128, 256, 128), cols] = (first[128:384] + second[0:256]).astype(BF)
            g_s[aligned(r * ROW + 384, 128, 128), cols] = second[256:384].astype(BF)

    def triple(group):
        return jnp.concatenate([g_s[:, pl.ds(D * n + 256 * group, 256)] for n in range(3)], 1)

    for group in range(3):

        def back_step(i, carry):
            attend_back(i // 2, 2 * group + i % 2)
            return carry

        lax.fori_loop(0, 2, back_step, 0)
        tick()
        lax.fori_loop(2, 4, back_step, 0)
        chunk(8 + group, lambda hh: x_s[:, aligned(384 * hh, 384, 128)], lambda: triple(group))
        tick(8 + group)

    for row, off in ((0, 0), (1, 2 * D)):
        vg[row : row + 1, :] = jnp.sum(g_s[:, pl.ds(off, D)].astype(F32), 0, keepdims=True)
    order = (dev_s, dev_x, dev_y, dev_z1, dev_z2)

    def v_copy(n):
        return remote(vg, vr.at[n], vsend.at[n], vrecv.at[n], order[n])

    def v_step(n):
        v_copy(n).wait()
        vg[...] = vg[...] + vr[n]
        if n + 1 < len(order):
            v_copy(n + 1).start()

    v_copy(0).start()

    def token_step(i, carry):
        rows = aligned(i * 256, 256, 256)
        ao[rows, :] = (n2[rows, :] + dg(g_s[rows, pl.ds(0, 3 * D)], wqkv[...], 1, 1)).astype(BF)
        return carry

    lax.fori_loop(0, 2, token_step, 0)
    tick()
    v_step(0)
    lax.fori_loop(2, 4, token_step, 0)
    dx_copy = pltpu.make_async_copy(ao, out_dx, osem.at[1])
    dx_copy.start()
    tick()
    v_step(1)
    tick()
    v_step(2)
    tick()
    v_step(3)
    tick()
    v_step(4)
    tick()
    out_vec[8:16, 0:128] = jnp.zeros((8, 128), F32)
    for k in range(8):

        @pl.when(f == k)
        def _():
            out_vec[0:8, 0:96] = vg[0:8, 96 * k : 96 * k + 96]
            line = jnp.concatenate([vg[8 + n : 9 + n, :] for n in range(4)], 1)
            out_vec[8:9, 0:384] = line[:, 384 * k : 384 * k + 384]

    dx_copy.wait()
    for i in range(NCHUNK):
        for copy in out_copies(i):
            copy.wait()


def fused_call(tokens, seg, meta, small, shards):
    vm = lambda shape, dtype: pltpu.VMEM(shape, dtype)
    sem = pltpu.SemaphoreType.DMA
    scratch = [
        vm((T, D), BF),
        vm((D, 3 * D), BF),
        vm((D, D), BF),
        vm((D, FF), BF),
        vm((FF, D), BF),
        vm((8, 8, 512), F32),
        vm((8, D), F32),
        vm((8, FF), F32),
        vm((T, 3 * D), BF),
        vm((4, 384, 256), F32),
        vm((T, 128), F32),
        vm((24, 8, 256), F32),
        vm((T, D), BF),
        vm((T, D), F32),
        vm((T, 128), F32),
        vm((T, D), BF),
        vm((T, FF), BF),
        vm((T, FF), BF),
        vm((T, D), F32),
        vm((T, 128), F32),
        vm((T, D), BF),
        vm((16, D), F32),
        vm((4, 8, 16, D), BF),
        vm((512, 128), F32),
        vm((2, 4, 2, 128, D), BF),
        vm((2, 4, 1, 128, D), BF),
        vm((ACCS, 4, 128, D), BF),
        vm((2, 2, 64, D), BF),
        vm((2, 2, 64, D), BF),
        vm((2, 64, D), BF),
        vm((2, 64, D), BF),
        vm((2, 64, D), BF),
        vm((2, 64, D // 2), BF),
        vm((NCHUNK, 128, D), BF),
        vm((16, D), F32),
        vm((5, 16, D), F32),
        sem((GROUPS, 14)),
        sem((GROUPS, 14)),
        sem((7,)),
        sem((7,)),
        sem((7,)),
        sem((10,)),
        sem((10,)),
        sem((2, 12)),
        sem((2, 12)),
        sem((5,)),
        sem((5,)),
        sem((2 + 3 * NCHUNK,)),
    ]
    shape = jax.ShapeDtypeStruct
    any_ = pl.BlockSpec(memory_space=pl.ANY)
    vmem = pl.BlockSpec(memory_space=pltpu.VMEM)
    return pl.pallas_call(
        fused_kernel,
        name="layer_step",
        out_shape=(
            shape((T, D), BF),
            shape((T, D), BF),
            shape((96, D), BF),
            shape((96, D), BF),
            shape((96, D), BF),
            shape((96, D), BF),
            shape((96, FF), BF),
            shape((384, D), BF),
            shape((16, 384), F32),
        ),
        in_specs=[any_, vmem, vmem, vmem] + [any_] * 6,
        out_specs=(any_,) * 8 + (vmem,),
        scratch_shapes=scratch,
        compiler_params=pltpu.CompilerParams(
            collective_id=0, has_side_effects=True, vmem_limit_bytes=64 * 2**20
        ),
        cost_estimate=pl.CostEstimate(
            flops=60 * 10**9, bytes_accessed=30 * 2**20, transcendentals=10**7
        ),
    )(tokens, seg, meta, small, *shards[:6])


def local_fused(tokens, segment_ids, pairing, *shards):
    row_count, row_length, width = tokens.shape
    order = jnp.arange(pairing.shape[0], dtype=jnp.int32)
    position = jnp.sum(
        jnp.where(pairing[:, None] == order[None, :], order[:, None], 0), 0, dtype=jnp.int32
    )
    meta = jnp.broadcast_to(position.astype(F32)[None, :], (8, position.shape[0]))
    (bq, bv, bo, bup, bdn, g1, s1, g2, s2) = shards[6:]
    narrow = jnp.stack([bq, bv, bo, bdn, g1, s1, g2, s2]).astype(F32)
    narrow = jnp.pad(narrow, ((0, 0), (0, 128 - narrow.shape[1])))
    small = jnp.concatenate(
        [jnp.broadcast_to(bup.astype(F32)[None, :], (8, bup.shape[0])), narrow], 1
    )
    results = fused_call(tokens.reshape(-1, width), segment_ids, meta, small, shards)
    out_y, out_dx, gq, gk, gv, go, gup, gdn, vec = results
    share = narrow.shape[1] and bq.shape[0]
    return (
        out_y.reshape(tokens.shape),
        out_dx.reshape(tokens.shape),
        gq.astype(F32),
        gk.astype(F32),
        gv.astype(F32),
        go.astype(F32),
        gup.astype(F32),
        gdn.astype(F32),
        vec[0, :share],
        vec[1, :share],
        vec[2, :share],
        vec[8, : bup.shape[0]],
        vec[3, :share],
        vec[4, :share],
        vec[5, :share],
        vec[6, :share],
        vec[7, :share],
    )


def norm_piece(residual, gain_vector, shift_vector):
    centre = jnp.mean(residual, -1, keepdims=True)
    offset = residual - centre
    spread = jnp.mean(offset * offset, -1, keepdims=True)
    return offset * lax.rsqrt(spread + 1e-12) * gain_vector + shift_vector


def gelu_exact(argument):
    return jax.nn.gelu(argument, approximate=False)


def pool_texts(layer_out, segments):
    member = (segments[:, None] == jnp.arange(SEGS)[None, :]).astype(jnp.float32)
    totals = jnp.dot(member.T, layer_out, precision=lax.Precision.HIGHEST)
    counts = jnp.sum(member, 0)
    pooled = totals / counts[:, None]
    return pooled * lax.rsqrt(jnp.sum(pooled * pooled, -1, keepdims=True) + 1e-06)


def project(inputs, weight, bias_vector):
    return jnp.dot(inputs, weight, preferred_element_type=jnp.float32) + bias_vector.astype(
        jnp.float32
    )


def head_scores(query_states, key_states, segments):
    row_length = query_states.shape[0]
    scores = jnp.einsum(
        "qhd,khd->hqk",
        query_states.reshape(row_length, H, HD),
        key_states.reshape(row_length, H, HD),
        preferred_element_type=jnp.float32,
    ) * HD ** (-0.5)
    same_text = segments[:, None] == segments[None, :]
    return jnp.where(same_text[None], scores, -1e30)


def attend_forward(pieces):
    query_states, key_states, value_states, segments = pieces
    row_length = query_states.shape[0]
    scores = head_scores(query_states, key_states, segments)
    row_peak = jnp.max(scores, -1, keepdims=True)
    exponent = jnp.exp(scores - row_peak)
    row_total = jnp.sum(exponent, -1, keepdims=True)
    probability = (exponent / row_total).astype(jnp.bfloat16)
    mixture = jnp.einsum(
        "hqk,khd->qhd",
        probability,
        value_states.reshape(row_length, H, HD),
        preferred_element_type=jnp.float32,
    )
    return (mixture.reshape(row_length, H * HD).astype(jnp.bfloat16), row_peak + jnp.log(row_total))


def attend_backward(pieces):
    query_states, key_states, value_states, segments, grad_mixture, log_total = pieces
    row_length = query_states.shape[0]
    query_heads = query_states.reshape(row_length, H, HD)
    key_heads = key_states.reshape(row_length, H, HD)
    value_heads = value_states.reshape(row_length, H, HD)
    grad_heads = grad_mixture.reshape(row_length, H, HD)
    probability = jnp.exp(head_scores(query_states, key_states, segments) - log_total)
    grad_probability = jnp.einsum(
        "qhd,khd->hqk", grad_heads, value_heads, preferred_element_type=jnp.float32
    )
    grad_values = jnp.einsum(
        "hqk,qhd->khd",
        probability.astype(jnp.bfloat16),
        grad_heads,
        preferred_element_type=jnp.float32,
    )
    grad_scores = probability * (
        grad_probability - jnp.sum(probability * grad_probability, -1, keepdims=True)
    )
    grad_scores = grad_scores.astype(jnp.bfloat16)
    score_scale = HD ** (-0.5)
    grad_queries = (
        jnp.einsum("hqk,khd->qhd", grad_scores, key_heads, preferred_element_type=jnp.float32)
        * score_scale
    )
    grad_keys = (
        jnp.einsum("hqk,qhd->khd", grad_scores, query_heads, preferred_element_type=jnp.float32)
        * score_scale
    )
    return (
        grad_queries.reshape(row_length, H * HD).astype(jnp.bfloat16),
        grad_keys.reshape(row_length, H * HD).astype(jnp.bfloat16),
        grad_values.reshape(row_length, H * HD).astype(jnp.bfloat16),
    )


def run_layer(tokens, params, segment_ids):
    (
        query_weight,
        key_weight,
        value_weight,
        out_weight,
        up_weight,
        down_weight,
        query_bias,
        value_bias,
        out_bias,
        up_bias,
        down_bias,
        first_gain,
        first_shift,
        second_gain,
        second_shift,
    ) = params
    row_count, row_length, feature_width = tokens.shape
    flat_tokens = tokens.reshape(row_count * row_length, feature_width)
    query_states = project(flat_tokens, query_weight, query_bias).astype(jnp.bfloat16)
    key_states = jnp.dot(flat_tokens, key_weight, preferred_element_type=jnp.float32).astype(
        jnp.bfloat16
    )
    value_states = project(flat_tokens, value_weight, value_bias).astype(jnp.bfloat16)
    row_shape = (row_count, row_length, feature_width)
    joined, log_total = lax.map(
        attend_forward,
        (
            query_states.reshape(row_shape),
            key_states.reshape(row_shape),
            value_states.reshape(row_shape),
            segment_ids,
        ),
    )
    joined = joined.reshape(row_count * row_length, feature_width)
    resid_one = flat_tokens.astype(jnp.float32) + project(joined, out_weight, out_bias)
    hidden = norm_piece(resid_one, first_gain.astype(jnp.float32), first_shift.astype(jnp.float32))
    expanded = project(hidden.astype(jnp.bfloat16), up_weight, up_bias)
    active = gelu_exact(expanded).astype(jnp.bfloat16)
    resid_two = hidden + project(active, down_weight, down_bias)
    output = norm_piece(
        resid_two, second_gain.astype(jnp.float32), second_shift.astype(jnp.float32)
    )
    return (
        flat_tokens,
        query_states,
        key_states,
        value_states,
        joined,
        log_total,
        resid_one,
        hidden,
        expanded,
        active,
        resid_two,
        output,
    )


def gather_all(shards):
    packed = jnp.concatenate([piece.reshape(-1) for piece in shards])
    gathered = lax.all_gather(packed, "fsdp", axis=0, tiled=True)
    gathered = gathered.reshape(-1, packed.size)
    params, at = [], 0
    for piece in shards:
        part = gathered[:, at : at + piece.size]
        params.append(part.reshape((-1,) + piece.shape[1:]))
        at += piece.size
    return tuple(params)


def reduce_all(grad_params):
    group = lax.axis_size("fsdp")
    packed = jnp.concatenate(
        [piece.astype(jnp.bfloat16).reshape(group, -1) for piece in grad_params], 1
    )
    share = lax.psum_scatter(packed.reshape(-1), "fsdp", scatter_dimension=0, tiled=True)
    total = lax.psum(share, "rep").astype(jnp.float32)
    totals, at = [], 0
    for piece in grad_params:
        count = piece.size // group
        shape = (piece.shape[0] // group,) + piece.shape[1:]
        totals.append(total[at : at + count].reshape(shape))
        at += count
    return tuple(totals)


def local(
    tokens,
    segment_ids,
    pairing,
    query_weight,
    key_weight,
    value_weight,
    out_weight,
    up_weight,
    down_weight,
    query_bias,
    value_bias,
    out_bias,
    up_bias,
    down_bias,
    first_gain,
    first_shift,
    second_gain,
    second_shift,
):
    shards = (
        query_weight,
        key_weight,
        value_weight,
        out_weight,
        up_weight,
        down_weight,
        query_bias,
        value_bias,
        out_bias,
        up_bias,
        down_bias,
        first_gain,
        first_shift,
        second_gain,
        second_shift,
    )
    params = gather_all(shards)
    row_count, row_length, feature_width = tokens.shape
    states = run_layer(tokens, params, segment_ids)
    output = states[11].reshape(row_count, row_length, feature_width)

    def embed_rows(layer_out):
        return jax.vmap(pool_texts)(layer_out, segment_ids)

    embedded, embed_pullback = jax.vjp(embed_rows, output)
    local_count = row_count * SEGS
    local_embed = embedded.reshape(local_count, feature_width).astype(jnp.bfloat16)
    everything = lax.all_gather(local_embed, ("rep", "fsdp"), axis=0, tiled=True)
    text_count = everything.shape[0]
    pair_count = text_count // 2
    local_ids = lax.axis_index(("rep", "fsdp")) * local_count + jnp.arange(
        local_count, dtype=jnp.int32
    )
    matches = pairing[None, :] == local_ids[:, None]
    position = jnp.sum(jnp.where(matches, jnp.arange(text_count, dtype=jnp.int32)[None, :], 0), 1)
    pair_index = position // 2
    query_flag = position % 2 == 0
    passages = everything[pairing[1::2]]
    logits = (
        jnp.einsum("td,pd->tp", local_embed, passages, preferred_element_type=jnp.float32) * 100.0
    )
    row_peak = jnp.max(logits, 1, keepdims=True)
    exponent = jnp.exp(logits - row_peak)
    softmax_rows = exponent / jnp.sum(exponent, 1, keepdims=True)
    pairs = jnp.arange(pair_count, dtype=jnp.int32)[None, :]
    target = (pairs == pair_index[:, None]).astype(jnp.float32)
    queries = everything[pairing[0::2]]
    whole = jnp.einsum("qd,pd->qp", queries, passages, preferred_element_type=jnp.float32) * 100.0
    peak_all = jnp.max(whole, 1)
    total_all = jnp.sum(jnp.exp(whole - peak_all[:, None]), 1)
    cross = jnp.einsum("td,qd->tq", local_embed, queries, preferred_element_type=jnp.float32) * 100.0
    softmax_columns = jnp.exp(cross - peak_all[None, :]) / total_all[None, :]
    scaled_rows = ((softmax_rows - target) * 100.0).astype(jnp.bfloat16)
    scaled_columns = ((softmax_columns - target) * 100.0).astype(jnp.bfloat16)
    grad_query = jnp.einsum("tp,pd->td", scaled_rows, passages, preferred_element_type=jnp.float32)
    grad_passage = jnp.einsum(
        "tq,qd->td", scaled_columns, queries, preferred_element_type=jnp.float32
    )
    grad_embed = jnp.where(query_flag[:, None], grad_query, grad_passage)
    (grad_output,) = embed_pullback(grad_embed.reshape(row_count, SEGS, feature_width))
    flat_tokens, query_states, key_states, value_states, joined, log_total = states[:6]
    resid_one, hidden, expanded, active, resid_two = states[6:11]
    w_query_full, w_key_full, w_value_full, w_out_full, w_up_full, w_down_full = params[:6]
    first_gain_f = params[11].astype(jnp.float32)
    first_shift_f = params[12].astype(jnp.float32)
    second_gain_f = params[13].astype(jnp.float32)
    second_shift_f = params[14].astype(jnp.float32)
    token_total = row_count * row_length
    norm_out, second_pullback = jax.vjp(norm_piece, resid_two, second_gain_f, second_shift_f)
    grad_resid_two, grad_second_gain, grad_second_shift = second_pullback(
        grad_output.reshape(token_total, feature_width)
    )
    grad_feed = grad_resid_two.astype(jnp.bfloat16)
    grad_down_weight = jnp.einsum(
        "nf,nd->fd", active, grad_feed, preferred_element_type=jnp.float32
    )
    grad_down_bias = jnp.sum(grad_feed.astype(jnp.float32), 0)
    grad_active = jnp.einsum(
        "nd,fd->nf", grad_feed, w_down_full, preferred_element_type=jnp.float32
    )
    gelu_out, gelu_pullback = jax.vjp(gelu_exact, expanded)
    grad_expanded = gelu_pullback(grad_active)[0].astype(jnp.bfloat16)
    grad_up_weight = jnp.einsum(
        "nd,nf->df", hidden.astype(jnp.bfloat16), grad_expanded, preferred_element_type=jnp.float32
    )
    grad_up_bias = jnp.sum(grad_expanded.astype(jnp.float32), 0)
    grad_hidden = grad_resid_two + jnp.einsum(
        "nf,df->nd", grad_expanded, w_up_full, preferred_element_type=jnp.float32
    )
    hidden_out, first_pullback = jax.vjp(norm_piece, resid_one, first_gain_f, first_shift_f)
    grad_resid_one, grad_first_gain, grad_first_shift = first_pullback(grad_hidden)
    grad_branch = grad_resid_one.astype(jnp.bfloat16)
    grad_out_weight = jnp.einsum(
        "nd,ne->de", joined, grad_branch, preferred_element_type=jnp.float32
    )
    grad_out_bias = jnp.sum(grad_branch.astype(jnp.float32), 0)
    grad_joined = jnp.einsum(
        "ne,de->nd", grad_branch, w_out_full, preferred_element_type=jnp.float32
    ).astype(jnp.bfloat16)
    row_shape = (row_count, row_length, feature_width)
    grad_queries, grad_keys, grad_values = lax.map(
        attend_backward,
        (
            query_states.reshape(row_shape),
            key_states.reshape(row_shape),
            value_states.reshape(row_shape),
            segment_ids,
            grad_joined.reshape(row_shape),
            log_total,
        ),
    )
    grad_queries = grad_queries.reshape(token_total, feature_width)
    grad_keys = grad_keys.reshape(token_total, feature_width)
    grad_values = grad_values.reshape(token_total, feature_width)
    grad_query_weight = jnp.einsum(
        "nd,ne->de", flat_tokens, grad_queries, preferred_element_type=jnp.float32
    )
    grad_key_weight = jnp.einsum(
        "nd,ne->de", flat_tokens, grad_keys, preferred_element_type=jnp.float32
    )
    grad_value_weight = jnp.einsum(
        "nd,ne->de", flat_tokens, grad_values, preferred_element_type=jnp.float32
    )
    grad_query_bias = jnp.sum(grad_queries.astype(jnp.float32), 0)
    grad_value_bias = jnp.sum(grad_values.astype(jnp.float32), 0)
    grad_inputs = grad_resid_one
    grad_inputs = grad_inputs + jnp.einsum(
        "ne,de->nd", grad_queries, w_query_full, preferred_element_type=jnp.float32
    )
    grad_inputs = grad_inputs + jnp.einsum(
        "ne,de->nd", grad_keys, w_key_full, preferred_element_type=jnp.float32
    )
    grad_inputs = grad_inputs + jnp.einsum(
        "ne,de->nd", grad_values, w_value_full, preferred_element_type=jnp.float32
    )
    grad_params = (
        grad_query_weight,
        grad_key_weight,
        grad_value_weight,
        grad_out_weight,
        grad_up_weight,
        grad_down_weight,
        grad_query_bias,
        grad_value_bias,
        grad_out_bias,
        grad_up_bias,
        grad_down_bias,
        grad_first_gain,
        grad_first_shift,
        grad_second_gain,
        grad_second_shift,
    )
    totals = reduce_all(grad_params)
    return (
        output.astype(jnp.bfloat16),
        grad_inputs.reshape(row_shape).astype(jnp.bfloat16),
    ) + tuple(totals)


def solution(mesh):
    in_specs = (
        P(("rep", "fsdp"), None, None),
        P(("rep", "fsdp"), None),
        P(),
        P("fsdp", None),
        P("fsdp", None),
        P("fsdp", None),
        P("fsdp", None),
        P("fsdp", None),
        P("fsdp", None),
        P("fsdp"),
        P("fsdp"),
        P("fsdp"),
        P("fsdp"),
        P("fsdp"),
        P("fsdp"),
        P("fsdp"),
        P("fsdp"),
        P("fsdp"),
    )
    out_specs = (
        P(("rep", "fsdp"), None, None),
        P(("rep", "fsdp"), None, None),
        P("fsdp", None),
        P("fsdp", None),
        P("fsdp", None),
        P("fsdp", None),
        P("fsdp", None),
        P("fsdp", None),
        P("fsdp"),
        P("fsdp"),
        P("fsdp"),
        P("fsdp"),
        P("fsdp"),
        P("fsdp"),
        P("fsdp"),
        P("fsdp"),
        P("fsdp"),
    )

    def whole(*arrays):
        fits = (
            mesh.shape["fsdp"] == 8
            and mesh.shape["rep"] == 4
            and arrays[0].shape == (64, 512, 768)
            and arrays[7].shape == (768, 3072)
        )
        return jax.shard_map(
            local_fused if fits else local,
            mesh=mesh,
            in_specs=in_specs,
            out_specs=out_specs,
            check_vma=False,
        )(*arrays)

    return whole
```

```python
import functools

import jax
import jax.numpy as jnp
from jax import lax
from jax.experimental import pallas as pl
from jax.experimental.pallas import tpu as pltpu
from jax.sharding import PartitionSpec as P

H = 12
HD = 64
SEGS = 8
MESH = pl.DeviceIdType.MESH
BF = jnp.bfloat16
F32 = jnp.float32


T = 1024
D = 768
FF = 3072
ROW = 512
NEG = -1e30
QA, QB, QC, WO, UA, UB, DA, DB = range(8)
GROUPS = 8
UNITS = (96, 96, 96, 96, 96, 96, 384, 384)
(XW, YW, S0, ZX, D2, SX, ZY, D1, SY, ZD, SD, SZX, SZY, SZD) = range(14)
ACCS = 4
OWN, XIN, YIN, DIN, ZXIN, ZYIN, ZDIN, READY = range(8)
START, MASKS, VECTORS, PROJECT, ATTEND, MERGE, EXPAND, REDUCE = range(8)
PLAN = {
    (START, 0): ((OWN, QA), (OWN, QB)),
    (MASKS, 0): (
        (XIN, QA), (YIN, QA), (OWN, QC),
    ),
    (VECTORS, 0): (
        (XIN, QB), (YIN, QB), (DIN, QA), (ZXIN, QA), (ZYIN, QA),
        (OWN, WO), (ZXIN, QB), (XIN, QC), (YIN, QC), (DIN, QB),
        (ZYIN, QB), (ZDIN, QA), (OWN, UA), (ZXIN, QC), (XIN, WO),
        (YIN, WO), (READY, QA),
    ),
    (PROJECT, 0): ((DIN, QC), (ZYIN, QC)),
    (PROJECT, 1): ((ZDIN, QB),),
    (ATTEND, 0): ((ZXIN, WO), (ZYIN, WO), (OWN, UB)),
    (ATTEND, 1): ((ZDIN, QC), (DIN, WO), (XIN, UA), (YIN, UA), (READY, QB)),
    (ATTEND, 2): ((ZDIN, WO), (XIN, UB), (YIN, UB)),
    (ATTEND, 3): ((DIN, UA), (ZXIN, UA), (OWN, DA), (READY, QC)),
    (PROJECT, 4): ((ZYIN, UA),),
    (PROJECT, 5): ((DIN, UB),),
    (ATTEND, 4): ((ZXIN, UB), (OWN, DB)),
    (ATTEND, 5): ((ZYIN, UB), (READY, WO)),
    (MERGE, 0): ((ZDIN, UA), (XIN, DA), (YIN, DA)),
    (MERGE, 2): ((ZDIN, UB),),
    (MERGE, 3): ((READY, UA),),
    (EXPAND, 0): ((XIN, DB), (ZXIN, DA), (YIN, DB)),
    (EXPAND, 2): ((DIN, DA), (ZYIN, DA)),
    (EXPAND, 5): ((DIN, DB), (ZXIN, DB), (READY, UB)),
    (EXPAND, 7): ((ZYIN, DB),),
    (EXPAND, 9): ((ZDIN, DA),),
    (EXPAND, 11): ((READY, DA),),
    (REDUCE, 0): ((ZDIN, DB),),
    (REDUCE, 1): ((READY, DB),),
}


DOWN, SLOPE, UP, FIRST, OUT, MIX, HEADS, GROUP, TOKEN, SUMS, SHARE = range(11)
SEND, X1, X2, Z1, Z2, Z3, END = range(11, 18)
BACK = (
    (DOWN, 1), (SEND, 0), (DOWN, 0), (X1, 0), (SEND, 1), (SLOPE, 0), (DOWN, 2), (X1, 1),
    (SEND, 2), (SLOPE, 1), (UP, 1), (X2, 0), (X1, 2), (SEND, 3), (SLOPE, 2), (SLOPE, 3),
    (X2, 1), (X1, 3), (FIRST, 0), (Z1, 0), (FIRST, 1), (FIRST, 2), (X2, 2), (FIRST, 3), (Z1, 1),
    (UP, 0), (SEND, 4), (Z2, 0), (UP, 2), (X2, 3), (X1, 4), (SEND, 5), (OUT, 0), (Z1, 2),
    (X1, 5), (SEND, 6), (Z2, 1), (MIX, 0), (Z3, 0), (Z1, 3), (HEADS, 0), (X2, 4), (X1, 6),
    (Z2, 2), (UP, 3), (SEND, 7), (Z3, 1), (X2, 5), (HEADS, 1), (END, 0), (Z2, 3), (Z1, 4),
    (X1, 7), (GROUP, 0), (SEND, 8), (Z3, 2), (X2, 6), (HEADS, 2), (END, 1), (Z3, 3), (Z2, 4),
    (Z1, 5), (X1, 8), (X2, 7), (HEADS, 3), (END, 2), (Z1, 6), (GROUP, 1), (SEND, 9), (Z3, 4),
    (Z2, 5), (X2, 8), (HEADS, 4), (END, 3), (Z1, 7), (Z2, 6), (X1, 9), (HEADS, 5), (END, 4),
    (Z3, 5), (Z1, 8), (GROUP, 2), (SEND, 10), (TOKEN, 0), (Z3, 6), (Z2, 7), (X2, 9), (X1, 10),
    (GROUP, 3), (SEND, 11), (TOKEN, 1), (END, 5), (Z2, 8), (X1, 11), (SUMS, 0), (Z1, 9),
    (TOKEN, 2), (Z3, 7), (X2, 10), (SHARE, 0), (END, 6), (TOKEN, 3), (X2, 11), (Z1, 10),
    (Z3, 8), (Z2, 9), (SHARE, 1), (END, 7), (Z1, 11), (Z2, 10), (SHARE, 2), (END, 8), (Z3, 9),
    (Z2, 11), (SHARE, 3), (Z3, 10), (Z3, 11), (SHARE, 4), (END, 9), (END, 10), (END, 11),
)
CHUNK_NAMES = tuple(step for step in BACK if step[0] in (DOWN, UP, OUT, GROUP))
NCHUNK = len(CHUNK_NAMES)


def chunk_shape(i):
    kind, number = CHUNK_NAMES[i]
    return (128 if kind == DOWN else 96), (D // 2 if kind == GROUP and number > 1 else D)


def dg(left, right, left_axis, right_axis):
    return lax.dot_general(
        left, right, (((left_axis,), (right_axis,)), ((), ())), preferred_element_type=F32
    )


def split_two(value):
    high = value.astype(BF)
    return high, (value - high.astype(F32)).astype(BF)


def aligned(start, size, step):
    return pl.ds(pl.multiple_of(start, step), size)


def gelu(z):
    return z * (0.5 + 0.5 * lax.erf(z * 0.7071067811865476))


def gelu_slope(z):
    below = 0.5 + 0.5 * lax.erf(z * 0.7071067811865476)
    return below + z * (0.3989422804014327 * jnp.exp(-0.5 * (z * z)))


def normalize(residual):
    centre = jnp.mean(residual, -1, keepdims=True)
    offset = residual - centre
    spread = jnp.mean(offset * offset, -1, keepdims=True)
    scale = lax.rsqrt(spread + 1e-12)
    return offset * scale, scale


def fused_kernel(
    tokens,
    seg,
    pairing,
    bq_in,
    bv_in,
    bo_in,
    bdn_in,
    g1_in,
    s1_in,
    g2_in,
    s2_in,
    bup_in,
    wq_in,
    wk_in,
    wv_in,
    wo_in,
    wup_in,
    wdn_in,
    out_y,
    out_dx,
    out_grads,
    out_vec,
    x_s,
    wqkv,
    wo,
    wup,
    wdn,
    sb,
    vecs,
    upb,
    qkv,
    seg_q,
    seg_k,
    lse,
    lse_t,
    dot_t,
    ao,
    n1,
    scales,
    h1b,
    g_s,
    gp,
    n2,
    df,
    npool,
    meta,
    c_s,
    rsib,
    acc,
    rx,
    ry,
    rx2,
    ry2,
    zs,
    rz1,
    rz2,
    fin,
    vg,
    vr,
    gsend,
    grecv,
    lsem,
    bsend,
    brecv,
    esend,
    erecv,
    xsend,
    xrecv,
    fsend,
    frecv,
    vsend,
    vrecv,
    osem,
):
    rep = lax.axis_index("rep")
    f = lax.axis_index("fsdp")
    core = f & 1
    chip = f >> 1
    pz = rep & 1
    dev_s, dev_x, dev_y, dev_d = (rep, f ^ 1), (rep, f ^ 2), (rep, f ^ 4), (rep, f ^ 6)
    dev_z1, dev_z2, dev_z3 = (rep ^ 1, f), (rep ^ 2, f), (rep ^ 3, f)
    weights = (
        (wqkv, 0, D),
        (wqkv, D, D),
        (wqkv, 2 * D, D),
        (wo, 0, D),
        (wup, 0, FF // 2),
        (wup, FF // 2, FF // 2),
        (wdn, 0, D // 2),
        (wdn, D // 2, D // 2),
    )

    def remote(src, dst, ssem, rsem, dev):
        return pltpu.make_async_remote_copy(
            src_ref=src, dst_ref=dst, send_sem=ssem, recv_sem=rsem, device_id=dev, device_id_type=MESH
        )

    def local_pairs():
        own = aligned(f * 96, 96, 16)
        pairs = []
        for group in range(3):
            for n, ref in enumerate((wq_in, wk_in, wv_in)):
                cols = pl.ds(D * group + 256 * n, 256)
                pairs.append((ref.at[:, pl.ds(256 * group, 256)], wqkv.at[own, cols]))
        pairs.append((wo_in, wo.at[own, :]))
        pairs.append((wup_in, wup.at[own, :]))
        pairs.append((wdn_in, wdn.at[aligned(f * 384, 384, 16), :]))
        pairs.append((tokens, x_s))
        return pairs

    locals_ = [
        pltpu.make_async_copy(src, dst, lsem.at[i]) for i, (src, dst) in enumerate(local_pairs())
    ]
    for copy in locals_:
        copy.start()
    for k, ref in enumerate((bq_in, bv_in, bo_in, bdn_in, g1_in, s1_in, g2_in, s2_in)):
        sb[pl.ds(f, 1), k : k + 1, 0:96] = ref[...].astype(F32).reshape(1, 1, 96)
        sb[pl.ds(f, 1), k : k + 1, 96:128] = jnp.zeros((1, 1, 32), F32)
    for k in range(3):
        sb[pl.ds(f, 1), 8 + k : 9 + k, :] = bup_in[k : k + 1, :].astype(F32).reshape(1, 1, 128)
    sb[pl.ds(f, 1), 11:16, :] = jnp.zeros((1, 5, 128), F32)

    barrier = pltpu.get_barrier_semaphore()
    peers = [(rep, f ^ k) for k in range(1, 8)] + [dev_z1, dev_z2, dev_z3]
    for peer in peers:
        pl.semaphore_signal(barrier, inc=1, device_id=peer, device_id_type=MESH)
    pl.semaphore_wait(barrier, len(peers))

    def full(g, who):
        return who * UNITS[g], UNITS[g]

    def wide(g, who):
        return who * UNITS[g] + (UNITS[g] // 3) * pz, 2 * (UNITS[g] // 3)

    def part_m(g, who):
        return who * UNITS[g] + 2 * (UNITS[g] // 3) * pz, UNITS[g] // 3

    def part_a(g, who):
        return who * UNITS[g] + UNITS[g] // 3, UNITS[g] // 3

    def part_o(g, who):
        return who * UNITS[g] + 2 * (UNITS[g] // 3) * (1 - pz), UNITS[g] // 3

    fx, fy, fd, fs = f ^ 2, f ^ 4, f ^ 6, f ^ 1
    fsx, fsy, fsd = fs ^ 2, fs ^ 4, fs ^ 6
    sent_rows = {
        XW: (wide, f, dev_x),
        YW: (wide, f, dev_y),
        S0: (full, f, dev_s),
        ZX: (part_m, fx, dev_z1),
        D2: (part_m, fx, dev_y),
        SX: (wide, fx, dev_s),
        ZY: (part_m, fy, dev_z1),
        D1: (part_a, fy, dev_x),
        SY: (wide, fy, dev_s),
        ZD: (part_m, fd, dev_z1),
        SD: (wide, fd, dev_s),
        SZX: (part_o, fx, dev_s),
        SZY: (part_o, fy, dev_s),
        SZD: (part_o, fd, dev_s),
    }
    got_rows = {
        XW: (wide, fx),
        YW: (wide, fy),
        S0: (full, fs),
        ZX: (part_o, fx),
        D2: (part_m, fd),
        SX: (wide, fsx),
        ZY: (part_o, fy),
        D1: (part_a, fd),
        SY: (wide, fsy),
        ZD: (part_o, fd),
        SD: (wide, fsd),
        SZX: (part_o, fsx),
        SZY: (part_o, fsy),
        SZD: (part_o, fsd),
    }

    def weight_rows(g, start, size):
        ref, first, width = weights[g]
        return ref.at[aligned(start, size, 16), pl.ds(first, width)]

    def gather_copy(g, piece):
        rows, who, dev = sent_rows[piece]
        start, size = rows(g, who)
        view = weight_rows(g, start, size)
        return remote(view, view, gsend.at[g, piece], grecv.at[g, piece], dev)

    def g_send(g, *pieces):
        for piece in pieces:
            gather_copy(g, piece).start()

    def g_recv(g, *pieces):
        for piece in pieces:
            rows, who = got_rows[piece]
            start, size = rows(g, who)
            view = weight_rows(g, start, size)
            remote(
                view, view, gsend.at[g, piece], grecv.at[g, piece], sent_rows[piece][2]
            ).wait_recv()

    def g_done(g):
        for piece in range(14):
            gather_copy(g, piece).wait_send()

    def step_own(g):
        for i in ((0, 1, 2), (3, 4, 5), (6, 7, 8), (9,), (10,), (), (11,), ())[g]:
            locals_[i].wait()
        g_send(g, XW, YW, S0)

    def step_ready(g):
        g_recv(g, S0, SX, SY, SD, SZX, SZY, SZD)

    def relay(waits, sends):
        def step(g):
            g_recv(g, *waits)
            g_send(g, *sends)

        return step

    gather_steps = {
        OWN: step_own,
        XIN: relay((XW,), (ZX, D2, SX)),
        YIN: relay((YW,), (D1, ZY, SY)),
        DIN: relay((D1, D2), (ZD, SD)),
        ZXIN: relay((ZX,), (SZX,)),
        ZYIN: relay((ZY,), (SZY,)),
        ZDIN: relay((ZD,), (SZD,)),
        READY: step_ready,
    }

    def after(kind, n):
        for step, g in PLAN.get((kind, n), ()):
            gather_steps[step](g)

    def stepped(count, body, kind, first=0):
        def one(i, carry):
            body(i)
            for k in range(count - 1):
                if (kind, first + k) in PLAN:
                    pl.when(i == k)(lambda n=first + k: after(kind, n))
            return carry

        lax.fori_loop(0, count, one, 0)
        after(kind, first + count - 1)

    def small_copy(k):
        view = sb.at[pl.ds(f, 1)]
        return remote(view, view, bsend.at[k - 1], brecv.at[k - 1], (rep, f ^ k))

    step_own(QA)
    for k in range(1, 8):
        small_copy(k).start()
    for step, g in PLAN[START, 0][1:]:
        gather_steps[step](g)

    segf = seg[...].astype(F32)

    def segment_columns():
        for r in range(2):
            lse[pl.ds(r * ROW, ROW), :] = jnp.broadcast_to(segf[r : r + 1, :], (128, ROW)).T

    segment_columns()
    seg_lane = lax.broadcasted_iota(jnp.int32, (T, 128), 1).astype(F32)
    same = jnp.where(lse[...] == seg_lane, 1.0, 0.0)
    seg_q[...] = same.astype(BF)
    seg_k[...] = jnp.where(seg_lane < SEGS, NEG * (1.0 - same), 0.0).astype(BF)

    after(MASKS, 0)

    places = jnp.broadcast_to(pairing[...].astype(F32), (128, 512)).T[:, 0:1]
    texts = lax.broadcasted_iota(jnp.int32, (512, 512), 1).astype(F32)
    order_no = lax.broadcasted_iota(jnp.int32, (512, 512), 0).astype(F32)
    found = jnp.sum(jnp.where(places == texts, order_no, 0.0), 0, keepdims=True)
    meta[...] = jnp.broadcast_to(found, (8, 512))

    for k in range(1, 8):
        view = sb.at[pl.ds(f ^ k, 1)]
        remote(view, view, bsend.at[k - 1], brecv.at[k - 1], (rep, f ^ k)).wait_recv()
    lane = lax.broadcasted_iota(jnp.int32, (128, D), 0)
    column = lax.broadcasted_iota(jnp.int32, (128, D), 1)
    total = jnp.zeros((8, D), F32)
    for k in range(8):
        for j in range(3):
            upb[0:1, k * 384 + 128 * j : k * 384 + 128 * j + 128] = sb[k, 8 + j : 9 + j, :]
        place = jnp.where((column == lane + 96 * k) & (lane < 96), 1.0, 0.0).astype(BF)
        total = total + dg(sb[k, 0:8, :].astype(BF), place, 1, 0)
    vecs[...] = total
    bq, bv, bo, bdn = (vecs[i : i + 1, :] for i in range(4))
    g1, s1, g2, s2 = (vecs[i : i + 1, :] for i in range(4, 8))
    locals_[12].wait()

    after(VECTORS, 0)

    lane_row = lax.broadcasted_iota(jnp.int32, (1, 128), 1)
    even = (lane_row < HD).astype(F32).astype(BF)
    odd = (lane_row >= HD).astype(F32).astype(BF)
    tile_lane = lax.broadcasted_iota(jnp.int32, (256, 128), 1)
    scaling = jnp.where(lax.broadcasted_iota(jnp.int32, (1, D), 1) < 256, 0.125, 1.0).astype(BF)

    def both(value):
        return jnp.concatenate([value * even, value * odd], axis=0)

    def project(group):
        cols = pl.ds(D * group, D)
        part = pl.ds(256 * group, 256)
        bias = jnp.concatenate([vecs[0:1, part], jnp.zeros((1, 256), F32), vecs[1:2, part]], 1)

        def qkv_step(i):
            rows = aligned(i * 512, 512, 512)
            qkv[rows, cols] = (dg(x_s[rows, :], wqkv[:, cols], 1, 0) + bias).astype(BF) * scaling

        stepped(2, qkv_step, PROJECT, 2 * group)

    def attend(r, pair, b):
        kq = aligned(r * ROW + 128 * b, 384, 128)
        qq = aligned(r * ROW + 256 * b, 256, 256)
        at = D * (pair // 2) + 128 * (pair % 2)
        q = qkv[qq, pl.ds(at, 128)]
        v = qkv[kq, pl.ds(at + 512, 128)]
        keys = jnp.concatenate([qkv[kq, pl.ds(at + 256, 128)], seg_k[kq, :]], 1)
        ids = seg_q[qq, :]
        queries = jnp.concatenate(
            [jnp.concatenate([q * even, ids], 1), jnp.concatenate([q * odd, ids], 1)], 0
        )
        scores = dg(queries, keys, 1, 1)
        mixed, peaks, totals = [], [], []
        for h in range(2):
            part = scores[256 * h : 256 * h + 256]
            peak = jnp.max(part, 1, keepdims=True)
            e = jnp.exp(part - peak)
            totals.append(jnp.sum(e, 1, keepdims=True))
            peaks.append(peak)
            mixed.append(dg(e.astype(BF), v, 1, 0))
        first = tile_lane < HD
        total = jnp.where(first, totals[0], totals[1])
        ao[qq, pl.ds(128 * pair, 128)] = (jnp.where(first, mixed[0], mixed[1]) * (1.0 / total)).astype(BF)
        logs = jnp.where(first, peaks[0], peaks[1]) + jnp.log(total)
        lse[qq, :] = jnp.where((tile_lane & 63) == pair, logs, lse[qq, :])

    def attend_group(group):
        def attend_step(r):
            for pair in (2 * group, 2 * group + 1):
                for b in range(2):
                    attend(r, pair, b)

        stepped(2, attend_step, ATTEND, 2 * group)

    lse[...] = jnp.zeros((T, 128), F32)
    for group in range(3):
        project(group)
        attend_group(group)
    for k in range(8):
        turned = lse[128 * k : 128 * k + 128, :].T
        lse_t[0:8, 128 * k : 128 * k + 128] = turned[0:8]
        lse_t[8:16, 128 * k : 128 * k + 128] = turned[64:72]

    def out_step(i):
        rows = aligned(i * 256, 256, 256)
        r1 = x_s[rows, :].astype(F32) + (dg(ao[rows, :], wo[...], 1, 0) + bo)
        n, scale = normalize(r1)
        n1[rows, :] = n
        scales[rows, 0:64] = jnp.broadcast_to(scale, (256, 64))
        h1b[rows, :] = (n * g1 + s1).astype(BF)

    stepped(4, out_step, MERGE)

    def up_step(i):
        cols = aligned((i // 2) * 512, 512, 512)
        rows = aligned((i % 2) * 512, 512, 512)
        z = dg(h1b[rows, :], wup[:, cols], 1, 0) + upb[0:1, cols]
        g_s[rows, cols] = gelu(z).astype(BF)
        gp[rows, cols] = z.astype(BF)

    stepped(12, up_step, EXPAND)

    def slope_part(first, last):
        def part(i, carry):
            rows = aligned(i * 64, 64, 64)
            gp[rows, :] = gelu_slope(gp[rows, :].astype(F32)).astype(BF)
            return carry

        lax.fori_loop(first, last, part, 0)

    npool[...] = jnp.zeros((16, D), F32)
    text_row = lax.broadcasted_iota(jnp.int32, (16, ROW), 0)

    def member_of(r):
        ids = seg[pl.ds(r, 1), :] + 8 * r
        return (text_row == ids).astype(F32)

    left, right = pl.ds(0, D // 2), pl.ds(D // 2, D // 2)

    def down_left(i):
        rows = aligned(i * 512, 512, 512)
        n2[rows, left] = dg(g_s[rows, :], wdn[:, left], 1, 0)

    stepped(2, down_left, REDUCE)
    for r in range(2):
        rows = pl.ds(r * ROW, ROW)
        h1 = n1[rows, :] * g1 + s1
        fed = jnp.concatenate([n2[rows, left], dg(g_s[rows, :], wdn[:, right], 1, 0)], 1)
        n, scale = normalize(h1 + (fed + bdn))
        n2[rows, :] = n
        scales[rows, 64:128] = jnp.broadcast_to(scale, (ROW, 64))
        df[rows, :] = (n * g2 + s2).astype(BF)
        member = member_of(r).astype(BF)
        high, low = split_two(n)
        npool[...] += dg(member, high, 1, 0) + dg(member, low, 1, 0)
    y_copy = pltpu.make_async_copy(df, out_y, osem.at[0])
    y_copy.start()

    lse[0:512, :] = jnp.broadcast_to(meta[0:1, :], (128, 512)).T

    members = jnp.concatenate([member_of(0), member_of(1)], axis=1)
    counts = jnp.sum(members, 1, keepdims=True)
    members = members.astype(BF)
    pooled = npool[...] / counts * g2 + s2
    inverse = lax.rsqrt(jnp.sum(pooled * pooled, 1, keepdims=True) + 1e-06)
    embed = pooled * inverse
    acc[pl.ds(rep, 1), 0, aligned(16 * f, 16, 16), :] = embed.astype(BF).reshape(1, 16, D)

    def e_copy(plane, who, dev, number):
        view = acc.at[pl.ds(plane, 1), 0, aligned(16 * who, 16, 16), :]
        return remote(view, view, esend.at[number], erecv.at[number], dev)

    def e_column(who, number):
        view = acc.at[:, 0, aligned(16 * who, 16, 16), :]
        return remote(view, view, esend.at[number], erecv.at[number], dev_s)

    plane_devs = (dev_x, dev_y, dev_d, dev_s)
    e_sends = [e_copy(rep, f, (rep ^ k, f), k - 1) for k in (1, 2, 3)]
    e_sends += [e_copy(rep, f, dev, 3 + 4 * n) for n, dev in enumerate(plane_devs)]
    for copy in e_sends:
        copy.start()
    slope_part(0, 5)
    for k in (1, 2, 3):
        e_copy(rep ^ k, f, (rep ^ k, f), k - 1).wait_recv()
        for n, dev in enumerate(plane_devs):
            e_sends.append(e_copy(rep ^ k, f, dev, 3 + 4 * n + k))
            e_sends[-1].start()
    slope_part(5, 14)
    for n, who in enumerate((fx, fy, fd)):
        for k in range(4):
            e_copy(rep ^ k, who, plane_devs[n], 3 + 4 * n + k).wait_recv()
        e_sends.append(e_column(who, 19 + n))
        e_sends[-1].start()
    slope_part(14, 16)
    for k in range(4):
        e_copy(rep ^ k, fs, dev_s, 15 + k).wait_recv()
    for n, who in enumerate((fsx, fsy, fsd)):
        e_column(who, 19 + n).wait_recv()
    for copy in e_sends:
        copy.wait_send()
    for g in range(GROUPS):
        g_done(g)
    for k in range(1, 8):
        small_copy(k).wait_send()

    every = jnp.concatenate([acc[k, 0] for k in range(4)], 0)
    pos_all = meta[0:1, :]
    pair_all = jnp.floor(pos_all * 0.5)
    second_all = pos_all - 2.0 * pair_all
    pos_col = lse[0:512, 0:1]
    second_col = pos_col - 2.0 * jnp.floor(pos_col * 0.5)
    whole = dg(every, every, 1, 1) * 100.0
    whole = jnp.where(second_col > 0.5, whole, NEG)
    peak_all = jnp.max(whole, 0, keepdims=True)
    total_all = jnp.sum(jnp.exp(whole - peak_all), 0, keepdims=True)
    own = embed.astype(BF)
    mine = dg(own, every, 1, 1) * 100.0
    pos_own = lse[aligned((rep * 8 + f) * 16, 16, 16), 0:1]
    pair_own = jnp.floor(pos_own * 0.5)
    second_own = pos_own - 2.0 * pair_own
    same_pair = jnp.where(pair_own == pair_all, 1.0, 0.0)
    rows_masked = jnp.where(second_all > 0.5, mine, NEG)
    row_peak = jnp.max(rows_masked, 1, keepdims=True)
    row_e = jnp.exp(rows_masked - row_peak)
    soft_rows = row_e / jnp.sum(row_e, 1, keepdims=True)
    soft_cols = jnp.exp(jnp.where(second_all > 0.5, NEG, mine - peak_all)) / total_all
    d_rows = (soft_rows - same_pair) * second_all
    d_cols = (soft_cols - same_pair) * (1.0 - second_all)
    d_logits = (jnp.where(second_own > 0.5, d_cols, d_rows) * 100.0).astype(BF)
    d_embed = dg(d_logits, every, 1, 0)
    d_pooled = (d_embed - embed * jnp.sum(embed * d_embed, 1, keepdims=True)) * inverse
    d_each = d_pooled / counts
    vg[...] = jnp.zeros((16, D), F32)
    vg[6:7, :] = jnp.sum(d_each * npool[...], 0, keepdims=True)
    vg[7:8, :] = jnp.sum(d_pooled, 0, keepdims=True)
    u_text = d_each * g2
    u_text = u_text - jnp.mean(u_text, 1, keepdims=True)
    u_high, u_low = split_two(u_text)
    u_both = jnp.concatenate([u_high, u_low], 0)
    y_copy.wait()

    for i in range(4):
        rows = pl.ds(i * 256, 256)
        part = members[:, 256 * i : 256 * i + 256]
        u = dg(jnp.concatenate([part, part], 0), u_both, 0, 0)
        n = n2[rows, :]
        d = (u - n * jnp.mean(u * n, 1, keepdims=True)) * scales[rows, 64:65]
        n2[rows, :] = d
        db = d.astype(BF)
        df[rows, :] = db
        vg[3:4, :] += jnp.sum(db.astype(F32), 0, keepdims=True)

    def small_ring(i):
        return i % 2

    def long_ring(i):
        return i % 4

    ch_x, ch_y, ch_d = chip ^ 1, chip ^ 2, chip ^ 3
    inner = (((rep + 1) >> 1) & 1) == 1
    outer = jnp.logical_not(inner)

    def view_s(i):
        (u, w), s = chunk_shape(i), small_ring(i)
        src = c_s.at[s, :, pl.ds(1 - core, 1), pl.ds(0, u), pl.ds(0, w)]
        dst = rsib.at[s, :, :, pl.ds(0, u), pl.ds(0, w)]
        return remote(src, dst, xsend.at[s, 0], xrecv.at[s, 0], dev_s)

    def views_x1(i):
        (u, w), s, a = chunk_shape(i), long_ring(i), i % ACCS
        half = u // 2
        low, high, cols = pl.ds(0, half), pl.ds(half, half), pl.ds(0, w)
        pieces = (
            (ch_x, low, rx.at[s, 0, low, cols], dev_x),
            (ch_d, low, rx.at[s, 1, low, cols], dev_x),
            (ch_y, high, ry.at[s, 0, low, cols], dev_y),
            (ch_d, high, ry.at[s, 1, low, cols], dev_y),
        )
        return [
            remote(acc.at[a, who, rows, cols], dst, xsend.at[s, 1 + n], xrecv.at[s, 1 + n], dev)
            for n, (who, rows, dst, dev) in enumerate(pieces)
        ]

    def views_x2(i):
        (u, w), s, a = chunk_shape(i), long_ring(i), i % ACCS
        half = u // 2
        low, high, cols = pl.ds(0, half), pl.ds(half, half), pl.ds(0, w)
        return [
            remote(acc.at[a, ch_y, low, cols], ry2.at[s, low, cols], xsend.at[s, 5], xrecv.at[s, 5], dev_y),
            remote(acc.at[a, ch_x, high, cols], rx2.at[s, low, cols], xsend.at[s, 6], xrecv.at[s, 6], dev_x),
        ]

    def view_z1(i):
        (u, w), s = chunk_shape(i), long_ring(i)
        rows, cols = pl.ds(0, u), pl.ds(0, w)
        return remote(
            zs.at[s, rows, cols], rz1.at[s, rows, cols], xsend.at[s, 7], xrecv.at[s, 7], dev_z1
        )

    def view_z2(i):
        (u, w), s = chunk_shape(i), long_ring(i)
        rows, cols = pl.ds(0, u), pl.ds(0, w)
        return remote(
            zs.at[s, rows, cols], rz2.at[s, rows, cols], xsend.at[s, 8], xrecv.at[s, 8], dev_z3
        )

    def view_z3(i):
        u, w = chunk_shape(i)
        place = fin.at[i, pl.ds(0, u), pl.ds(0, w)]
        return remote(place, place, fsend.at[i], frecv.at[i], dev_z1)

    def stage_x1(i):
        (u, w), s, a = chunk_shape(i), small_ring(i), i % ACCS
        view_s(i).wait()
        for ch in range(4):
            acc[a, ch, 0:u, 0:w] = c_s[s, ch, pl.ds(core, 1), 0:u, 0:w][0] + rsib[s, ch, 0, 0:u, 0:w]
        for copy in views_x1(i):
            copy.start()

    def stage_x2(i):
        (u, w), s, a = chunk_shape(i), long_ring(i), i % ACCS
        half = u // 2
        for copy in views_x1(i):
            copy.wait()
        acc[a, pl.ds(ch_y, 1), 0:half, 0:w] += rx[s, 1:2, 0:half, 0:w]
        acc[a, pl.ds(ch_x, 1), half:u, 0:w] += ry[s, 1:2, 0:half, 0:w]
        for copy in views_x2(i):
            copy.start()
        acc[a, pl.ds(chip, 1), 0:half, 0:w] += rx[s, 0:1, 0:half, 0:w]
        acc[a, pl.ds(chip, 1), half:u, 0:w] += ry[s, 0:1, 0:half, 0:w]

    def stage_z1(i):
        (u, w), s, a = chunk_shape(i), long_ring(i), i % ACCS
        half = u // 2
        for copy in views_x2(i):
            copy.wait()
        zs[s, 0:half, 0:w] = acc[a, pl.ds(chip, 1), 0:half, 0:w][0] + ry2[s, 0:half, 0:w]
        zs[s, half:u, 0:w] = acc[a, pl.ds(chip, 1), half:u, 0:w][0] + rx2[s, 0:half, 0:w]

        @pl.when(outer)
        def _():
            view_z1(i).start()

    def stage_z2(i):
        (u, w), s = chunk_shape(i), long_ring(i)

        @pl.when(outer)
        def _():
            view_z1(i).wait_send()

        @pl.when(inner)
        def _():
            view_z1(i).wait_recv()
            zs[s, 0:u, 0:w] += rz1[s, 0:u, 0:w]
            view_z2(i).start()

    def stage_z3(i):
        (u, w), s = chunk_shape(i), long_ring(i)

        @pl.when(inner)
        def _():
            view_z2(i).wait()
            fin[i, 0:u, 0:w] = zs[s, 0:u, 0:w] + rz2[s, 0:u, 0:w]
            view_z3(i).start()

    def out_copy(i):
        u, w = chunk_shape(i)
        rows, cols = pl.ds(0, u), pl.ds(0, w)
        return pltpu.make_async_copy(fin.at[i, rows, cols], out_grads.at[i, rows, cols], osem.at[2 + i])

    def stage_end(i):
        @pl.when(inner)
        def _():
            view_z3(i).wait_send()

        @pl.when(outer)
        def _():
            view_z3(i).wait_recv()

        out_copy(i).start()

    def store_slabs(i, hh, result):
        (u, w), s = chunk_shape(i), small_ring(i)
        for k in range(4):
            c_s[s, pl.ds(2 * hh + k // 2, 1), k % 2, 0:u, 0:w] = (
                result[u * k : u * k + u].astype(BF).reshape(1, u, w)
            )

    def chunk(i, left_of, right):
        def half(hh, carry):
            store_slabs(i, hh, dg(left_of(hh), right(), 0, 0))
            return carry

        lax.fori_loop(0, 2, half, 0)

    def down_chunk(i, j):
        def left_of(hh):
            return jnp.concatenate(
                [g_s[:, aligned((4 * hh + k) * 384 + j * 128, 128, 128)] for k in range(4)], 1
            )

        chunk(i, left_of, lambda: df[...])

    def slope(j):
        cols = pl.ds(D * j, D)

        def slope_step(m, carry):
            rows = aligned(m * 512, 512, 512)
            dz = (dg(df[rows, :], wdn[cols, :], 1, 1) * gp[rows, cols].astype(F32)).astype(BF)
            gp[rows, cols] = dz
            vg[8 + j : 9 + j, :] += jnp.sum(dz.astype(F32), 0, keepdims=True)
            return carry

        lax.fori_loop(0, 2, slope_step, 0)

    def up_chunk(i, j):
        chunk(i, lambda hh: h1b[:, aligned(384 * hh, 384, 128)], lambda: gp[:, pl.ds(D * j, D)])

    def first_step(i, carry):
        rows = aligned(i * 256, 256, 256)
        dh = n2[rows, :] + dg(gp[rows, :], wup[...], 1, 1)
        n = n1[rows, :]
        vg[4:5, :] += jnp.sum(dh * n, 0, keepdims=True)
        vg[5:6, :] += jnp.sum(dh, 0, keepdims=True)
        u = dh * g1
        d = (u - jnp.mean(u, 1, keepdims=True) - n * jnp.mean(u * n, 1, keepdims=True)) * scales[rows, 0:1]
        n2[rows, :] = d
        db = d.astype(BF)
        df[rows, :] = db
        vg[2:3, :] += jnp.sum(db.astype(F32), 0, keepdims=True)
        return carry

    def out_chunk(i):
        chunk(i, lambda hh: ao[:, aligned(384 * hh, 384, 128)], lambda: df[...])

    def mask_place(r, b):
        m = 2 * r + b
        return pl.ds(384 * (m // 3), 384), pl.ds(256 * (m % 3), 256)

    def place_masks():
        segment_columns()
        for r in range(2):
            for b in range(2):
                key_side = lse[pl.ds(r * ROW + 128 * b, 384), 0:1]
                query_side = segf[r : r + 1, 256 * b : 256 * b + 256]
                n1[mask_place(r, b)] = jnp.where(key_side == query_side, 0.0, NEG)

    head = lax.broadcasted_iota(jnp.int32, (D, 128), 0) // HD
    head_lane = lax.broadcasted_iota(jnp.int32, (D, 128), 1)
    one_hot = jnp.where(head_lane == head // 2 + 8 * (head % 2), 1.0, 0.0).astype(BF)

    def mix_step(m, carry):
        rows = aligned(m * 512, 512, 512)
        da = dg(df[rows, :], wo[...], 1, 1).astype(BF)
        high, low = split_two(da.astype(F32) * ao[rows, :].astype(F32))
        dots = dg(high, one_hot, 1, 0) + dg(low, one_hot, 1, 0)
        dot_t[:, rows] = dots.T[0:16]
        ao[rows, :] = da
        return carry

    def mix():
        place_masks()
        lax.fori_loop(0, 2, mix_step, 0)

    def attend_back(r, pair, at):
        grads_k, grads_v = [], []
        for b in range(2):
            kq = aligned(r * ROW + 128 * b, 384, 128)
            qq = aligned(r * ROW + 256 * b, 256, 256)
            k = qkv[kq, aligned(at + 256, 128, 128)]
            v = qkv[kq, aligned(at + 512, 128, 128)]
            q = qkv[qq, aligned(at, 128, 128)]
            da = ao[qq, aligned(pair * 128, 128, 128)]
            scores = dg(both(k), q, 1, 1)
            dp = dg(both(v), da, 1, 1)
            bias = n1[mask_place(r, b)]
            probs, dscores = [], []
            for h in range(2):
                rows = slice(384 * h, 384 * h + 384)
                prob = jnp.exp(scores[rows] + bias - lse_t[pair + 8 * h : pair + 8 * h + 1, qq])
                probs.append(prob.astype(BF))
                dscores.append((prob * (dp[rows] - dot_t[pair + 8 * h : pair + 8 * h + 1, qq])).astype(BF))
            grads_v.append(dg(jnp.concatenate(probs, 1), both(da), 1, 0))
            grads_k.append(dg(jnp.concatenate(dscores, 1), both(q), 1, 0))
            even_q, odd_q = dg(k, dscores[0], 0, 0), dg(k, dscores[1], 0, 0)
            dq = jnp.concatenate([even_q[0:HD], odd_q[HD : 2 * HD]], 0).T
            g_s[qq, aligned(at, 128, 128)] = (dq * 0.125).astype(BF)
        for off, (first, second) in ((256, grads_k), (512, grads_v)):
            cols = aligned(at + off, 128, 128)
            g_s[aligned(r * ROW, 128, 128), cols] = first[0:128].astype(BF)
            g_s[aligned(r * ROW + 128, 256, 128), cols] = (first[128:384] + second[0:256]).astype(BF)
            g_s[aligned(r * ROW + 384, 128, 128), cols] = second[256:384].astype(BF)

    def heads(pair):
        def back_step(r, carry):
            attend_back(r, pair, D * (pair // 2) + 128 * (pair % 2))
            return carry

        lax.fori_loop(0, 2, back_step, 0, unroll=True)

    def group_chunk(i, group):
        def right():
            if group < 2:
                return g_s[:, pl.ds(D * group, D)]
            first = 2 * D + 128 * (group - 2)
            return jnp.concatenate([g_s[:, pl.ds(first + 256 * n, 128)] for n in range(3)], 1)

        chunk(i, lambda hh: x_s[:, aligned(384 * hh, 384, 128)], right)

    def vector_sums():
        for row, off in ((0, 0), (1, 512)):
            for group in range(3):
                vg[row : row + 1, 256 * group : 256 * group + 256] = jnp.sum(
                    g_s[:, pl.ds(D * group + off, 256)].astype(F32), 0, keepdims=True
                )
        v_copy(0).start()

    order = (dev_s, dev_x, dev_y, dev_z1, dev_z2)

    def v_copy(n):
        return remote(vg, vr.at[n], vsend.at[n], vrecv.at[n], order[n])

    def v_step(n):
        v_copy(n).wait()
        vg[...] = vg[...] + vr[n]
        if n + 1 < len(order):
            v_copy(n + 1).start()

    def token_step(i, carry):
        rows = aligned(i * 256, 256, 256)
        h1b[rows, :] = (n2[rows, :] + dg(g_s[rows, pl.ds(0, 3 * D)], wqkv[...], 1, 1)).astype(BF)
        return carry

    dx_copy = pltpu.make_async_copy(h1b, out_dx, osem.at[1])

    numbers = {name: i for i, name in enumerate(CHUNK_NAMES)}
    stages = {
        X1: stage_x1,
        X2: stage_x2,
        Z1: stage_z1,
        Z2: stage_z2,
        Z3: stage_z3,
        END: stage_end,
        SHARE: v_step,
        SLOPE: slope,
        HEADS: heads,
    }
    for kind, n in BACK:
        if kind in stages:
            stages[kind](n)
        elif kind == SEND:
            view_s(n).start()
        elif kind == DOWN:
            down_chunk(numbers[kind, n], n)
        elif kind == UP:
            up_chunk(numbers[kind, n], n)
        elif kind == OUT:
            out_chunk(numbers[kind, n])
        elif kind == GROUP:
            group_chunk(numbers[kind, n], n)
        elif kind == FIRST:
            lax.fori_loop(n, n + 1, first_step, 0)
        elif kind == MIX:
            mix()
        elif kind == SUMS:
            vector_sums()
        elif kind == TOKEN:
            lax.fori_loop(n, n + 1, token_step, 0)
            if n == 3:
                dx_copy.start()

    out_vec[8:16, 0:128] = jnp.zeros((8, 128), F32)
    for k in range(8):

        @pl.when(f == k)
        def _():
            out_vec[0:8, 0:96] = vg[0:8, 96 * k : 96 * k + 96]
            line = jnp.concatenate([vg[8 + n : 9 + n, :] for n in range(4)], 1)
            out_vec[8:9, 0:384] = line[:, 384 * k : 384 * k + 384]

    dx_copy.wait()
    for i in range(NCHUNK):
        out_copy(i).wait()


def finish_kernel(
    raw_y,
    raw_dx,
    raw_grads,
    vec,
    out_y,
    out_dx,
    out_gq,
    out_gk,
    out_gv,
    out_go,
    out_gup,
    out_gdn,
    *rest,
):
    vectors = rest[:9]
    y, dx, grads, gq, gk, gv, go, gup, gdn, sems = rest[9:]
    reads = [(raw_y, y), (raw_dx, dx), (raw_grads, grads)]
    reads = [pltpu.make_async_copy(src, dst, sems.at[i]) for i, (src, dst) in enumerate(reads)]
    writes = [(gq, out_gq), (gk, out_gk), (gv, out_gv), (go, out_go), (gup, out_gup), (gdn, out_gdn)]
    writes = [(y, out_y), (dx, out_dx)] + writes
    writes = [pltpu.make_async_copy(src, dst, sems.at[3 + i]) for i, (src, dst) in enumerate(writes)]
    for copy in reads:
        copy.start()
    for n, row in enumerate((0, 1, 2, 8, 3, 4, 5, 6, 7)):
        if row == 8:
            for k in range(3):
                vectors[n][k : k + 1, :] = vec[8:9, 128 * k : 128 * k + 128]
        else:
            vectors[n][...] = vec[row : row + 1, 0:96]
    for n in range(2):
        reads[n].wait()
        writes[n].start()
    reads[2].wait()
    for i, (kind, j) in enumerate(CHUNK_NAMES):
        if kind == DOWN:
            gdn[128 * j : 128 * j + 128, :] = grads[i].astype(F32)
        elif kind == UP:
            gup[:, D * j : D * j + D] = grads[i, 0:96].astype(F32)
        elif kind == OUT:
            go[...] = grads[i, 0:96].astype(F32)
        else:
            first, width = (256 * j, 256) if j < 2 else (512 + 128 * (j - 2), 128)
            for n, ref in enumerate((gq, gk, gv)):
                ref[:, first : first + width] = grads[i, 0:96, width * n : width * n + width].astype(F32)
    for copy in writes[2:]:
        copy.start()
    for copy in writes:
        copy.wait()


def finish_call(raw_y, raw_dx, grads, vec):
    shape = jax.ShapeDtypeStruct
    any_ = pl.BlockSpec(memory_space=pl.ANY)
    vmem = pl.BlockSpec(memory_space=pltpu.VMEM)
    shapes = ((1, 96),) * 3 + ((3, 128),) + ((1, 96),) * 5
    weights = ((96, D), (96, D), (96, D), (96, D), (96, FF), (384, D))
    return pl.pallas_call(
        finish_kernel,
        name="write_results",
        out_shape=(shape((T, D), BF), shape((T, D), BF))
        + tuple(shape(dims, F32) for dims in weights)
        + tuple(shape(dims, F32) for dims in shapes),
        in_specs=[any_, any_, any_, vmem],
        out_specs=(any_,) * 8 + (vmem,) * 9,
        scratch_shapes=[pltpu.VMEM((T, D), BF), pltpu.VMEM((T, D), BF), pltpu.VMEM((NCHUNK, 128, D), BF)]
        + [pltpu.VMEM(dims, F32) for dims in weights]
        + [pltpu.SemaphoreType.DMA((11,))],
        compiler_params=pltpu.CompilerParams(vmem_limit_bytes=60 * 2**20),
    )(raw_y, raw_dx, grads, vec)


def fused_call(tokens, seg, pairing, vectors, shards):
    vm = lambda shape, dtype: pltpu.VMEM(shape, dtype)
    sem = pltpu.SemaphoreType.DMA
    scratch = [
        vm((T, D), BF),
        vm((D, 3 * D), BF),
        vm((D, D), BF),
        vm((D, FF), BF),
        vm((FF, D), BF),
        vm((8, 16, 128), F32),
        vm((8, D), F32),
        vm((8, FF), F32),
        vm((T, 3 * D), BF),
        vm((T, 128), BF),
        vm((T, 128), BF),
        vm((T, 128), F32),
        vm((16, T), F32),
        vm((16, T), F32),
        vm((T, D), BF),
        vm((T, D), F32),
        vm((T, 128), F32),
        vm((T, D), BF),
        vm((T, FF), BF),
        vm((T, FF), BF),
        vm((T, D), F32),
        vm((T, D), BF),
        vm((16, D), F32),
        vm((8, 512), F32),
        vm((2, 4, 2, 128, D), BF),
        vm((2, 4, 1, 128, D), BF),
        vm((ACCS, 4, 128, D), BF),
        vm((4, 2, 64, D), BF),
        vm((4, 2, 64, D), BF),
        vm((4, 64, D), BF),
        vm((4, 64, D), BF),
        vm((4, 128, D), BF),
        vm((4, 128, D), BF),
        vm((4, 128, D), BF),
        vm((NCHUNK, 128, D), BF),
        vm((16, D), F32),
        vm((5, 16, D), F32),
        sem((GROUPS, 14)),
        sem((GROUPS, 14)),
        sem((13,)),
        sem((7,)),
        sem((7,)),
        sem((22,)),
        sem((22,)),
        sem((4, 9)),
        sem((4, 9)),
        sem((NCHUNK,)),
        sem((NCHUNK,)),
        sem((5,)),
        sem((5,)),
        sem((2 + NCHUNK,)),
    ]
    shape = jax.ShapeDtypeStruct
    any_ = pl.BlockSpec(memory_space=pl.ANY)
    vmem = pl.BlockSpec(memory_space=pltpu.VMEM)
    return pl.pallas_call(
        fused_kernel,
        name="layer_step",
        out_shape=(
            shape((T, D), BF),
            shape((T, D), BF),
            shape((NCHUNK, 128, D), BF),
            shape((16, 384), F32),
        ),
        in_specs=[any_, vmem, vmem] + [vmem] * 9 + [any_] * 6,
        out_specs=(any_,) * 3 + (vmem,),
        scratch_shapes=scratch,
        compiler_params=pltpu.CompilerParams(
            collective_id=0, has_side_effects=True, vmem_limit_bytes=64 * 2**20
        ),
        cost_estimate=pl.CostEstimate(
            flops=60 * 10**9, bytes_accessed=30 * 2**20, transcendentals=10**7
        ),
    )(tokens, seg, pairing, *vectors, *shards[:6])


def local_fused(tokens, segment_ids, pairing, *shards):
    width = tokens.shape[-1]
    (bq, bv, bo, bup, bdn, g1, s1, g2, s2) = shards[6:]
    vectors = [piece.reshape(1, -1) for piece in (bq, bv, bo, bdn, g1, s1, g2, s2)]
    vectors.append(bup.reshape(3, 128))
    raw = fused_call(tokens.reshape(-1, width), segment_ids, pairing.reshape(1, -1), vectors, shards)
    results = finish_call(*raw)
    return (
        (results[0].reshape(tokens.shape), results[1].reshape(tokens.shape))
        + tuple(results[2:8])
        + tuple(piece.reshape(-1) for piece in results[8:])
    )


def norm_piece(residual, gain_vector, shift_vector):
    centre = jnp.mean(residual, -1, keepdims=True)
    offset = residual - centre
    spread = jnp.mean(offset * offset, -1, keepdims=True)
    return offset * lax.rsqrt(spread + 1e-12) * gain_vector + shift_vector


def gelu_exact(argument):
    return jax.nn.gelu(argument, approximate=False)


def pool_texts(layer_out, segments):
    member = (segments[:, None] == jnp.arange(SEGS)[None, :]).astype(jnp.float32)
    totals = jnp.dot(member.T, layer_out, precision=lax.Precision.HIGHEST)
    counts = jnp.sum(member, 0)
    pooled = totals / counts[:, None]
    return pooled * lax.rsqrt(jnp.sum(pooled * pooled, -1, keepdims=True) + 1e-06)


def project(inputs, weight, bias_vector):
    return jnp.dot(inputs, weight, preferred_element_type=jnp.float32) + bias_vector.astype(
        jnp.float32
    )


def head_scores(query_states, key_states, segments):
    row_length = query_states.shape[0]
    scores = jnp.einsum(
        "qhd,khd->hqk",
        query_states.reshape(row_length, H, HD),
        key_states.reshape(row_length, H, HD),
        preferred_element_type=jnp.float32,
    ) * HD ** (-0.5)
    same_text = segments[:, None] == segments[None, :]
    return jnp.where(same_text[None], scores, -1e30)


def attend_forward(pieces):
    query_states, key_states, value_states, segments = pieces
    row_length = query_states.shape[0]
    scores = head_scores(query_states, key_states, segments)
    row_peak = jnp.max(scores, -1, keepdims=True)
    exponent = jnp.exp(scores - row_peak)
    row_total = jnp.sum(exponent, -1, keepdims=True)
    probability = (exponent / row_total).astype(jnp.bfloat16)
    mixture = jnp.einsum(
        "hqk,khd->qhd",
        probability,
        value_states.reshape(row_length, H, HD),
        preferred_element_type=jnp.float32,
    )
    return (mixture.reshape(row_length, H * HD).astype(jnp.bfloat16), row_peak + jnp.log(row_total))


def attend_backward(pieces):
    query_states, key_states, value_states, segments, grad_mixture, log_total = pieces
    row_length = query_states.shape[0]
    query_heads = query_states.reshape(row_length, H, HD)
    key_heads = key_states.reshape(row_length, H, HD)
    value_heads = value_states.reshape(row_length, H, HD)
    grad_heads = grad_mixture.reshape(row_length, H, HD)
    probability = jnp.exp(head_scores(query_states, key_states, segments) - log_total)
    grad_probability = jnp.einsum(
        "qhd,khd->hqk", grad_heads, value_heads, preferred_element_type=jnp.float32
    )
    grad_values = jnp.einsum(
        "hqk,qhd->khd",
        probability.astype(jnp.bfloat16),
        grad_heads,
        preferred_element_type=jnp.float32,
    )
    grad_scores = probability * (
        grad_probability - jnp.sum(probability * grad_probability, -1, keepdims=True)
    )
    grad_scores = grad_scores.astype(jnp.bfloat16)
    score_scale = HD ** (-0.5)
    grad_queries = (
        jnp.einsum("hqk,khd->qhd", grad_scores, key_heads, preferred_element_type=jnp.float32)
        * score_scale
    )
    grad_keys = (
        jnp.einsum("hqk,qhd->khd", grad_scores, query_heads, preferred_element_type=jnp.float32)
        * score_scale
    )
    return (
        grad_queries.reshape(row_length, H * HD).astype(jnp.bfloat16),
        grad_keys.reshape(row_length, H * HD).astype(jnp.bfloat16),
        grad_values.reshape(row_length, H * HD).astype(jnp.bfloat16),
    )


def run_layer(tokens, params, segment_ids):
    (
        query_weight,
        key_weight,
        value_weight,
        out_weight,
        up_weight,
        down_weight,
        query_bias,
        value_bias,
        out_bias,
        up_bias,
        down_bias,
        first_gain,
        first_shift,
        second_gain,
        second_shift,
    ) = params
    row_count, row_length, feature_width = tokens.shape
    flat_tokens = tokens.reshape(row_count * row_length, feature_width)
    query_states = project(flat_tokens, query_weight, query_bias).astype(jnp.bfloat16)
    key_states = jnp.dot(flat_tokens, key_weight, preferred_element_type=jnp.float32).astype(
        jnp.bfloat16
    )
    value_states = project(flat_tokens, value_weight, value_bias).astype(jnp.bfloat16)
    row_shape = (row_count, row_length, feature_width)
    joined, log_total = lax.map(
        attend_forward,
        (
            query_states.reshape(row_shape),
            key_states.reshape(row_shape),
            value_states.reshape(row_shape),
            segment_ids,
        ),
    )
    joined = joined.reshape(row_count * row_length, feature_width)
    resid_one = flat_tokens.astype(jnp.float32) + project(joined, out_weight, out_bias)
    hidden = norm_piece(resid_one, first_gain.astype(jnp.float32), first_shift.astype(jnp.float32))
    expanded = project(hidden.astype(jnp.bfloat16), up_weight, up_bias)
    active = gelu_exact(expanded).astype(jnp.bfloat16)
    resid_two = hidden + project(active, down_weight, down_bias)
    output = norm_piece(
        resid_two, second_gain.astype(jnp.float32), second_shift.astype(jnp.float32)
    )
    return (
        flat_tokens,
        query_states,
        key_states,
        value_states,
        joined,
        log_total,
        resid_one,
        hidden,
        expanded,
        active,
        resid_two,
        output,
    )


def gather_all(shards):
    packed = jnp.concatenate([piece.reshape(-1) for piece in shards])
    gathered = lax.all_gather(packed, "fsdp", axis=0, tiled=True)
    gathered = gathered.reshape(-1, packed.size)
    params, at = [], 0
    for piece in shards:
        part = gathered[:, at : at + piece.size]
        params.append(part.reshape((-1,) + piece.shape[1:]))
        at += piece.size
    return tuple(params)


def reduce_all(grad_params):
    group = lax.axis_size("fsdp")
    packed = jnp.concatenate(
        [piece.astype(jnp.bfloat16).reshape(group, -1) for piece in grad_params], 1
    )
    share = lax.psum_scatter(packed.reshape(-1), "fsdp", scatter_dimension=0, tiled=True)
    total = lax.psum(share, "rep").astype(jnp.float32)
    totals, at = [], 0
    for piece in grad_params:
        count = piece.size // group
        shape = (piece.shape[0] // group,) + piece.shape[1:]
        totals.append(total[at : at + count].reshape(shape))
        at += count
    return tuple(totals)


def local(
    tokens,
    segment_ids,
    pairing,
    query_weight,
    key_weight,
    value_weight,
    out_weight,
    up_weight,
    down_weight,
    query_bias,
    value_bias,
    out_bias,
    up_bias,
    down_bias,
    first_gain,
    first_shift,
    second_gain,
    second_shift,
):
    shards = (
        query_weight,
        key_weight,
        value_weight,
        out_weight,
        up_weight,
        down_weight,
        query_bias,
        value_bias,
        out_bias,
        up_bias,
        down_bias,
        first_gain,
        first_shift,
        second_gain,
        second_shift,
    )
    params = gather_all(shards)
    row_count, row_length, feature_width = tokens.shape
    states = run_layer(tokens, params, segment_ids)
    output = states[11].reshape(row_count, row_length, feature_width)

    def embed_rows(layer_out):
        return jax.vmap(pool_texts)(layer_out, segment_ids)

    embedded, embed_pullback = jax.vjp(embed_rows, output)
    local_count = row_count * SEGS
    local_embed = embedded.reshape(local_count, feature_width).astype(jnp.bfloat16)
    everything = lax.all_gather(local_embed, ("rep", "fsdp"), axis=0, tiled=True)
    text_count = everything.shape[0]
    pair_count = text_count // 2
    local_ids = lax.axis_index(("rep", "fsdp")) * local_count + jnp.arange(
        local_count, dtype=jnp.int32
    )
    matches = pairing[None, :] == local_ids[:, None]
    position = jnp.sum(jnp.where(matches, jnp.arange(text_count, dtype=jnp.int32)[None, :], 0), 1)
    pair_index = position // 2
    query_flag = position % 2 == 0
    passages = everything[pairing[1::2]]
    logits = (
        jnp.einsum("td,pd->tp", local_embed, passages, preferred_element_type=jnp.float32) * 100.0
    )
    row_peak = jnp.max(logits, 1, keepdims=True)
    exponent = jnp.exp(logits - row_peak)
    softmax_rows = exponent / jnp.sum(exponent, 1, keepdims=True)
    pairs = jnp.arange(pair_count, dtype=jnp.int32)[None, :]
    target = (pairs == pair_index[:, None]).astype(jnp.float32)
    queries = everything[pairing[0::2]]
    whole = jnp.einsum("qd,pd->qp", queries, passages, preferred_element_type=jnp.float32) * 100.0
    peak_all = jnp.max(whole, 1)
    total_all = jnp.sum(jnp.exp(whole - peak_all[:, None]), 1)
    cross = jnp.einsum("td,qd->tq", local_embed, queries, preferred_element_type=jnp.float32) * 100.0
    softmax_columns = jnp.exp(cross - peak_all[None, :]) / total_all[None, :]
    scaled_rows = ((softmax_rows - target) * 100.0).astype(jnp.bfloat16)
    scaled_columns = ((softmax_columns - target) * 100.0).astype(jnp.bfloat16)
    grad_query = jnp.einsum("tp,pd->td", scaled_rows, passages, preferred_element_type=jnp.float32)
    grad_passage = jnp.einsum(
        "tq,qd->td", scaled_columns, queries, preferred_element_type=jnp.float32
    )
    grad_embed = jnp.where(query_flag[:, None], grad_query, grad_passage)
    (grad_output,) = embed_pullback(grad_embed.reshape(row_count, SEGS, feature_width))
    flat_tokens, query_states, key_states, value_states, joined, log_total = states[:6]
    resid_one, hidden, expanded, active, resid_two = states[6:11]
    w_query_full, w_key_full, w_value_full, w_out_full, w_up_full, w_down_full = params[:6]
    first_gain_f = params[11].astype(jnp.float32)
    first_shift_f = params[12].astype(jnp.float32)
    second_gain_f = params[13].astype(jnp.float32)
    second_shift_f = params[14].astype(jnp.float32)
    token_total = row_count * row_length
    norm_out, second_pullback = jax.vjp(norm_piece, resid_two, second_gain_f, second_shift_f)
    grad_resid_two, grad_second_gain, grad_second_shift = second_pullback(
        grad_output.reshape(token_total, feature_width)
    )
    grad_feed = grad_resid_two.astype(jnp.bfloat16)
    grad_down_weight = jnp.einsum(
        "nf,nd->fd", active, grad_feed, preferred_element_type=jnp.float32
    )
    grad_down_bias = jnp.sum(grad_feed.astype(jnp.float32), 0)
    grad_active = jnp.einsum(
        "nd,fd->nf", grad_feed, w_down_full, preferred_element_type=jnp.float32
    )
    gelu_out, gelu_pullback = jax.vjp(gelu_exact, expanded)
    grad_expanded = gelu_pullback(grad_active)[0].astype(jnp.bfloat16)
    grad_up_weight = jnp.einsum(
        "nd,nf->df", hidden.astype(jnp.bfloat16), grad_expanded, preferred_element_type=jnp.float32
    )
    grad_up_bias = jnp.sum(grad_expanded.astype(jnp.float32), 0)
    grad_hidden = grad_resid_two + jnp.einsum(
        "nf,df->nd", grad_expanded, w_up_full, preferred_element_type=jnp.float32
    )
    hidden_out, first_pullback = jax.vjp(norm_piece, resid_one, first_gain_f, first_shift_f)
    grad_resid_one, grad_first_gain, grad_first_shift = first_pullback(grad_hidden)
    grad_branch = grad_resid_one.astype(jnp.bfloat16)
    grad_out_weight = jnp.einsum(
        "nd,ne->de", joined, grad_branch, preferred_element_type=jnp.float32
    )
    grad_out_bias = jnp.sum(grad_branch.astype(jnp.float32), 0)
    grad_joined = jnp.einsum(
        "ne,de->nd", grad_branch, w_out_full, preferred_element_type=jnp.float32
    ).astype(jnp.bfloat16)
    row_shape = (row_count, row_length, feature_width)
    grad_queries, grad_keys, grad_values = lax.map(
        attend_backward,
        (
            query_states.reshape(row_shape),
            key_states.reshape(row_shape),
            value_states.reshape(row_shape),
            segment_ids,
            grad_joined.reshape(row_shape),
            log_total,
        ),
    )
    grad_queries = grad_queries.reshape(token_total, feature_width)
    grad_keys = grad_keys.reshape(token_total, feature_width)
    grad_values = grad_values.reshape(token_total, feature_width)
    grad_query_weight = jnp.einsum(
        "nd,ne->de", flat_tokens, grad_queries, preferred_element_type=jnp.float32
    )
    grad_key_weight = jnp.einsum(
        "nd,ne->de", flat_tokens, grad_keys, preferred_element_type=jnp.float32
    )
    grad_value_weight = jnp.einsum(
        "nd,ne->de", flat_tokens, grad_values, preferred_element_type=jnp.float32
    )
    grad_query_bias = jnp.sum(grad_queries.astype(jnp.float32), 0)
    grad_value_bias = jnp.sum(grad_values.astype(jnp.float32), 0)
    grad_inputs = grad_resid_one
    grad_inputs = grad_inputs + jnp.einsum(
        "ne,de->nd", grad_queries, w_query_full, preferred_element_type=jnp.float32
    )
    grad_inputs = grad_inputs + jnp.einsum(
        "ne,de->nd", grad_keys, w_key_full, preferred_element_type=jnp.float32
    )
    grad_inputs = grad_inputs + jnp.einsum(
        "ne,de->nd", grad_values, w_value_full, preferred_element_type=jnp.float32
    )
    grad_params = (
        grad_query_weight,
        grad_key_weight,
        grad_value_weight,
        grad_out_weight,
        grad_up_weight,
        grad_down_weight,
        grad_query_bias,
        grad_value_bias,
        grad_out_bias,
        grad_up_bias,
        grad_down_bias,
        grad_first_gain,
        grad_first_shift,
        grad_second_gain,
        grad_second_shift,
    )
    totals = reduce_all(grad_params)
    return (
        output.astype(jnp.bfloat16),
        grad_inputs.reshape(row_shape).astype(jnp.bfloat16),
    ) + tuple(totals)


def solution(mesh):
    in_specs = (
        P(("rep", "fsdp"), None, None),
        P(("rep", "fsdp"), None),
        P(),
        P("fsdp", None),
        P("fsdp", None),
        P("fsdp", None),
        P("fsdp", None),
        P("fsdp", None),
        P("fsdp", None),
        P("fsdp"),
        P("fsdp"),
        P("fsdp"),
        P("fsdp"),
        P("fsdp"),
        P("fsdp"),
        P("fsdp"),
        P("fsdp"),
        P("fsdp"),
    )
    out_specs = (
        P(("rep", "fsdp"), None, None),
        P(("rep", "fsdp"), None, None),
        P("fsdp", None),
        P("fsdp", None),
        P("fsdp", None),
        P("fsdp", None),
        P("fsdp", None),
        P("fsdp", None),
        P("fsdp"),
        P("fsdp"),
        P("fsdp"),
        P("fsdp"),
        P("fsdp"),
        P("fsdp"),
        P("fsdp"),
        P("fsdp"),
        P("fsdp"),
    )

    def whole(*arrays):
        fits = (
            mesh.shape["fsdp"] == 8
            and mesh.shape["rep"] == 4
            and arrays[0].shape == (64, 512, 768)
            and arrays[7].shape == (768, 3072)
        )
        return jax.shard_map(
            local_fused if fits else local,
            mesh=mesh,
            in_specs=in_specs,
            out_specs=out_specs,
            check_vma=False,
        )(*arrays)

    return whole
```

```python
import functools

import jax
import jax.numpy as jnp
from jax import lax
from jax.experimental import pallas as pl
from jax.experimental.pallas import tpu as pltpu
from jax.sharding import PartitionSpec as P

H = 12
HD = 64
SEGS = 8
MESH = pl.DeviceIdType.MESH
BF = jnp.bfloat16
F32 = jnp.float32


T = 1024
D = 768
FF = 3072
ROW = 512
NEG = -1e30
QA, QB, QC, WO, UA, UB, DA, DB = range(8)
GROUPS = 8
UNITS = (96, 96, 96, 96, 96, 96, 384, 384)
(XW, YW, S0, ZX, D2, SX, ZY, D1, SY, ZD, SD, SZX, SZY, SZD) = range(14)
ACCS = 4
OWN, XIN, YIN, DIN, ZXIN, ZYIN, ZDIN, READY = range(8)
START, MASKS, VECTORS, PROJECT, ATTEND, MERGE, EXPAND, REDUCE = range(8)
PLAN = {
    (START, 0): ((OWN, QA), (OWN, QB)),
    (MASKS, 0): (
        (XIN, QA), (YIN, QA), (OWN, QC),
    ),
    (VECTORS, 0): (
        (XIN, QB), (YIN, QB), (DIN, QA), (ZXIN, QA), (ZYIN, QA),
        (OWN, WO), (ZXIN, QB), (XIN, QC), (YIN, QC), (DIN, QB),
        (ZYIN, QB), (ZDIN, QA), (OWN, UA), (ZXIN, QC), (XIN, WO),
        (YIN, WO), (READY, QA),
    ),
    (PROJECT, 0): ((DIN, QC), (ZYIN, QC)),
    (PROJECT, 1): ((ZDIN, QB),),
    (ATTEND, 0): ((ZXIN, WO), (ZYIN, WO), (OWN, UB)),
    (ATTEND, 1): ((ZDIN, QC), (DIN, WO), (XIN, UA), (YIN, UA), (READY, QB)),
    (ATTEND, 2): ((ZDIN, WO), (XIN, UB), (YIN, UB)),
    (ATTEND, 3): ((DIN, UA), (ZXIN, UA), (OWN, DA), (READY, QC)),
    (PROJECT, 4): ((ZYIN, UA),),
    (PROJECT, 5): ((DIN, UB),),
    (ATTEND, 4): ((ZXIN, UB), (OWN, DB)),
    (ATTEND, 5): ((ZYIN, UB), (READY, WO)),
    (MERGE, 0): ((ZDIN, UA), (XIN, DA), (YIN, DA)),
    (MERGE, 2): ((ZDIN, UB),),
    (MERGE, 3): ((READY, UA),),
    (EXPAND, 0): ((XIN, DB), (ZXIN, DA), (YIN, DB)),
    (EXPAND, 2): ((DIN, DA), (ZYIN, DA)),
    (EXPAND, 5): ((DIN, DB), (ZXIN, DB), (READY, UB)),
    (EXPAND, 7): ((ZYIN, DB),),
    (EXPAND, 9): ((ZDIN, DA),),
    (EXPAND, 11): ((READY, DA),),
    (REDUCE, 0): ((ZDIN, DB),),
    (REDUCE, 1): ((READY, DB),),
}


DOWN, SLOPE, UP, FIRST, OUT, MIX, HEADS, GROUP, TOKEN, SUMS, SHARE = range(11)
SEND, X1, X2, Z1, Z2, Z3, END = range(11, 18)
BACK = (
    (DOWN, 1), (SEND, 0), (DOWN, 0), (X1, 0), (SEND, 1), (SLOPE, 0), (DOWN, 2), (X1, 1),
    (SEND, 2), (SLOPE, 1), (UP, 1), (X2, 0), (X1, 2), (SEND, 3), (SLOPE, 2), (SLOPE, 3),
    (X2, 1), (X1, 3), (FIRST, 0), (Z1, 0), (FIRST, 1), (FIRST, 2), (X2, 2), (FIRST, 3), (Z1, 1),
    (UP, 0), (SEND, 4), (Z2, 0), (UP, 2), (X2, 3), (X1, 4), (SEND, 5), (OUT, 0), (Z1, 2),
    (X1, 5), (SEND, 6), (Z2, 1), (MIX, 0), (Z3, 0), (Z1, 3), (HEADS, 0), (X2, 4), (X1, 6),
    (Z2, 2), (UP, 3), (SEND, 7), (Z3, 1), (X2, 5), (HEADS, 1), (END, 0), (Z2, 3), (Z1, 4),
    (X1, 7), (GROUP, 0), (SEND, 8), (Z3, 2), (X2, 6), (HEADS, 2), (END, 1), (Z3, 3), (Z2, 4),
    (Z1, 5), (X1, 8), (X2, 7), (HEADS, 3), (END, 2), (Z1, 6), (GROUP, 1), (SEND, 9), (Z3, 4),
    (Z2, 5), (X2, 8), (HEADS, 4), (END, 3), (Z1, 7), (Z2, 6), (X1, 9), (HEADS, 5), (END, 4),
    (Z3, 5), (Z1, 8), (GROUP, 2), (SEND, 10), (TOKEN, 0), (Z3, 6), (Z2, 7), (X2, 9), (X1, 10),
    (GROUP, 3), (SEND, 11), (TOKEN, 1), (END, 5), (Z2, 8), (X1, 11), (SUMS, 0), (Z1, 9),
    (TOKEN, 2), (Z3, 7), (X2, 10), (SHARE, 0), (END, 6), (TOKEN, 3), (X2, 11), (Z1, 10),
    (Z3, 8), (Z2, 9), (SHARE, 1), (END, 7), (Z1, 11), (Z2, 10), (SHARE, 2), (END, 8), (Z3, 9),
    (Z2, 11), (SHARE, 3), (Z3, 10), (Z3, 11), (SHARE, 4), (END, 9), (END, 10), (END, 11),
)
CHUNK_NAMES = tuple(step for step in BACK if step[0] in (DOWN, UP, OUT, GROUP))
NCHUNK = len(CHUNK_NAMES)


def chunk_shape(i):
    kind, number = CHUNK_NAMES[i]
    return (128 if kind == DOWN else 96), (D // 2 if kind == GROUP and number > 1 else D)


def dg(left, right, left_axis, right_axis):
    return lax.dot_general(
        left, right, (((left_axis,), (right_axis,)), ((), ())), preferred_element_type=F32
    )


def split_two(value):
    high = value.astype(BF)
    return high, (value - high.astype(F32)).astype(BF)


def aligned(start, size, step):
    return pl.ds(pl.multiple_of(start, step), size)


def gelu(z):
    return z * (0.5 + 0.5 * lax.erf(z * 0.7071067811865476))


def gelu_slope(z):
    below = 0.5 + 0.5 * lax.erf(z * 0.7071067811865476)
    return below + z * (0.3989422804014327 * jnp.exp(-0.5 * (z * z)))


def normalize(residual):
    centre = jnp.mean(residual, -1, keepdims=True)
    offset = residual - centre
    spread = jnp.mean(offset * offset, -1, keepdims=True)
    scale = lax.rsqrt(spread + 1e-12)
    return offset * scale, scale


def fused_kernel(
    tokens,
    seg,
    pairing,
    bq_in,
    bv_in,
    bo_in,
    bdn_in,
    g1_in,
    s1_in,
    g2_in,
    s2_in,
    bup_in,
    wq_in,
    wk_in,
    wv_in,
    wo_in,
    wup_in,
    wdn_in,
    out_y,
    out_dx,
    out_grads,
    out_vec,
    x_s,
    wqkv,
    wo,
    wup,
    wdn,
    sb,
    vecs,
    upb,
    qkv,
    seg_q,
    seg_k,
    lse,
    lse_t,
    dot_t,
    ao,
    n1,
    scales,
    h1b,
    g_s,
    gp,
    n2,
    df,
    npool,
    meta,
    c_s,
    rsib,
    acc,
    rx,
    ry,
    rx2,
    ry2,
    zs,
    rz1,
    rz2,
    fin,
    vg,
    vr,
    gsend,
    grecv,
    lsem,
    bsend,
    brecv,
    esend,
    erecv,
    xsend,
    xrecv,
    fsend,
    frecv,
    vsend,
    vrecv,
    osem,
):
    rep = lax.axis_index("rep")
    f = lax.axis_index("fsdp")
    core = f & 1
    chip = f >> 1
    pz = rep & 1
    dev_s, dev_x, dev_y, dev_d = (rep, f ^ 1), (rep, f ^ 2), (rep, f ^ 4), (rep, f ^ 6)
    dev_z1, dev_z2, dev_z3 = (rep ^ 1, f), (rep ^ 2, f), (rep ^ 3, f)
    weights = (
        (wqkv, 0, D),
        (wqkv, D, D),
        (wqkv, 2 * D, D),
        (wo, 0, D),
        (wup, 0, FF // 2),
        (wup, FF // 2, FF // 2),
        (wdn, 0, D // 2),
        (wdn, D // 2, D // 2),
    )

    def remote(src, dst, ssem, rsem, dev):
        return pltpu.make_async_remote_copy(
            src_ref=src, dst_ref=dst, send_sem=ssem, recv_sem=rsem, device_id=dev, device_id_type=MESH
        )

    def local_pairs():
        own = aligned(f * 96, 96, 16)
        pairs = []
        for group in range(3):
            for n, ref in enumerate((wq_in, wk_in, wv_in)):
                cols = pl.ds(D * group + 256 * n, 256)
                pairs.append((ref.at[:, pl.ds(256 * group, 256)], wqkv.at[own, cols]))
        pairs.append((wo_in, wo.at[own, :]))
        pairs.append((wup_in, wup.at[own, :]))
        pairs.append((wdn_in, wdn.at[aligned(f * 384, 384, 16), :]))
        pairs.append((tokens, x_s))
        return pairs

    locals_ = [
        pltpu.make_async_copy(src, dst, lsem.at[i]) for i, (src, dst) in enumerate(local_pairs())
    ]
    for copy in locals_:
        copy.start()
    for k, ref in enumerate((bq_in, bv_in, bo_in, bdn_in, g1_in, s1_in, g2_in, s2_in)):
        sb[pl.ds(f, 1), k : k + 1, 0:96] = ref[...].astype(F32).reshape(1, 1, 96)
        sb[pl.ds(f, 1), k : k + 1, 96:128] = jnp.zeros((1, 1, 32), F32)
    for k in range(3):
        sb[pl.ds(f, 1), 8 + k : 9 + k, :] = bup_in[k : k + 1, :].astype(F32).reshape(1, 1, 128)
    sb[pl.ds(f, 1), 11:16, :] = jnp.zeros((1, 5, 128), F32)

    barrier = pltpu.get_barrier_semaphore()
    peers = [(rep, f ^ k) for k in range(1, 8)] + [dev_z1, dev_z2, dev_z3]
    for peer in peers:
        pl.semaphore_signal(barrier, inc=1, device_id=peer, device_id_type=MESH)
    pl.semaphore_wait(barrier, len(peers))

    def full(g, who):
        return who * UNITS[g], UNITS[g]

    def wide(g, who):
        return who * UNITS[g] + (UNITS[g] // 3) * pz, 2 * (UNITS[g] // 3)

    def part_m(g, who):
        return who * UNITS[g] + 2 * (UNITS[g] // 3) * pz, UNITS[g] // 3

    def part_a(g, who):
        return who * UNITS[g] + UNITS[g] // 3, UNITS[g] // 3

    def part_o(g, who):
        return who * UNITS[g] + 2 * (UNITS[g] // 3) * (1 - pz), UNITS[g] // 3

    fx, fy, fd, fs = f ^ 2, f ^ 4, f ^ 6, f ^ 1
    fsx, fsy, fsd = fs ^ 2, fs ^ 4, fs ^ 6
    sent_rows = {
        XW: (wide, f, dev_x),
        YW: (wide, f, dev_y),
        S0: (full, f, dev_s),
        ZX: (part_m, fx, dev_z1),
        D2: (part_m, fx, dev_y),
        SX: (wide, fx, dev_s),
        ZY: (part_m, fy, dev_z1),
        D1: (part_a, fy, dev_x),
        SY: (wide, fy, dev_s),
        ZD: (part_m, fd, dev_z1),
        SD: (wide, fd, dev_s),
        SZX: (part_o, fx, dev_s),
        SZY: (part_o, fy, dev_s),
        SZD: (part_o, fd, dev_s),
    }
    got_rows = {
        XW: (wide, fx),
        YW: (wide, fy),
        S0: (full, fs),
        ZX: (part_o, fx),
        D2: (part_m, fd),
        SX: (wide, fsx),
        ZY: (part_o, fy),
        D1: (part_a, fd),
        SY: (wide, fsy),
        ZD: (part_o, fd),
        SD: (wide, fsd),
        SZX: (part_o, fsx),
        SZY: (part_o, fsy),
        SZD: (part_o, fsd),
    }

    def weight_rows(g, start, size):
        ref, first, width = weights[g]
        return ref.at[aligned(start, size, 16), pl.ds(first, width)]

    def gather_copy(g, piece):
        rows, who, dev = sent_rows[piece]
        start, size = rows(g, who)
        view = weight_rows(g, start, size)
        return remote(view, view, gsend.at[g, piece], grecv.at[g, piece], dev)

    def g_send(g, *pieces):
        for piece in pieces:
            gather_copy(g, piece).start()

    def g_recv(g, *pieces):
        for piece in pieces:
            rows, who = got_rows[piece]
            start, size = rows(g, who)
            view = weight_rows(g, start, size)
            remote(
                view, view, gsend.at[g, piece], grecv.at[g, piece], sent_rows[piece][2]
            ).wait_recv()

    def g_done(g):
        for piece in range(14):
            gather_copy(g, piece).wait_send()

    def step_own(g):
        for i in ((0, 1, 2), (3, 4, 5), (6, 7, 8), (9,), (10,), (), (11,), ())[g]:
            locals_[i].wait()
        g_send(g, XW, YW, S0)

    def step_ready(g):
        g_recv(g, S0, SX, SY, SD, SZX, SZY, SZD)

    def relay(waits, sends):
        def step(g):
            g_recv(g, *waits)
            g_send(g, *sends)

        return step

    gather_steps = {
        OWN: step_own,
        XIN: relay((XW,), (ZX, D2, SX)),
        YIN: relay((YW,), (D1, ZY, SY)),
        DIN: relay((D1, D2), (ZD, SD)),
        ZXIN: relay((ZX,), (SZX,)),
        ZYIN: relay((ZY,), (SZY,)),
        ZDIN: relay((ZD,), (SZD,)),
        READY: step_ready,
    }

    def after(kind, n):
        for step, g in PLAN.get((kind, n), ()):
            gather_steps[step](g)

    def stepped(count, body, kind, first=0):
        def one(i, carry):
            body(i)
            for k in range(count - 1):
                if (kind, first + k) in PLAN:
                    pl.when(i == k)(lambda n=first + k: after(kind, n))
            return carry

        lax.fori_loop(0, count, one, 0)
        after(kind, first + count - 1)

    def small_copy(k):
        view = sb.at[pl.ds(f, 1)]
        return remote(view, view, bsend.at[k - 1], brecv.at[k - 1], (rep, f ^ k))

    step_own(QA)
    for k in range(1, 8):
        small_copy(k).start()
    for step, g in PLAN[START, 0][1:]:
        gather_steps[step](g)

    segf = seg[...].astype(F32)

    def segment_columns():
        for r in range(2):
            lse[pl.ds(r * ROW, ROW), :] = jnp.broadcast_to(segf[r : r + 1, :], (128, ROW)).T

    segment_columns()
    seg_lane = lax.broadcasted_iota(jnp.int32, (T, 128), 1).astype(F32)
    same = jnp.where(lse[...] == seg_lane, 1.0, 0.0)
    seg_q[...] = same.astype(BF)
    seg_k[...] = jnp.where(seg_lane < SEGS, NEG * (1.0 - same), 0.0).astype(BF)

    after(MASKS, 0)

    places = jnp.broadcast_to(pairing[...].astype(F32), (128, 512)).T[:, 0:1]
    texts = lax.broadcasted_iota(jnp.int32, (512, 512), 1).astype(F32)
    order_no = lax.broadcasted_iota(jnp.int32, (512, 512), 0).astype(F32)
    found = jnp.sum(jnp.where(places == texts, order_no, 0.0), 0, keepdims=True)
    meta[...] = jnp.broadcast_to(found, (8, 512))

    for k in range(1, 8):
        view = sb.at[pl.ds(f ^ k, 1)]
        remote(view, view, bsend.at[k - 1], brecv.at[k - 1], (rep, f ^ k)).wait_recv()
    lane = lax.broadcasted_iota(jnp.int32, (128, D), 0)
    column = lax.broadcasted_iota(jnp.int32, (128, D), 1)
    total = jnp.zeros((8, D), F32)
    for k in range(8):
        for j in range(3):
            upb[0:1, k * 384 + 128 * j : k * 384 + 128 * j + 128] = sb[k, 8 + j : 9 + j, :]
        place = jnp.where((column == lane + 96 * k) & (lane < 96), 1.0, 0.0).astype(BF)
        total = total + dg(sb[k, 0:8, :].astype(BF), place, 1, 0)
    vecs[...] = total
    bq, bv, bo, bdn = (vecs[i : i + 1, :] for i in range(4))
    g1, s1, g2, s2 = (vecs[i : i + 1, :] for i in range(4, 8))
    locals_[12].wait()

    after(VECTORS, 0)

    lane_row = lax.broadcasted_iota(jnp.int32, (1, 128), 1)
    even = (lane_row < HD).astype(F32).astype(BF)
    odd = (lane_row >= HD).astype(F32).astype(BF)
    tile_lane = lax.broadcasted_iota(jnp.int32, (256, 128), 1)
    scaling = jnp.where(lax.broadcasted_iota(jnp.int32, (1, D), 1) < 256, 0.125, 1.0).astype(BF)

    def both(value):
        return jnp.concatenate([value * even, value * odd], axis=0)

    def project(group):
        cols = pl.ds(D * group, D)
        part = pl.ds(256 * group, 256)
        bias = jnp.concatenate([vecs[0:1, part], jnp.zeros((1, 256), F32), vecs[1:2, part]], 1)

        def qkv_step(i):
            rows = aligned(i * 512, 512, 512)
            qkv[rows, cols] = (dg(x_s[rows, :], wqkv[:, cols], 1, 0) + bias).astype(BF) * scaling

        stepped(2, qkv_step, PROJECT, 2 * group)

    def attend(r, pair, b):
        kq = aligned(r * ROW + 128 * b, 384, 128)
        qq = aligned(r * ROW + 256 * b, 256, 256)
        at = D * (pair // 2) + 128 * (pair % 2)
        q = qkv[qq, pl.ds(at, 128)]
        v = qkv[kq, pl.ds(at + 512, 128)]
        keys = jnp.concatenate([qkv[kq, pl.ds(at + 256, 128)], seg_k[kq, :]], 1)
        ids = seg_q[qq, :]
        queries = jnp.concatenate(
            [jnp.concatenate([q * even, ids], 1), jnp.concatenate([q * odd, ids], 1)], 0
        )
        scores = dg(queries, keys, 1, 1)
        mixed, peaks, totals = [], [], []
        for h in range(2):
            part = scores[256 * h : 256 * h + 256]
            peak = jnp.max(part, 1, keepdims=True)
            e = jnp.exp(part - peak)
            totals.append(jnp.sum(e, 1, keepdims=True))
            peaks.append(peak)
            mixed.append(dg(e.astype(BF), v, 1, 0))
        first = tile_lane < HD
        total = jnp.where(first, totals[0], totals[1])
        ao[qq, pl.ds(128 * pair, 128)] = (jnp.where(first, mixed[0], mixed[1]) * (1.0 / total)).astype(BF)
        logs = jnp.where(first, peaks[0], peaks[1]) + jnp.log(total)
        lse[qq, :] = jnp.where((tile_lane & 63) == pair, logs, lse[qq, :])

    def attend_group(group):
        def attend_step(r):
            for pair in (2 * group, 2 * group + 1):
                for b in range(2):
                    attend(r, pair, b)

        stepped(2, attend_step, ATTEND, 2 * group)

    lse[...] = jnp.zeros((T, 128), F32)
    for group in range(3):
        project(group)
        attend_group(group)
    for k in range(8):
        turned = lse[128 * k : 128 * k + 128, :].T
        lse_t[0:8, 128 * k : 128 * k + 128] = turned[0:8]
        lse_t[8:16, 128 * k : 128 * k + 128] = turned[64:72]

    def out_step(i):
        rows = aligned(i * 256, 256, 256)
        r1 = x_s[rows, :].astype(F32) + (dg(ao[rows, :], wo[...], 1, 0) + bo)
        n, scale = normalize(r1)
        n1[rows, :] = n
        scales[rows, 0:64] = jnp.broadcast_to(scale, (256, 64))
        h1b[rows, :] = (n * g1 + s1).astype(BF)

    stepped(4, out_step, MERGE)

    def up_step(i):
        cols = aligned(i * 256, 256, 256)
        z = dg(h1b[...], wup[:, cols], 1, 0) + upb[0:1, cols]
        g_s[:, cols] = gelu(z).astype(BF)
        gp[:, cols] = z.astype(BF)

    stepped(12, up_step, EXPAND)

    def slope_part(first, last):
        def part(i, carry):
            rows = aligned(i * 64, 64, 64)
            gp[rows, :] = gelu_slope(gp[rows, :].astype(F32)).astype(BF)
            return carry

        lax.fori_loop(first, last, part, 0)

    npool[...] = jnp.zeros((16, D), F32)
    text_row = lax.broadcasted_iota(jnp.int32, (16, ROW), 0)

    def member_of(r):
        ids = seg[pl.ds(r, 1), :] + 8 * r
        return (text_row == ids).astype(F32)

    left, right = pl.ds(0, D // 2), pl.ds(D // 2, D // 2)

    def down_left(i):
        rows = aligned(i * 512, 512, 512)
        n2[rows, left] = dg(g_s[rows, :], wdn[:, left], 1, 0)

    stepped(2, down_left, REDUCE)
    for r in range(2):
        rows = pl.ds(r * ROW, ROW)
        h1 = n1[rows, :] * g1 + s1
        fed = jnp.concatenate([n2[rows, left], dg(g_s[rows, :], wdn[:, right], 1, 0)], 1)
        n, scale = normalize(h1 + (fed + bdn))
        n2[rows, :] = n
        scales[rows, 64:128] = jnp.broadcast_to(scale, (ROW, 64))
        member = member_of(r).astype(BF)
        high, low = split_two(n)
        npool[...] += dg(member, high, 1, 0) + dg(member, low, 1, 0)

    lse[0:512, :] = jnp.broadcast_to(meta[0:1, :], (128, 512)).T

    members = jnp.concatenate([member_of(0), member_of(1)], axis=1)
    counts = jnp.sum(members, 1, keepdims=True)
    members = members.astype(BF)
    pooled = npool[...] / counts * g2 + s2
    inverse = lax.rsqrt(jnp.sum(pooled * pooled, 1, keepdims=True) + 1e-06)
    embed = pooled * inverse
    acc[pl.ds(rep, 1), 0, aligned(16 * f, 16, 16), :] = embed.astype(BF).reshape(1, 16, D)

    def e_copy(plane, who, dev, number):
        view = acc.at[pl.ds(plane, 1), 0, aligned(16 * who, 16, 16), :]
        return remote(view, view, esend.at[number], erecv.at[number], dev)

    def e_column(who, number):
        view = acc.at[:, 0, aligned(16 * who, 16, 16), :]
        return remote(view, view, esend.at[number], erecv.at[number], dev_s)

    plane_devs = (dev_x, dev_y, dev_d, dev_s)
    e_sends = [e_copy(rep, f, (rep ^ k, f), k - 1) for k in (1, 2, 3)]
    e_sends += [e_copy(rep, f, dev, 3 + 4 * n) for n, dev in enumerate(plane_devs)]
    for copy in e_sends:
        copy.start()
    slope_part(0, 4)
    for g in range(GROUPS):
        g_done(g)
    for k in range(1, 8):
        small_copy(k).wait_send()
    for k in (1, 2, 3):
        e_copy(rep ^ k, f, (rep ^ k, f), k - 1).wait_recv()
        for n, dev in enumerate(plane_devs):
            e_sends.append(e_copy(rep ^ k, f, dev, 3 + 4 * n + k))
            e_sends[-1].start()
    slope_part(4, 13)
    for r in range(2):
        rows = pl.ds(r * ROW, ROW)
        df[rows, :] = (n2[rows, :] * g2 + s2).astype(BF)
    y_copy = pltpu.make_async_copy(df, out_y, osem.at[0])
    y_copy.start()
    for n, who in enumerate((fx, fy, fd)):
        for k in range(4):
            e_copy(rep ^ k, who, plane_devs[n], 3 + 4 * n + k).wait_recv()
        e_sends.append(e_column(who, 19 + n))
        e_sends[-1].start()
    slope_part(13, 16)
    for k in range(4):
        e_copy(rep ^ k, fs, dev_s, 15 + k).wait_recv()
    for n, who in enumerate((fsx, fsy, fsd)):
        e_column(who, 19 + n).wait_recv()
    for copy in e_sends:
        copy.wait_send()

    every = jnp.concatenate([acc[k, 0] for k in range(4)], 0)
    pos_all = meta[0:1, :]
    pair_all = jnp.floor(pos_all * 0.5)
    second_all = pos_all - 2.0 * pair_all
    pos_col = lse[0:512, 0:1]
    second_col = pos_col - 2.0 * jnp.floor(pos_col * 0.5)
    whole = dg(every, every, 1, 1) * 100.0
    whole = jnp.where(second_col > 0.5, whole, NEG)
    peak_all = jnp.max(whole, 0, keepdims=True)
    total_all = jnp.sum(jnp.exp(whole - peak_all), 0, keepdims=True)
    own = embed.astype(BF)
    mine = dg(own, every, 1, 1) * 100.0
    pos_own = lse[aligned((rep * 8 + f) * 16, 16, 16), 0:1]
    pair_own = jnp.floor(pos_own * 0.5)
    second_own = pos_own - 2.0 * pair_own
    same_pair = jnp.where(pair_own == pair_all, 1.0, 0.0)
    rows_masked = jnp.where(second_all > 0.5, mine, NEG)
    row_peak = jnp.max(rows_masked, 1, keepdims=True)
    row_e = jnp.exp(rows_masked - row_peak)
    soft_rows = row_e / jnp.sum(row_e, 1, keepdims=True)
    soft_cols = jnp.exp(jnp.where(second_all > 0.5, NEG, mine - peak_all)) / total_all
    d_rows = (soft_rows - same_pair) * second_all
    d_cols = (soft_cols - same_pair) * (1.0 - second_all)
    d_logits = (jnp.where(second_own > 0.5, d_cols, d_rows) * 100.0).astype(BF)
    d_embed = dg(d_logits, every, 1, 0)
    d_pooled = (d_embed - embed * jnp.sum(embed * d_embed, 1, keepdims=True)) * inverse
    d_each = d_pooled / counts
    vg[...] = jnp.zeros((16, D), F32)
    vg[6:7, :] = jnp.sum(d_each * npool[...], 0, keepdims=True)
    vg[7:8, :] = jnp.sum(d_pooled, 0, keepdims=True)
    u_text = d_each * g2
    u_text = u_text - jnp.mean(u_text, 1, keepdims=True)
    u_high, u_low = split_two(u_text)
    u_both = jnp.concatenate([u_high, u_low], 0)
    y_copy.wait()

    for i in range(4):
        rows = pl.ds(i * 256, 256)
        part = members[:, 256 * i : 256 * i + 256]
        u = dg(jnp.concatenate([part, part], 0), u_both, 0, 0)
        n = n2[rows, :]
        d = (u - n * jnp.mean(u * n, 1, keepdims=True)) * scales[rows, 64:65]
        n2[rows, :] = d
        db = d.astype(BF)
        df[rows, :] = db
        vg[3:4, :] += jnp.sum(db.astype(F32), 0, keepdims=True)

    def small_ring(i):
        return i % 2

    def long_ring(i):
        return i % 4

    ch_x, ch_y, ch_d = chip ^ 1, chip ^ 2, chip ^ 3
    inner = (((rep + 1) >> 1) & 1) == 1
    outer = jnp.logical_not(inner)

    def view_s(i):
        (u, w), s = chunk_shape(i), small_ring(i)
        src = c_s.at[s, :, pl.ds(1 - core, 1), pl.ds(0, u), pl.ds(0, w)]
        dst = rsib.at[s, :, :, pl.ds(0, u), pl.ds(0, w)]
        return remote(src, dst, xsend.at[s, 0], xrecv.at[s, 0], dev_s)

    def views_x1(i):
        (u, w), s, a = chunk_shape(i), long_ring(i), i % ACCS
        half = u // 2
        low, high, cols = pl.ds(0, half), pl.ds(half, half), pl.ds(0, w)
        pieces = (
            (ch_x, low, rx.at[s, 0, low, cols], dev_x),
            (ch_d, low, rx.at[s, 1, low, cols], dev_x),
            (ch_y, high, ry.at[s, 0, low, cols], dev_y),
            (ch_d, high, ry.at[s, 1, low, cols], dev_y),
        )
        return [
            remote(acc.at[a, who, rows, cols], dst, xsend.at[s, 1 + n], xrecv.at[s, 1 + n], dev)
            for n, (who, rows, dst, dev) in enumerate(pieces)
        ]

    def views_x2(i):
        (u, w), s, a = chunk_shape(i), long_ring(i), i % ACCS
        half = u // 2
        low, high, cols = pl.ds(0, half), pl.ds(half, half), pl.ds(0, w)
        return [
            remote(acc.at[a, ch_y, low, cols], ry2.at[s, low, cols], xsend.at[s, 5], xrecv.at[s, 5], dev_y),
            remote(acc.at[a, ch_x, high, cols], rx2.at[s, low, cols], xsend.at[s, 6], xrecv.at[s, 6], dev_x),
        ]

    def view_z1(i):
        (u, w), s = chunk_shape(i), long_ring(i)
        rows, cols = pl.ds(0, u), pl.ds(0, w)
        return remote(
            zs.at[s, rows, cols], rz1.at[s, rows, cols], xsend.at[s, 7], xrecv.at[s, 7], dev_z1
        )

    def view_z2(i):
        (u, w), s = chunk_shape(i), long_ring(i)
        rows, cols = pl.ds(0, u), pl.ds(0, w)
        return remote(
            zs.at[s, rows, cols], rz2.at[s, rows, cols], xsend.at[s, 8], xrecv.at[s, 8], dev_z3
        )

    def view_z3(i):
        u, w = chunk_shape(i)
        place = fin.at[i, pl.ds(0, u), pl.ds(0, w)]
        return remote(place, place, fsend.at[i], frecv.at[i], dev_z1)

    def stage_x1(i):
        (u, w), s, a = chunk_shape(i), small_ring(i), i % ACCS
        view_s(i).wait()
        for ch in range(4):
            acc[a, ch, 0:u, 0:w] = c_s[s, ch, pl.ds(core, 1), 0:u, 0:w][0] + rsib[s, ch, 0, 0:u, 0:w]
        for copy in views_x1(i):
            copy.start()

    def stage_x2(i):
        (u, w), s, a = chunk_shape(i), long_ring(i), i % ACCS
        half = u // 2
        for copy in views_x1(i):
            copy.wait()
        acc[a, pl.ds(ch_y, 1), 0:half, 0:w] += rx[s, 1:2, 0:half, 0:w]
        acc[a, pl.ds(ch_x, 1), half:u, 0:w] += ry[s, 1:2, 0:half, 0:w]
        for copy in views_x2(i):
            copy.start()
        acc[a, pl.ds(chip, 1), 0:half, 0:w] += rx[s, 0:1, 0:half, 0:w]
        acc[a, pl.ds(chip, 1), half:u, 0:w] += ry[s, 0:1, 0:half, 0:w]

    def stage_z1(i):
        (u, w), s, a = chunk_shape(i), long_ring(i), i % ACCS
        half = u // 2
        for copy in views_x2(i):
            copy.wait()
        zs[s, 0:half, 0:w] = acc[a, pl.ds(chip, 1), 0:half, 0:w][0] + ry2[s, 0:half, 0:w]
        zs[s, half:u, 0:w] = acc[a, pl.ds(chip, 1), half:u, 0:w][0] + rx2[s, 0:half, 0:w]

        @pl.when(outer)
        def _():
            view_z1(i).start()

    def stage_z2(i):
        (u, w), s = chunk_shape(i), long_ring(i)

        @pl.when(outer)
        def _():
            view_z1(i).wait_send()

        @pl.when(inner)
        def _():
            view_z1(i).wait_recv()
            zs[s, 0:u, 0:w] += rz1[s, 0:u, 0:w]
            view_z2(i).start()

    def stage_z3(i):
        (u, w), s = chunk_shape(i), long_ring(i)

        @pl.when(inner)
        def _():
            view_z2(i).wait()
            fin[i, 0:u, 0:w] = zs[s, 0:u, 0:w] + rz2[s, 0:u, 0:w]
            view_z3(i).start()

    def out_copy(i):
        u, w = chunk_shape(i)
        rows, cols = pl.ds(0, u), pl.ds(0, w)
        return pltpu.make_async_copy(fin.at[i, rows, cols], out_grads.at[i, rows, cols], osem.at[2 + i])

    def stage_end(i):
        @pl.when(inner)
        def _():
            view_z3(i).wait_send()

        @pl.when(outer)
        def _():
            view_z3(i).wait_recv()

        out_copy(i).start()

    def store_slabs(i, hh, result):
        (u, w), s = chunk_shape(i), small_ring(i)
        for k in range(4):
            c_s[s, pl.ds(2 * hh + k // 2, 1), k % 2, 0:u, 0:w] = (
                result[u * k : u * k + u].astype(BF).reshape(1, u, w)
            )

    def chunk(i, left_of, right):
        def half(hh, carry):
            store_slabs(i, hh, dg(left_of(hh), right(), 0, 0))
            return carry

        lax.fori_loop(0, 2, half, 0)

    def down_chunk(i, j):
        def left_of(hh):
            return jnp.concatenate(
                [g_s[:, aligned((4 * hh + k) * 384 + j * 128, 128, 128)] for k in range(4)], 1
            )

        chunk(i, left_of, lambda: df[...])

    def slope(j):
        cols = pl.ds(D * j, D)

        def slope_step(m, carry):
            rows = aligned(m * 512, 512, 512)
            dz = (dg(df[rows, :], wdn[cols, :], 1, 1) * gp[rows, cols].astype(F32)).astype(BF)
            gp[rows, cols] = dz
            vg[8 + j : 9 + j, :] += jnp.sum(dz.astype(F32), 0, keepdims=True)
            return carry

        lax.fori_loop(0, 2, slope_step, 0)

    def up_chunk(i, j):
        chunk(i, lambda hh: h1b[:, aligned(384 * hh, 384, 128)], lambda: gp[:, pl.ds(D * j, D)])

    def first_step(i, carry):
        rows = aligned(i * 256, 256, 256)
        dh = n2[rows, :] + dg(gp[rows, :], wup[...], 1, 1)
        n = n1[rows, :]
        vg[4:5, :] += jnp.sum(dh * n, 0, keepdims=True)
        vg[5:6, :] += jnp.sum(dh, 0, keepdims=True)
        u = dh * g1
        d = (u - jnp.mean(u, 1, keepdims=True) - n * jnp.mean(u * n, 1, keepdims=True)) * scales[rows, 0:1]
        n2[rows, :] = d
        db = d.astype(BF)
        df[rows, :] = db
        vg[2:3, :] += jnp.sum(db.astype(F32), 0, keepdims=True)
        return carry

    def out_chunk(i):
        chunk(i, lambda hh: ao[:, aligned(384 * hh, 384, 128)], lambda: df[...])

    def mask_place(r, b):
        m = 2 * r + b
        return pl.ds(384 * (m // 3), 384), pl.ds(256 * (m % 3), 256)

    def place_masks():
        segment_columns()
        for r in range(2):
            for b in range(2):
                key_side = lse[pl.ds(r * ROW + 128 * b, 384), 0:1]
                query_side = segf[r : r + 1, 256 * b : 256 * b + 256]
                n1[mask_place(r, b)] = jnp.where(key_side == query_side, 0.0, NEG)

    head = lax.broadcasted_iota(jnp.int32, (D, 128), 0) // HD
    head_lane = lax.broadcasted_iota(jnp.int32, (D, 128), 1)
    one_hot = jnp.where(head_lane == head // 2 + 8 * (head % 2), 1.0, 0.0).astype(BF)

    def mix_step(m, carry):
        rows = aligned(m * 512, 512, 512)
        da = dg(df[rows, :], wo[...], 1, 1).astype(BF)
        high, low = split_two(da.astype(F32) * ao[rows, :].astype(F32))
        dots = dg(high, one_hot, 1, 0) + dg(low, one_hot, 1, 0)
        dot_t[:, rows] = dots.T[0:16]
        ao[rows, :] = da
        return carry

    def mix():
        place_masks()
        lax.fori_loop(0, 2, mix_step, 0)

    def attend_back(r, pair, at):
        grads_k, grads_v = [], []
        for b in range(2):
            kq = aligned(r * ROW + 128 * b, 384, 128)
            qq = aligned(r * ROW + 256 * b, 256, 256)
            k = qkv[kq, aligned(at + 256, 128, 128)]
            v = qkv[kq, aligned(at + 512, 128, 128)]
            q = qkv[qq, aligned(at, 128, 128)]
            da = ao[qq, aligned(pair * 128, 128, 128)]
            scores = dg(both(k), q, 1, 1)
            dp = dg(both(v), da, 1, 1)
            bias = n1[mask_place(r, b)]
            probs, dscores = [], []
            for h in range(2):
                rows = slice(384 * h, 384 * h + 384)
                prob = jnp.exp(scores[rows] + bias - lse_t[pair + 8 * h : pair + 8 * h + 1, qq])
                probs.append(prob.astype(BF))
                dscores.append((prob * (dp[rows] - dot_t[pair + 8 * h : pair + 8 * h + 1, qq])).astype(BF))
            grads_v.append(dg(jnp.concatenate(probs, 1), both(da), 1, 0))
            grads_k.append(dg(jnp.concatenate(dscores, 1), both(q), 1, 0))
            even_q, odd_q = dg(k, dscores[0], 0, 0), dg(k, dscores[1], 0, 0)
            dq = jnp.concatenate([even_q[0:HD], odd_q[HD : 2 * HD]], 0).T
            g_s[qq, aligned(at, 128, 128)] = (dq * 0.125).astype(BF)
        for off, (first, second) in ((256, grads_k), (512, grads_v)):
            cols = aligned(at + off, 128, 128)
            g_s[aligned(r * ROW, 128, 128), cols] = first[0:128].astype(BF)
            g_s[aligned(r * ROW + 128, 256, 128), cols] = (first[128:384] + second[0:256]).astype(BF)
            g_s[aligned(r * ROW + 384, 128, 128), cols] = second[256:384].astype(BF)

    def heads(pair):
        def back_step(r, carry):
            attend_back(r, pair, D * (pair // 2) + 128 * (pair % 2))
            return carry

        lax.fori_loop(0, 2, back_step, 0, unroll=True)

    def group_chunk(i, group):
        def right():
            if group < 2:
                return g_s[:, pl.ds(D * group, D)]
            first = 2 * D + 128 * (group - 2)
            return jnp.concatenate([g_s[:, pl.ds(first + 256 * n, 128)] for n in range(3)], 1)

        chunk(i, lambda hh: x_s[:, aligned(384 * hh, 384, 128)], right)

    def vector_sums():
        for row, off in ((0, 0), (1, 512)):
            for group in range(3):
                vg[row : row + 1, 256 * group : 256 * group + 256] = jnp.sum(
                    g_s[:, pl.ds(D * group + off, 256)].astype(F32), 0, keepdims=True
                )
        v_copy(0).start()

    order = (dev_s, dev_x, dev_y, dev_z1, dev_z2)

    def v_copy(n):
        return remote(vg, vr.at[n], vsend.at[n], vrecv.at[n], order[n])

    def v_step(n):
        v_copy(n).wait()
        vg[...] = vg[...] + vr[n]
        if n + 1 < len(order):
            v_copy(n + 1).start()

    def token_step(i, carry):
        rows = aligned(i * 256, 256, 256)
        h1b[rows, :] = (n2[rows, :] + dg(g_s[rows, pl.ds(0, 3 * D)], wqkv[...], 1, 1)).astype(BF)
        return carry

    dx_copy = pltpu.make_async_copy(h1b, out_dx, osem.at[1])

    numbers = {name: i for i, name in enumerate(CHUNK_NAMES)}
    stages = {
        X1: stage_x1,
        X2: stage_x2,
        Z1: stage_z1,
        Z2: stage_z2,
        Z3: stage_z3,
        END: stage_end,
        SHARE: v_step,
        SLOPE: slope,
        HEADS: heads,
    }
    for kind, n in BACK:
        if kind in stages:
            stages[kind](n)
        elif kind == SEND:
            view_s(n).start()
        elif kind == DOWN:
            down_chunk(numbers[kind, n], n)
        elif kind == UP:
            up_chunk(numbers[kind, n], n)
        elif kind == OUT:
            out_chunk(numbers[kind, n])
        elif kind == GROUP:
            group_chunk(numbers[kind, n], n)
        elif kind == FIRST:
            lax.fori_loop(n, n + 1, first_step, 0)
        elif kind == MIX:
            mix()
        elif kind == SUMS:
            vector_sums()
        elif kind == TOKEN:
            lax.fori_loop(n, n + 1, token_step, 0)
            if n == 3:
                dx_copy.start()

    out_vec[8:16, 0:128] = jnp.zeros((8, 128), F32)
    for k in range(8):

        @pl.when(f == k)
        def _():
            out_vec[0:8, 0:96] = vg[0:8, 96 * k : 96 * k + 96]
            line = jnp.concatenate([vg[8 + n : 9 + n, :] for n in range(4)], 1)
            out_vec[8:9, 0:384] = line[:, 384 * k : 384 * k + 384]

    dx_copy.wait()
    for i in range(NCHUNK):
        out_copy(i).wait()


def finish_kernel(
    raw_y,
    raw_dx,
    raw_grads,
    vec,
    out_y,
    out_dx,
    out_gq,
    out_gk,
    out_gv,
    out_go,
    out_gup,
    out_gdn,
    *rest,
):
    vectors = rest[:9]
    y, dx, grads, gq, gk, gv, go, gup, gdn, sems = rest[9:19]
    rows, small = rest[19:], []
    reads = [(raw_y, y), (raw_dx, dx), (raw_grads, grads)]
    reads = [pltpu.make_async_copy(src, dst, sems.at[i]) for i, (src, dst) in enumerate(reads)]
    writes = [(gq, out_gq), (gk, out_gk), (gv, out_gv), (go, out_go), (gup, out_gup), (gdn, out_gdn)]
    writes = [(y, out_y), (dx, out_dx)] + writes
    writes = [pltpu.make_async_copy(src, dst, sems.at[3 + i]) for i, (src, dst) in enumerate(writes)]
    for copy in reads:
        copy.start()
    for n, row in enumerate((0, 1, 2, 8, 3, 4, 5, 6, 7)):
        if row == 8:
            for k in range(3):
                rows[n][k : k + 1, :] = vec[8:9, 128 * k : 128 * k + 128]
        else:
            rows[n][...] = vec[row : row + 1, 0:96]
        small.append(pltpu.make_async_copy(rows[n], vectors[n], sems.at[11 + n]))
        small[-1].start()
    for n in range(2):
        reads[n].wait()
        writes[n].start()
    reads[2].wait()
    for i, (kind, j) in enumerate(CHUNK_NAMES):
        if kind == DOWN:
            gdn[128 * j : 128 * j + 128, :] = grads[i].astype(F32)
        elif kind == UP:
            gup[:, D * j : D * j + D] = grads[i, 0:96].astype(F32)
        elif kind == OUT:
            go[...] = grads[i, 0:96].astype(F32)
        else:
            first, width = (256 * j, 256) if j < 2 else (512 + 128 * (j - 2), 128)
            for n, ref in enumerate((gq, gk, gv)):
                ref[:, first : first + width] = grads[i, 0:96, width * n : width * n + width].astype(F32)
    for copy in writes[2:]:
        copy.start()
    for copy in writes + small:
        copy.wait()


def finish_call(raw_y, raw_dx, grads, vec):
    shape = jax.ShapeDtypeStruct
    any_ = pl.BlockSpec(memory_space=pl.ANY)
    vmem = pl.BlockSpec(memory_space=pltpu.VMEM)
    shapes = ((1, 96),) * 3 + ((3, 128),) + ((1, 96),) * 5
    weights = ((96, D), (96, D), (96, D), (96, D), (96, FF), (384, D))
    return pl.pallas_call(
        finish_kernel,
        name="write_results",
        out_shape=(shape((T, D), BF), shape((T, D), BF))
        + tuple(shape(dims, F32) for dims in weights)
        + tuple(shape(dims, F32) for dims in shapes),
        in_specs=[any_, any_, any_, vmem],
        out_specs=(any_,) * 17,
        scratch_shapes=[pltpu.VMEM((T, D), BF), pltpu.VMEM((T, D), BF), pltpu.VMEM((NCHUNK, 128, D), BF)]
        + [pltpu.VMEM(dims, F32) for dims in weights]
        + [pltpu.SemaphoreType.DMA((20,))]
        + [pltpu.VMEM(dims, F32) for dims in shapes],
        compiler_params=pltpu.CompilerParams(vmem_limit_bytes=60 * 2**20),
    )(raw_y, raw_dx, grads, vec)


def fused_call(tokens, seg, pairing, vectors, shards):
    vm = lambda shape, dtype: pltpu.VMEM(shape, dtype)
    sem = pltpu.SemaphoreType.DMA
    scratch = [
        vm((T, D), BF),
        vm((D, 3 * D), BF),
        vm((D, D), BF),
        vm((D, FF), BF),
        vm((FF, D), BF),
        vm((8, 16, 128), F32),
        vm((8, D), F32),
        vm((8, FF), F32),
        vm((T, 3 * D), BF),
        vm((T, 128), BF),
        vm((T, 128), BF),
        vm((T, 128), F32),
        vm((16, T), F32),
        vm((16, T), F32),
        vm((T, D), BF),
        vm((T, D), F32),
        vm((T, 128), F32),
        vm((T, D), BF),
        vm((T, FF), BF),
        vm((T, FF), BF),
        vm((T, D), F32),
        vm((T, D), BF),
        vm((16, D), F32),
        vm((8, 512), F32),
        vm((2, 4, 2, 128, D), BF),
        vm((2, 4, 1, 128, D), BF),
        vm((ACCS, 4, 128, D), BF),
        vm((4, 2, 64, D), BF),
        vm((4, 2, 64, D), BF),
        vm((4, 64, D), BF),
        vm((4, 64, D), BF),
        vm((4, 128, D), BF),
        vm((4, 128, D), BF),
        vm((4, 128, D), BF),
        vm((NCHUNK, 128, D), BF),
        vm((16, D), F32),
        vm((5, 16, D), F32),
        sem((GROUPS, 14)),
        sem((GROUPS, 14)),
        sem((13,)),
        sem((7,)),
        sem((7,)),
        sem((22,)),
        sem((22,)),
        sem((4, 9)),
        sem((4, 9)),
        sem((NCHUNK,)),
        sem((NCHUNK,)),
        sem((5,)),
        sem((5,)),
        sem((2 + NCHUNK,)),
    ]
    shape = jax.ShapeDtypeStruct
    any_ = pl.BlockSpec(memory_space=pl.ANY)
    vmem = pl.BlockSpec(memory_space=pltpu.VMEM)
    return pl.pallas_call(
        fused_kernel,
        name="layer_step",
        out_shape=(
            shape((T, D), BF),
            shape((T, D), BF),
            shape((NCHUNK, 128, D), BF),
            shape((16, 384), F32),
        ),
        in_specs=[any_, vmem, vmem] + [vmem] * 9 + [any_] * 6,
        out_specs=(any_,) * 3 + (vmem,),
        scratch_shapes=scratch,
        compiler_params=pltpu.CompilerParams(
            collective_id=0, has_side_effects=True, vmem_limit_bytes=64 * 2**20
        ),
        cost_estimate=pl.CostEstimate(
            flops=60 * 10**9, bytes_accessed=30 * 2**20, transcendentals=10**7
        ),
    )(tokens, seg, pairing, *vectors, *shards[:6])


def local_fused(tokens, segment_ids, pairing, *shards):
    width = tokens.shape[-1]
    (bq, bv, bo, bup, bdn, g1, s1, g2, s2) = shards[6:]
    vectors = [piece.reshape(1, -1) for piece in (bq, bv, bo, bdn, g1, s1, g2, s2)]
    vectors.append(bup.reshape(3, 128))
    raw = fused_call(tokens.reshape(-1, width), segment_ids, pairing.reshape(1, -1), vectors, shards)
    results = finish_call(*raw)
    return (
        (results[0].reshape(tokens.shape), results[1].reshape(tokens.shape))
        + tuple(results[2:8])
        + tuple(piece.reshape(-1) for piece in results[8:])
    )


def norm_piece(residual, gain_vector, shift_vector):
    centre = jnp.mean(residual, -1, keepdims=True)
    offset = residual - centre
    spread = jnp.mean(offset * offset, -1, keepdims=True)
    return offset * lax.rsqrt(spread + 1e-12) * gain_vector + shift_vector


def gelu_exact(argument):
    return jax.nn.gelu(argument, approximate=False)


def pool_texts(layer_out, segments):
    member = (segments[:, None] == jnp.arange(SEGS)[None, :]).astype(jnp.float32)
    totals = jnp.dot(member.T, layer_out, precision=lax.Precision.HIGHEST)
    counts = jnp.sum(member, 0)
    pooled = totals / counts[:, None]
    return pooled * lax.rsqrt(jnp.sum(pooled * pooled, -1, keepdims=True) + 1e-06)


def project(inputs, weight, bias_vector):
    return jnp.dot(inputs, weight, preferred_element_type=jnp.float32) + bias_vector.astype(
        jnp.float32
    )


def head_scores(query_states, key_states, segments):
    row_length = query_states.shape[0]
    scores = jnp.einsum(
        "qhd,khd->hqk",
        query_states.reshape(row_length, H, HD),
        key_states.reshape(row_length, H, HD),
        preferred_element_type=jnp.float32,
    ) * HD ** (-0.5)
    same_text = segments[:, None] == segments[None, :]
    return jnp.where(same_text[None], scores, -1e30)


def attend_forward(pieces):
    query_states, key_states, value_states, segments = pieces
    row_length = query_states.shape[0]
    scores = head_scores(query_states, key_states, segments)
    row_peak = jnp.max(scores, -1, keepdims=True)
    exponent = jnp.exp(scores - row_peak)
    row_total = jnp.sum(exponent, -1, keepdims=True)
    probability = (exponent / row_total).astype(jnp.bfloat16)
    mixture = jnp.einsum(
        "hqk,khd->qhd",
        probability,
        value_states.reshape(row_length, H, HD),
        preferred_element_type=jnp.float32,
    )
    return (mixture.reshape(row_length, H * HD).astype(jnp.bfloat16), row_peak + jnp.log(row_total))


def attend_backward(pieces):
    query_states, key_states, value_states, segments, grad_mixture, log_total = pieces
    row_length = query_states.shape[0]
    query_heads = query_states.reshape(row_length, H, HD)
    key_heads = key_states.reshape(row_length, H, HD)
    value_heads = value_states.reshape(row_length, H, HD)
    grad_heads = grad_mixture.reshape(row_length, H, HD)
    probability = jnp.exp(head_scores(query_states, key_states, segments) - log_total)
    grad_probability = jnp.einsum(
        "qhd,khd->hqk", grad_heads, value_heads, preferred_element_type=jnp.float32
    )
    grad_values = jnp.einsum(
        "hqk,qhd->khd",
        probability.astype(jnp.bfloat16),
        grad_heads,
        preferred_element_type=jnp.float32,
    )
    grad_scores = probability * (
        grad_probability - jnp.sum(probability * grad_probability, -1, keepdims=True)
    )
    grad_scores = grad_scores.astype(jnp.bfloat16)
    score_scale = HD ** (-0.5)
    grad_queries = (
        jnp.einsum("hqk,khd->qhd", grad_scores, key_heads, preferred_element_type=jnp.float32)
        * score_scale
    )
    grad_keys = (
        jnp.einsum("hqk,qhd->khd", grad_scores, query_heads, preferred_element_type=jnp.float32)
        * score_scale
    )
    return (
        grad_queries.reshape(row_length, H * HD).astype(jnp.bfloat16),
        grad_keys.reshape(row_length, H * HD).astype(jnp.bfloat16),
        grad_values.reshape(row_length, H * HD).astype(jnp.bfloat16),
    )


def run_layer(tokens, params, segment_ids):
    (
        query_weight,
        key_weight,
        value_weight,
        out_weight,
        up_weight,
        down_weight,
        query_bias,
        value_bias,
        out_bias,
        up_bias,
        down_bias,
        first_gain,
        first_shift,
        second_gain,
        second_shift,
    ) = params
    row_count, row_length, feature_width = tokens.shape
    flat_tokens = tokens.reshape(row_count * row_length, feature_width)
    query_states = project(flat_tokens, query_weight, query_bias).astype(jnp.bfloat16)
    key_states = jnp.dot(flat_tokens, key_weight, preferred_element_type=jnp.float32).astype(
        jnp.bfloat16
    )
    value_states = project(flat_tokens, value_weight, value_bias).astype(jnp.bfloat16)
    row_shape = (row_count, row_length, feature_width)
    joined, log_total = lax.map(
        attend_forward,
        (
            query_states.reshape(row_shape),
            key_states.reshape(row_shape),
            value_states.reshape(row_shape),
            segment_ids,
        ),
    )
    joined = joined.reshape(row_count * row_length, feature_width)
    resid_one = flat_tokens.astype(jnp.float32) + project(joined, out_weight, out_bias)
    hidden = norm_piece(resid_one, first_gain.astype(jnp.float32), first_shift.astype(jnp.float32))
    expanded = project(hidden.astype(jnp.bfloat16), up_weight, up_bias)
    active = gelu_exact(expanded).astype(jnp.bfloat16)
    resid_two = hidden + project(active, down_weight, down_bias)
    output = norm_piece(
        resid_two, second_gain.astype(jnp.float32), second_shift.astype(jnp.float32)
    )
    return (
        flat_tokens,
        query_states,
        key_states,
        value_states,
        joined,
        log_total,
        resid_one,
        hidden,
        expanded,
        active,
        resid_two,
        output,
    )


def gather_all(shards):
    packed = jnp.concatenate([piece.reshape(-1) for piece in shards])
    gathered = lax.all_gather(packed, "fsdp", axis=0, tiled=True)
    gathered = gathered.reshape(-1, packed.size)
    params, at = [], 0
    for piece in shards:
        part = gathered[:, at : at + piece.size]
        params.append(part.reshape((-1,) + piece.shape[1:]))
        at += piece.size
    return tuple(params)


def reduce_all(grad_params):
    group = lax.axis_size("fsdp")
    packed = jnp.concatenate(
        [piece.astype(jnp.bfloat16).reshape(group, -1) for piece in grad_params], 1
    )
    share = lax.psum_scatter(packed.reshape(-1), "fsdp", scatter_dimension=0, tiled=True)
    total = lax.psum(share, "rep").astype(jnp.float32)
    totals, at = [], 0
    for piece in grad_params:
        count = piece.size // group
        shape = (piece.shape[0] // group,) + piece.shape[1:]
        totals.append(total[at : at + count].reshape(shape))
        at += count
    return tuple(totals)


def local(
    tokens,
    segment_ids,
    pairing,
    query_weight,
    key_weight,
    value_weight,
    out_weight,
    up_weight,
    down_weight,
    query_bias,
    value_bias,
    out_bias,
    up_bias,
    down_bias,
    first_gain,
    first_shift,
    second_gain,
    second_shift,
):
    shards = (
        query_weight,
        key_weight,
        value_weight,
        out_weight,
        up_weight,
        down_weight,
        query_bias,
        value_bias,
        out_bias,
        up_bias,
        down_bias,
        first_gain,
        first_shift,
        second_gain,
        second_shift,
    )
    params = gather_all(shards)
    row_count, row_length, feature_width = tokens.shape
    states = run_layer(tokens, params, segment_ids)
    output = states[11].reshape(row_count, row_length, feature_width)

    def embed_rows(layer_out):
        return jax.vmap(pool_texts)(layer_out, segment_ids)

    embedded, embed_pullback = jax.vjp(embed_rows, output)
    local_count = row_count * SEGS
    local_embed = embedded.reshape(local_count, feature_width).astype(jnp.bfloat16)
    everything = lax.all_gather(local_embed, ("rep", "fsdp"), axis=0, tiled=True)
    text_count = everything.shape[0]
    pair_count = text_count // 2
    local_ids = lax.axis_index(("rep", "fsdp")) * local_count + jnp.arange(
        local_count, dtype=jnp.int32
    )
    matches = pairing[None, :] == local_ids[:, None]
    position = jnp.sum(jnp.where(matches, jnp.arange(text_count, dtype=jnp.int32)[None, :], 0), 1)
    pair_index = position // 2
    query_flag = position % 2 == 0
    passages = everything[pairing[1::2]]
    logits = (
        jnp.einsum("td,pd->tp", local_embed, passages, preferred_element_type=jnp.float32) * 100.0
    )
    row_peak = jnp.max(logits, 1, keepdims=True)
    exponent = jnp.exp(logits - row_peak)
    softmax_rows = exponent / jnp.sum(exponent, 1, keepdims=True)
    pairs = jnp.arange(pair_count, dtype=jnp.int32)[None, :]
    target = (pairs == pair_index[:, None]).astype(jnp.float32)
    queries = everything[pairing[0::2]]
    whole = jnp.einsum("qd,pd->qp", queries, passages, preferred_element_type=jnp.float32) * 100.0
    peak_all = jnp.max(whole, 1)
    total_all = jnp.sum(jnp.exp(whole - peak_all[:, None]), 1)
    cross = jnp.einsum("td,qd->tq", local_embed, queries, preferred_element_type=jnp.float32) * 100.0
    softmax_columns = jnp.exp(cross - peak_all[None, :]) / total_all[None, :]
    scaled_rows = ((softmax_rows - target) * 100.0).astype(jnp.bfloat16)
    scaled_columns = ((softmax_columns - target) * 100.0).astype(jnp.bfloat16)
    grad_query = jnp.einsum("tp,pd->td", scaled_rows, passages, preferred_element_type=jnp.float32)
    grad_passage = jnp.einsum(
        "tq,qd->td", scaled_columns, queries, preferred_element_type=jnp.float32
    )
    grad_embed = jnp.where(query_flag[:, None], grad_query, grad_passage)
    (grad_output,) = embed_pullback(grad_embed.reshape(row_count, SEGS, feature_width))
    flat_tokens, query_states, key_states, value_states, joined, log_total = states[:6]
    resid_one, hidden, expanded, active, resid_two = states[6:11]
    w_query_full, w_key_full, w_value_full, w_out_full, w_up_full, w_down_full = params[:6]
    first_gain_f = params[11].astype(jnp.float32)
    first_shift_f = params[12].astype(jnp.float32)
    second_gain_f = params[13].astype(jnp.float32)
    second_shift_f = params[14].astype(jnp.float32)
    token_total = row_count * row_length
    norm_out, second_pullback = jax.vjp(norm_piece, resid_two, second_gain_f, second_shift_f)
    grad_resid_two, grad_second_gain, grad_second_shift = second_pullback(
        grad_output.reshape(token_total, feature_width)
    )
    grad_feed = grad_resid_two.astype(jnp.bfloat16)
    grad_down_weight = jnp.einsum(
        "nf,nd->fd", active, grad_feed, preferred_element_type=jnp.float32
    )
    grad_down_bias = jnp.sum(grad_feed.astype(jnp.float32), 0)
    grad_active = jnp.einsum(
        "nd,fd->nf", grad_feed, w_down_full, preferred_element_type=jnp.float32
    )
    gelu_out, gelu_pullback = jax.vjp(gelu_exact, expanded)
    grad_expanded = gelu_pullback(grad_active)[0].astype(jnp.bfloat16)
    grad_up_weight = jnp.einsum(
        "nd,nf->df", hidden.astype(jnp.bfloat16), grad_expanded, preferred_element_type=jnp.float32
    )
    grad_up_bias = jnp.sum(grad_expanded.astype(jnp.float32), 0)
    grad_hidden = grad_resid_two + jnp.einsum(
        "nf,df->nd", grad_expanded, w_up_full, preferred_element_type=jnp.float32
    )
    hidden_out, first_pullback = jax.vjp(norm_piece, resid_one, first_gain_f, first_shift_f)
    grad_resid_one, grad_first_gain, grad_first_shift = first_pullback(grad_hidden)
    grad_branch = grad_resid_one.astype(jnp.bfloat16)
    grad_out_weight = jnp.einsum(
        "nd,ne->de", joined, grad_branch, preferred_element_type=jnp.float32
    )
    grad_out_bias = jnp.sum(grad_branch.astype(jnp.float32), 0)
    grad_joined = jnp.einsum(
        "ne,de->nd", grad_branch, w_out_full, preferred_element_type=jnp.float32
    ).astype(jnp.bfloat16)
    row_shape = (row_count, row_length, feature_width)
    grad_queries, grad_keys, grad_values = lax.map(
        attend_backward,
        (
            query_states.reshape(row_shape),
            key_states.reshape(row_shape),
            value_states.reshape(row_shape),
            segment_ids,
            grad_joined.reshape(row_shape),
            log_total,
        ),
    )
    grad_queries = grad_queries.reshape(token_total, feature_width)
    grad_keys = grad_keys.reshape(token_total, feature_width)
    grad_values = grad_values.reshape(token_total, feature_width)
    grad_query_weight = jnp.einsum(
        "nd,ne->de", flat_tokens, grad_queries, preferred_element_type=jnp.float32
    )
    grad_key_weight = jnp.einsum(
        "nd,ne->de", flat_tokens, grad_keys, preferred_element_type=jnp.float32
    )
    grad_value_weight = jnp.einsum(
        "nd,ne->de", flat_tokens, grad_values, preferred_element_type=jnp.float32
    )
    grad_query_bias = jnp.sum(grad_queries.astype(jnp.float32), 0)
    grad_value_bias = jnp.sum(grad_values.astype(jnp.float32), 0)
    grad_inputs = grad_resid_one
    grad_inputs = grad_inputs + jnp.einsum(
        "ne,de->nd", grad_queries, w_query_full, preferred_element_type=jnp.float32
    )
    grad_inputs = grad_inputs + jnp.einsum(
        "ne,de->nd", grad_keys, w_key_full, preferred_element_type=jnp.float32
    )
    grad_inputs = grad_inputs + jnp.einsum(
        "ne,de->nd", grad_values, w_value_full, preferred_element_type=jnp.float32
    )
    grad_params = (
        grad_query_weight,
        grad_key_weight,
        grad_value_weight,
        grad_out_weight,
        grad_up_weight,
        grad_down_weight,
        grad_query_bias,
        grad_value_bias,
        grad_out_bias,
        grad_up_bias,
        grad_down_bias,
        grad_first_gain,
        grad_first_shift,
        grad_second_gain,
        grad_second_shift,
    )
    totals = reduce_all(grad_params)
    return (
        output.astype(jnp.bfloat16),
        grad_inputs.reshape(row_shape).astype(jnp.bfloat16),
    ) + tuple(totals)


def solution(mesh):
    in_specs = (
        P(("rep", "fsdp"), None, None),
        P(("rep", "fsdp"), None),
        P(),
        P("fsdp", None),
        P("fsdp", None),
        P("fsdp", None),
        P("fsdp", None),
        P("fsdp", None),
        P("fsdp", None),
        P("fsdp"),
        P("fsdp"),
        P("fsdp"),
        P("fsdp"),
        P("fsdp"),
        P("fsdp"),
        P("fsdp"),
        P("fsdp"),
        P("fsdp"),
    )
    out_specs = (
        P(("rep", "fsdp"), None, None),
        P(("rep", "fsdp"), None, None),
        P("fsdp", None),
        P("fsdp", None),
        P("fsdp", None),
        P("fsdp", None),
        P("fsdp", None),
        P("fsdp", None),
        P("fsdp"),
        P("fsdp"),
        P("fsdp"),
        P("fsdp"),
        P("fsdp"),
        P("fsdp"),
        P("fsdp"),
        P("fsdp"),
        P("fsdp"),
    )

    def whole(*arrays):
        fits = (
            mesh.shape["fsdp"] == 8
            and mesh.shape["rep"] == 4
            and arrays[0].shape == (64, 512, 768)
            and arrays[7].shape == (768, 3072)
        )
        return jax.shard_map(
            local_fused if fits else local,
            mesh=mesh,
            in_specs=in_specs,
            out_specs=out_specs,
            check_vma=False,
        )(*arrays)

    return whole
```

```python
import functools

import jax
import jax.numpy as jnp
from jax import lax
from jax.experimental import pallas as pl
from jax.experimental.pallas import tpu as pltpu
from jax.sharding import PartitionSpec as P

H = 12
HD = 64
SEGS = 8
MESH = pl.DeviceIdType.MESH
BF = jnp.bfloat16
F32 = jnp.float32


T = 1024
D = 768
FF = 3072
ROW = 512
NEG = -1e30
QA, QB, QC, WO, UA, UB, DA, DB = range(8)
GROUPS = 8
UNITS = (96, 96, 96, 96, 96, 96, 384, 384)
(XW, YW, S0, ZX, D2, SX, ZY, D1, SY, ZD, SD, SZX, SZY, SZD) = range(14)
ACCS = 4
OWN, XIN, YIN, DIN, ZXIN, ZYIN, ZDIN, READY = range(8)
START, MASKS, VECTORS, PROJECT, ATTEND, MERGE, EXPAND, REDUCE = range(8)
PLAN = {
    (START, 0): (
        (OWN, QA), (OWN, QB),
    ),
    (MASKS, 0): (
        (OWN, QC), (XIN, QA), (YIN, QA),
    ),
    (VECTORS, 0): (
        (XIN, QB), (YIN, QB), (ZXIN, QA), (OWN, WO), (ZYIN, QA),
        (XIN, QC), (YIN, QC), (DIN, QA), (ZXIN, QB), (DIN, QB),
        (ZYIN, QB), (OWN, UA), (ZXIN, QC), (ZYIN, QC), (XIN, WO),
        (YIN, WO), (ZDIN, QA), (DIN, QC), (ZDIN, QB), (READY, QA),
    ),
    (PROJECT, 0): (
        (ZXIN, WO), (OWN, UB),
    ),
    (PROJECT, 1): (
        (ZYIN, WO),
    ),
    (ATTEND, 0): (
        (ZDIN, QC), (DIN, WO), (XIN, UA), (YIN, UA),
    ),
    (ATTEND, 1): (
        (READY, QB),
    ),
    (PROJECT, 3): (
        (ZDIN, WO), (OWN, DA),
    ),
    (ATTEND, 2): (
        (ZXIN, UA), (XIN, UB), (YIN, UB),
    ),
    (ATTEND, 3): (
        (DIN, UA), (ZYIN, UA), (READY, QC),
    ),
    (ATTEND, 4): (
        (ZXIN, UB), (XIN, DA), (YIN, DA),
    ),
    (ATTEND, 5): (
        (DIN, UB), (ZYIN, UB), (OWN, DB), (READY, WO),
    ),
    (MERGE, 0): (
        (ZDIN, UA),
    ),
    (MERGE, 1): (
        (DIN, DA),
    ),
    (MERGE, 2): (
        (ZXIN, DA),
    ),
    (MERGE, 3): (
        (READY, UA),
    ),
    (EXPAND, 1): (
        (ZYIN, DA),
    ),
    (EXPAND, 2): (
        (XIN, DB), (YIN, DB),
    ),
    (EXPAND, 3): (
        (ZDIN, UB),
    ),
    (EXPAND, 5): (
        (READY, UB),
    ),
    (EXPAND, 6): (
        (ZDIN, DA),
    ),
    (EXPAND, 8): (
        (DIN, DB),
    ),
    (EXPAND, 9): (
        (ZXIN, DB),
    ),
    (EXPAND, 11): (
        (READY, DA),
    ),
    (REDUCE, 0): (
        (ZYIN, DB),
    ),
    (REDUCE, 1): (
        (ZDIN, DB), (READY, DB),
    ),
}


DOWN, SLOPE, UP, FIRST, OUT, MIX, HEADS, GROUP, TOKEN, SUMS, SHARE = range(11)
SEND, X1, X2, Z1, Z2, Z3, END = range(11, 18)
BACK = (
    (DOWN, 1), (SEND, 0), (DOWN, 0), (X1, 0), (SEND, 1), (SLOPE, 0), (DOWN, 2), (X1, 1),
    (SEND, 2), (SLOPE, 1), (UP, 1), (X2, 0), (X1, 2), (SEND, 3), (SLOPE, 2), (SLOPE, 3),
    (X2, 1), (X1, 3), (FIRST, 0), (Z1, 0), (FIRST, 1), (FIRST, 2), (X2, 2), (FIRST, 3), (Z1, 1),
    (UP, 0), (SEND, 4), (Z2, 0), (UP, 2), (X2, 3), (X1, 4), (SEND, 5), (OUT, 0), (Z1, 2),
    (X1, 5), (SEND, 6), (Z2, 1), (MIX, 0), (Z3, 0), (Z1, 3), (HEADS, 0), (X2, 4), (X1, 6),
    (Z2, 2), (UP, 3), (SEND, 7), (Z3, 1), (X2, 5), (HEADS, 1), (END, 0), (Z2, 3), (Z1, 4),
    (X1, 7), (GROUP, 0), (SEND, 8), (Z3, 2), (X2, 6), (HEADS, 2), (END, 1), (Z3, 3), (Z2, 4),
    (Z1, 5), (X1, 8), (X2, 7), (HEADS, 3), (END, 2), (Z1, 6), (GROUP, 1), (SEND, 9), (Z3, 4),
    (Z2, 5), (X2, 8), (HEADS, 4), (END, 3), (Z1, 7), (Z2, 6), (X1, 9), (HEADS, 5), (END, 4),
    (Z3, 5), (Z1, 8), (GROUP, 2), (SEND, 10), (TOKEN, 0), (Z3, 6), (Z2, 7), (X2, 9), (X1, 10),
    (GROUP, 3), (SEND, 11), (TOKEN, 1), (END, 5), (Z2, 8), (X1, 11), (SUMS, 0), (Z1, 9),
    (TOKEN, 2), (Z3, 7), (X2, 10), (SHARE, 0), (END, 6), (TOKEN, 3), (X2, 11), (Z1, 10),
    (Z3, 8), (Z2, 9), (SHARE, 1), (END, 7), (Z1, 11), (Z2, 10), (SHARE, 2), (END, 8), (Z3, 9),
    (Z2, 11), (SHARE, 3), (Z3, 10), (Z3, 11), (SHARE, 4), (END, 9), (END, 10), (END, 11),
)
CHUNK_NAMES = tuple(step for step in BACK if step[0] in (DOWN, UP, OUT, GROUP))
NCHUNK = len(CHUNK_NAMES)


def chunk_shape(i):
    kind, number = CHUNK_NAMES[i]
    return (128 if kind == DOWN else 96), (D // 2 if kind == GROUP and number > 1 else D)


def dg(left, right, left_axis, right_axis):
    return lax.dot_general(
        left, right, (((left_axis,), (right_axis,)), ((), ())), preferred_element_type=F32
    )


def split_two(value):
    high = value.astype(BF)
    return high, (value - high.astype(F32)).astype(BF)


def aligned(start, size, step):
    return pl.ds(pl.multiple_of(start, step), size)


def gelu(z):
    return z * (0.5 + 0.5 * lax.erf(z * 0.7071067811865476))


def gelu_slope(z):
    below = 0.5 + 0.5 * lax.erf(z * 0.7071067811865476)
    return below + z * (0.3989422804014327 * jnp.exp(-0.5 * (z * z)))


def normalize(residual):
    centre = jnp.mean(residual, -1, keepdims=True)
    offset = residual - centre
    spread = jnp.mean(offset * offset, -1, keepdims=True)
    scale = lax.rsqrt(spread + 1e-12)
    return offset * scale, scale


def fused_kernel(
    tokens,
    seg,
    pairing,
    bq_in,
    bv_in,
    bo_in,
    bdn_in,
    g1_in,
    s1_in,
    g2_in,
    s2_in,
    bup_in,
    wq_in,
    wk_in,
    wv_in,
    wo_in,
    wup_in,
    wdn_in,
    out_y,
    out_dx,
    out_grads,
    out_vec,
    x_s,
    wqkv,
    wo,
    wup,
    wdn,
    sb,
    vecs,
    upb,
    qkv,
    seg_q,
    seg_k,
    lse,
    lse_t,
    dot_t,
    ao,
    n1,
    scales,
    h1b,
    g_s,
    gp,
    n2,
    df,
    npool,
    meta,
    c_s,
    rsib,
    acc,
    rx,
    ry,
    rx2,
    ry2,
    zs,
    rz1,
    rz2,
    fin,
    vg,
    vr,
    gsend,
    grecv,
    lsem,
    bsend,
    brecv,
    esend,
    erecv,
    xsend,
    xrecv,
    fsend,
    frecv,
    vsend,
    vrecv,
    osem,
):
    rep = lax.axis_index("rep")
    f = lax.axis_index("fsdp")
    core = f & 1
    chip = f >> 1
    pz = rep & 1
    dev_s, dev_x, dev_y, dev_d = (rep, f ^ 1), (rep, f ^ 2), (rep, f ^ 4), (rep, f ^ 6)
    dev_z1, dev_z2, dev_z3 = (rep ^ 1, f), (rep ^ 2, f), (rep ^ 3, f)
    weights = (
        (wqkv, 0, D),
        (wqkv, D, D),
        (wqkv, 2 * D, D),
        (wo, 0, D),
        (wup, 0, FF // 2),
        (wup, FF // 2, FF // 2),
        (wdn, 0, D // 2),
        (wdn, D // 2, D // 2),
    )

    def remote(src, dst, ssem, rsem, dev):
        return pltpu.make_async_remote_copy(
            src_ref=src, dst_ref=dst, send_sem=ssem, recv_sem=rsem, device_id=dev, device_id_type=MESH
        )

    def local_pairs():
        own = aligned(f * 96, 96, 16)
        pairs = []
        for group in range(3):
            for n, ref in enumerate((wq_in, wk_in, wv_in)):
                cols = pl.ds(D * group + 256 * n, 256)
                pairs.append((ref.at[:, pl.ds(256 * group, 256)], wqkv.at[own, cols]))
        pairs.append((wo_in, wo.at[own, :]))
        pairs.append((wup_in, wup.at[own, :]))
        pairs.append((wdn_in, wdn.at[aligned(f * 384, 384, 16), :]))
        pairs.append((tokens, x_s))
        return pairs

    locals_ = [
        pltpu.make_async_copy(src, dst, lsem.at[i]) for i, (src, dst) in enumerate(local_pairs())
    ]
    for copy in locals_:
        copy.start()
    for k, ref in enumerate((bq_in, bv_in, bo_in, bdn_in, g1_in, s1_in, g2_in, s2_in)):
        sb[pl.ds(f, 1), k : k + 1, 0:96] = ref[...].astype(F32).reshape(1, 1, 96)
        sb[pl.ds(f, 1), k : k + 1, 96:128] = jnp.zeros((1, 1, 32), F32)
    for k in range(3):
        sb[pl.ds(f, 1), 8 + k : 9 + k, :] = bup_in[k : k + 1, :].astype(F32).reshape(1, 1, 128)
    sb[pl.ds(f, 1), 11:16, :] = jnp.zeros((1, 5, 128), F32)

    barrier = pltpu.get_barrier_semaphore()
    peers = [(rep, f ^ k) for k in range(1, 8)] + [dev_z1, dev_z2, dev_z3]
    for peer in peers:
        pl.semaphore_signal(barrier, inc=1, device_id=peer, device_id_type=MESH)
    pl.semaphore_wait(barrier, len(peers))

    def full(g, who):
        return who * UNITS[g], UNITS[g]

    def wide(g, who):
        return who * UNITS[g] + (UNITS[g] // 3) * pz, 2 * (UNITS[g] // 3)

    def part_m(g, who):
        return who * UNITS[g] + 2 * (UNITS[g] // 3) * pz, UNITS[g] // 3

    def part_a(g, who):
        return who * UNITS[g] + UNITS[g] // 3, UNITS[g] // 3

    def part_o(g, who):
        return who * UNITS[g] + 2 * (UNITS[g] // 3) * (1 - pz), UNITS[g] // 3

    fx, fy, fd, fs = f ^ 2, f ^ 4, f ^ 6, f ^ 1
    fsx, fsy, fsd = fs ^ 2, fs ^ 4, fs ^ 6
    sent_rows = {
        XW: (wide, f, dev_x),
        YW: (wide, f, dev_y),
        S0: (full, f, dev_s),
        ZX: (part_m, fx, dev_z1),
        D2: (part_m, fx, dev_y),
        SX: (wide, fx, dev_s),
        ZY: (part_m, fy, dev_z1),
        D1: (part_a, fy, dev_x),
        SY: (wide, fy, dev_s),
        ZD: (part_m, fd, dev_z1),
        SD: (wide, fd, dev_s),
        SZX: (part_o, fx, dev_s),
        SZY: (part_o, fy, dev_s),
        SZD: (part_o, fd, dev_s),
    }
    got_rows = {
        XW: (wide, fx),
        YW: (wide, fy),
        S0: (full, fs),
        ZX: (part_o, fx),
        D2: (part_m, fd),
        SX: (wide, fsx),
        ZY: (part_o, fy),
        D1: (part_a, fd),
        SY: (wide, fsy),
        ZD: (part_o, fd),
        SD: (wide, fsd),
        SZX: (part_o, fsx),
        SZY: (part_o, fsy),
        SZD: (part_o, fsd),
    }

    def weight_rows(g, start, size):
        ref, first, width = weights[g]
        return ref.at[aligned(start, size, 16), pl.ds(first, width)]

    def gather_copy(g, piece):
        rows, who, dev = sent_rows[piece]
        start, size = rows(g, who)
        view = weight_rows(g, start, size)
        return remote(view, view, gsend.at[g, piece], grecv.at[g, piece], dev)

    def g_send(g, *pieces):
        for piece in pieces:
            gather_copy(g, piece).start()

    def g_recv(g, *pieces):
        for piece in pieces:
            rows, who = got_rows[piece]
            start, size = rows(g, who)
            view = weight_rows(g, start, size)
            remote(
                view, view, gsend.at[g, piece], grecv.at[g, piece], sent_rows[piece][2]
            ).wait_recv()

    def g_done(g):
        for piece in range(14):
            gather_copy(g, piece).wait_send()

    def step_own(g):
        for i in ((0, 1, 2), (3, 4, 5), (6, 7, 8), (9,), (10,), (), (11,), ())[g]:
            locals_[i].wait()
        g_send(g, XW, YW, S0)

    def step_ready(g):
        g_recv(g, S0, SX, SY, SD, SZX, SZY, SZD)

    def relay(waits, sends):
        def step(g):
            g_recv(g, *waits)
            g_send(g, *sends)

        return step

    gather_steps = {
        OWN: step_own,
        XIN: relay((XW,), (ZX, D2, SX)),
        YIN: relay((YW,), (D1, ZY, SY)),
        DIN: relay((D1, D2), (ZD, SD)),
        ZXIN: relay((ZX,), (SZX,)),
        ZYIN: relay((ZY,), (SZY,)),
        ZDIN: relay((ZD,), (SZD,)),
        READY: step_ready,
    }

    def after(kind, n):
        for step, g in PLAN.get((kind, n), ()):
            gather_steps[step](g)

    def stepped(count, body, kind, first=0):
        def one(i, carry):
            body(i)
            for k in range(count - 1):
                if (kind, first + k) in PLAN:
                    pl.when(i == k)(lambda n=first + k: after(kind, n))
            return carry

        lax.fori_loop(0, count, one, 0)
        after(kind, first + count - 1)

    def small_copy(k):
        view = sb.at[pl.ds(f, 1)]
        return remote(view, view, bsend.at[k - 1], brecv.at[k - 1], (rep, f ^ k))

    step_own(QA)
    for k in range(1, 8):
        small_copy(k).start()
    for step, g in PLAN[START, 0][1:]:
        gather_steps[step](g)

    segf = seg[...].astype(F32)

    def segment_columns():
        for r in range(2):
            lse[pl.ds(r * ROW, ROW), :] = jnp.broadcast_to(segf[r : r + 1, :], (128, ROW)).T

    segment_columns()
    seg_lane = lax.broadcasted_iota(jnp.int32, (T, 128), 1).astype(F32)
    same = jnp.where(lse[...] == seg_lane, 1.0, 0.0)
    seg_q[...] = same.astype(BF)
    seg_k[...] = jnp.where(seg_lane < SEGS, NEG * (1.0 - same), 0.0).astype(BF)

    after(MASKS, 0)

    places = jnp.broadcast_to(pairing[...].astype(F32), (128, 512)).T[:, 0:1]
    texts = lax.broadcasted_iota(jnp.int32, (512, 512), 1).astype(F32)
    order_no = lax.broadcasted_iota(jnp.int32, (512, 512), 0).astype(F32)
    found = jnp.sum(jnp.where(places == texts, order_no, 0.0), 0, keepdims=True)
    meta[...] = jnp.broadcast_to(found, (8, 512))

    for k in range(1, 8):
        view = sb.at[pl.ds(f ^ k, 1)]
        remote(view, view, bsend.at[k - 1], brecv.at[k - 1], (rep, f ^ k)).wait_recv()
    lane = lax.broadcasted_iota(jnp.int32, (128, D), 0)
    column = lax.broadcasted_iota(jnp.int32, (128, D), 1)
    total = jnp.zeros((8, D), F32)
    for k in range(8):
        for j in range(3):
            upb[0:1, k * 384 + 128 * j : k * 384 + 128 * j + 128] = sb[k, 8 + j : 9 + j, :]
        place = jnp.where((column == lane + 96 * k) & (lane < 96), 1.0, 0.0).astype(BF)
        total = total + dg(sb[k, 0:8, :].astype(BF), place, 1, 0)
    vecs[...] = total
    bq, bv, bo, bdn = (vecs[i : i + 1, :] for i in range(4))
    g1, s1, g2, s2 = (vecs[i : i + 1, :] for i in range(4, 8))
    locals_[12].wait()

    after(VECTORS, 0)

    lane_row = lax.broadcasted_iota(jnp.int32, (1, 128), 1)
    even = (lane_row < HD).astype(F32).astype(BF)
    odd = (lane_row >= HD).astype(F32).astype(BF)
    tile_lane = lax.broadcasted_iota(jnp.int32, (256, 128), 1)
    scaling = jnp.where(lax.broadcasted_iota(jnp.int32, (1, D), 1) < 256, 0.125, 1.0).astype(BF)

    def both(value):
        return jnp.concatenate([value * even, value * odd], axis=0)

    def project(group):
        cols = pl.ds(D * group, D)
        part = pl.ds(256 * group, 256)
        bias = jnp.concatenate([vecs[0:1, part], jnp.zeros((1, 256), F32), vecs[1:2, part]], 1)

        def qkv_step(i):
            rows = aligned(i * 512, 512, 512)
            qkv[rows, cols] = (dg(x_s[rows, :], wqkv[:, cols], 1, 0) + bias).astype(BF) * scaling

        stepped(2, qkv_step, PROJECT, 2 * group)

    def attend(r, pair, b):
        kq = aligned(r * ROW + 128 * b, 384, 128)
        qq = aligned(r * ROW + 256 * b, 256, 256)
        at = D * (pair // 2) + 128 * (pair % 2)
        q = qkv[qq, pl.ds(at, 128)]
        v = qkv[kq, pl.ds(at + 512, 128)]
        keys = jnp.concatenate([qkv[kq, pl.ds(at + 256, 128)], seg_k[kq, :]], 1)
        ids = seg_q[qq, :]
        queries = jnp.concatenate(
            [jnp.concatenate([q * even, ids], 1), jnp.concatenate([q * odd, ids], 1)], 0
        )
        scores = dg(queries, keys, 1, 1)
        mixed, peaks, totals = [], [], []
        for h in range(2):
            part = scores[256 * h : 256 * h + 256]
            peak = jnp.max(part, 1, keepdims=True)
            e = jnp.exp(part - peak)
            totals.append(jnp.sum(e, 1, keepdims=True))
            peaks.append(peak)
            mixed.append(dg(e.astype(BF), v, 1, 0))
        first = tile_lane < HD
        total = jnp.where(first, totals[0], totals[1])
        ao[qq, pl.ds(128 * pair, 128)] = (jnp.where(first, mixed[0], mixed[1]) * (1.0 / total)).astype(BF)
        logs = jnp.where(first, peaks[0], peaks[1]) + jnp.log(total)
        lse[qq, :] = jnp.where((tile_lane & 63) == pair, logs, lse[qq, :])

    def attend_group(group):
        def attend_step(r):
            for pair in (2 * group, 2 * group + 1):
                for b in range(2):
                    attend(r, pair, b)

        stepped(2, attend_step, ATTEND, 2 * group)

    lse[...] = jnp.zeros((T, 128), F32)
    for group in range(3):
        project(group)
        attend_group(group)
    for k in range(8):
        turned = lse[128 * k : 128 * k + 128, :].T
        lse_t[0:8, 128 * k : 128 * k + 128] = turned[0:8]
        lse_t[8:16, 128 * k : 128 * k + 128] = turned[64:72]

    def out_step(i):
        rows = aligned(i * 256, 256, 256)
        r1 = x_s[rows, :].astype(F32) + (dg(ao[rows, :], wo[...], 1, 0) + bo)
        n, scale = normalize(r1)
        n1[rows, :] = n
        scales[rows, 0:64] = jnp.broadcast_to(scale, (256, 64))
        h1b[rows, :] = (n * g1 + s1).astype(BF)

    stepped(4, out_step, MERGE)

    def up_step(i):
        cols = aligned(i * 256, 256, 256)
        z = dg(h1b[...], wup[:, cols], 1, 0) + upb[0:1, cols]
        g_s[:, cols] = gelu(z).astype(BF)
        gp[:, cols] = z.astype(BF)

    stepped(12, up_step, EXPAND)

    def slope_part(first, last):
        def part(i, carry):
            rows = aligned(i * 64, 64, 64)
            gp[rows, :] = gelu_slope(gp[rows, :].astype(F32)).astype(BF)
            return carry

        lax.fori_loop(first, last, part, 0)

    npool[...] = jnp.zeros((16, D), F32)
    text_row = lax.broadcasted_iota(jnp.int32, (16, ROW), 0)

    def member_of(r):
        ids = seg[pl.ds(r, 1), :] + 8 * r
        return (text_row == ids).astype(F32)

    left, right = pl.ds(0, D // 2), pl.ds(D // 2, D // 2)

    def down_left(i):
        rows = aligned(i * 512, 512, 512)
        n2[rows, left] = dg(g_s[rows, :], wdn[:, left], 1, 0)

    stepped(2, down_left, REDUCE)
    for r in range(2):
        rows = pl.ds(r * ROW, ROW)
        h1 = n1[rows, :] * g1 + s1
        fed = jnp.concatenate([n2[rows, left], dg(g_s[rows, :], wdn[:, right], 1, 0)], 1)
        n, scale = normalize(h1 + (fed + bdn))
        n2[rows, :] = n
        scales[rows, 64:128] = jnp.broadcast_to(scale, (ROW, 64))
        member = member_of(r).astype(BF)
        high, low = split_two(n)
        npool[...] += dg(member, high, 1, 0) + dg(member, low, 1, 0)

    lse[0:512, :] = jnp.broadcast_to(meta[0:1, :], (128, 512)).T

    members = jnp.concatenate([member_of(0), member_of(1)], axis=1)
    counts = jnp.sum(members, 1, keepdims=True)
    members = members.astype(BF)
    pooled = npool[...] / counts * g2 + s2
    inverse = lax.rsqrt(jnp.sum(pooled * pooled, 1, keepdims=True) + 1e-06)
    embed = pooled * inverse
    acc[pl.ds(rep, 1), 0, aligned(16 * f, 16, 16), :] = embed.astype(BF).reshape(1, 16, D)

    def e_copy(plane, who, dev, number):
        view = acc.at[pl.ds(plane, 1), 0, aligned(16 * who, 16, 16), :]
        return remote(view, view, esend.at[number], erecv.at[number], dev)

    def e_column(who, number):
        view = acc.at[:, 0, aligned(16 * who, 16, 16), :]
        return remote(view, view, esend.at[number], erecv.at[number], dev_s)

    plane_devs = (dev_x, dev_y, dev_d, dev_s)
    e_sends = [e_copy(rep, f, (rep ^ k, f), k - 1) for k in (1, 2, 3)]
    e_sends += [e_copy(rep, f, dev, 3 + 4 * n) for n, dev in enumerate(plane_devs)]
    for copy in e_sends:
        copy.start()
    slope_part(0, 4)
    for g in range(GROUPS):
        g_done(g)
    for k in range(1, 8):
        small_copy(k).wait_send()
    for k in (1, 2, 3):
        e_copy(rep ^ k, f, (rep ^ k, f), k - 1).wait_recv()
        for n, dev in enumerate(plane_devs):
            e_sends.append(e_copy(rep ^ k, f, dev, 3 + 4 * n + k))
            e_sends[-1].start()
    slope_part(4, 13)
    for r in range(2):
        rows = pl.ds(r * ROW, ROW)
        df[rows, :] = (n2[rows, :] * g2 + s2).astype(BF)
    y_copy = pltpu.make_async_copy(df, out_y, osem.at[0])
    y_copy.start()
    for n, who in enumerate((fx, fy, fd)):
        for k in range(4):
            e_copy(rep ^ k, who, plane_devs[n], 3 + 4 * n + k).wait_recv()
        e_sends.append(e_column(who, 19 + n))
        e_sends[-1].start()
    slope_part(13, 16)
    for k in range(4):
        e_copy(rep ^ k, fs, dev_s, 15 + k).wait_recv()
    for n, who in enumerate((fsx, fsy, fsd)):
        e_column(who, 19 + n).wait_recv()
    for copy in e_sends:
        copy.wait_send()

    every = jnp.concatenate([acc[k, 0] for k in range(4)], 0)
    pos_all = meta[0:1, :]
    pair_all = jnp.floor(pos_all * 0.5)
    second_all = pos_all - 2.0 * pair_all
    pos_col = lse[0:512, 0:1]
    second_col = pos_col - 2.0 * jnp.floor(pos_col * 0.5)
    whole = dg(every, every, 1, 1) * 100.0
    whole = jnp.where(second_col > 0.5, whole, NEG)
    peak_all = jnp.max(whole, 0, keepdims=True)
    total_all = jnp.sum(jnp.exp(whole - peak_all), 0, keepdims=True)
    own = embed.astype(BF)
    mine = dg(own, every, 1, 1) * 100.0
    pos_own = lse[aligned((rep * 8 + f) * 16, 16, 16), 0:1]
    pair_own = jnp.floor(pos_own * 0.5)
    second_own = pos_own - 2.0 * pair_own
    same_pair = jnp.where(pair_own == pair_all, 1.0, 0.0)
    rows_masked = jnp.where(second_all > 0.5, mine, NEG)
    row_peak = jnp.max(rows_masked, 1, keepdims=True)
    row_e = jnp.exp(rows_masked - row_peak)
    soft_rows = row_e / jnp.sum(row_e, 1, keepdims=True)
    soft_cols = jnp.exp(jnp.where(second_all > 0.5, NEG, mine - peak_all)) / total_all
    d_rows = (soft_rows - same_pair) * second_all
    d_cols = (soft_cols - same_pair) * (1.0 - second_all)
    d_logits = (jnp.where(second_own > 0.5, d_cols, d_rows) * 100.0).astype(BF)
    d_embed = dg(d_logits, every, 1, 0)
    d_pooled = (d_embed - embed * jnp.sum(embed * d_embed, 1, keepdims=True)) * inverse
    d_each = d_pooled / counts
    vg[...] = jnp.zeros((16, D), F32)
    vg[6:7, :] = jnp.sum(d_each * npool[...], 0, keepdims=True)
    vg[7:8, :] = jnp.sum(d_pooled, 0, keepdims=True)
    u_text = d_each * g2
    u_text = u_text - jnp.mean(u_text, 1, keepdims=True)
    u_high, u_low = split_two(u_text)
    u_both = jnp.concatenate([u_high, u_low], 0)
    y_copy.wait()

    for i in range(4):
        rows = pl.ds(i * 256, 256)
        part = members[:, 256 * i : 256 * i + 256]
        u = dg(jnp.concatenate([part, part], 0), u_both, 0, 0)
        n = n2[rows, :]
        d = (u - n * jnp.mean(u * n, 1, keepdims=True)) * scales[rows, 64:65]
        n2[rows, :] = d
        db = d.astype(BF)
        df[rows, :] = db
        vg[3:4, :] += jnp.sum(db.astype(F32), 0, keepdims=True)

    def small_ring(i):
        return i % 2

    def long_ring(i):
        return i % 4

    ch_x, ch_y, ch_d = chip ^ 1, chip ^ 2, chip ^ 3
    inner = (((rep + 1) >> 1) & 1) == 1
    outer = jnp.logical_not(inner)

    def view_s(i):
        (u, w), s = chunk_shape(i), small_ring(i)
        src = c_s.at[s, :, pl.ds(1 - core, 1), pl.ds(0, u), pl.ds(0, w)]
        dst = rsib.at[s, :, :, pl.ds(0, u), pl.ds(0, w)]
        return remote(src, dst, xsend.at[s, 0], xrecv.at[s, 0], dev_s)

    def views_x1(i):
        (u, w), s, a = chunk_shape(i), long_ring(i), i % ACCS
        half = u // 2
        low, high, cols = pl.ds(0, half), pl.ds(half, half), pl.ds(0, w)
        pieces = (
            (ch_x, low, rx.at[s, 0, low, cols], dev_x),
            (ch_d, low, rx.at[s, 1, low, cols], dev_x),
            (ch_y, high, ry.at[s, 0, low, cols], dev_y),
            (ch_d, high, ry.at[s, 1, low, cols], dev_y),
        )
        return [
            remote(acc.at[a, who, rows, cols], dst, xsend.at[s, 1 + n], xrecv.at[s, 1 + n], dev)
            for n, (who, rows, dst, dev) in enumerate(pieces)
        ]

    def views_x2(i):
        (u, w), s, a = chunk_shape(i), long_ring(i), i % ACCS
        half = u // 2
        low, high, cols = pl.ds(0, half), pl.ds(half, half), pl.ds(0, w)
        return [
            remote(acc.at[a, ch_y, low, cols], ry2.at[s, low, cols], xsend.at[s, 5], xrecv.at[s, 5], dev_y),
            remote(acc.at[a, ch_x, high, cols], rx2.at[s, low, cols], xsend.at[s, 6], xrecv.at[s, 6], dev_x),
        ]

    def view_z1(i):
        (u, w), s = chunk_shape(i), long_ring(i)
        rows, cols = pl.ds(0, u), pl.ds(0, w)
        return remote(
            zs.at[s, rows, cols], rz1.at[s, rows, cols], xsend.at[s, 7], xrecv.at[s, 7], dev_z1
        )

    def view_z2(i):
        (u, w), s = chunk_shape(i), long_ring(i)
        rows, cols = pl.ds(0, u), pl.ds(0, w)
        return remote(
            zs.at[s, rows, cols], rz2.at[s, rows, cols], xsend.at[s, 8], xrecv.at[s, 8], dev_z3
        )

    def view_z3(i):
        u, w = chunk_shape(i)
        place = fin.at[i, pl.ds(0, u), pl.ds(0, w)]
        return remote(place, place, fsend.at[i], frecv.at[i], dev_z1)

    def stage_x1(i):
        (u, w), s, a = chunk_shape(i), small_ring(i), i % ACCS
        view_s(i).wait()
        for ch in range(4):
            acc[a, ch, 0:u, 0:w] = c_s[s, ch, pl.ds(core, 1), 0:u, 0:w][0] + rsib[s, ch, 0, 0:u, 0:w]
        for copy in views_x1(i):
            copy.start()

    def stage_x2(i):
        (u, w), s, a = chunk_shape(i), long_ring(i), i % ACCS
        half = u // 2
        for copy in views_x1(i):
            copy.wait()
        acc[a, pl.ds(ch_y, 1), 0:half, 0:w] += rx[s, 1:2, 0:half, 0:w]
        acc[a, pl.ds(ch_x, 1), half:u, 0:w] += ry[s, 1:2, 0:half, 0:w]
        for copy in views_x2(i):
            copy.start()
        acc[a, pl.ds(chip, 1), 0:half, 0:w] += rx[s, 0:1, 0:half, 0:w]
        acc[a, pl.ds(chip, 1), half:u, 0:w] += ry[s, 0:1, 0:half, 0:w]

    def stage_z1(i):
        (u, w), s, a = chunk_shape(i), long_ring(i), i % ACCS
        half = u // 2
        for copy in views_x2(i):
            copy.wait()
        zs[s, 0:half, 0:w] = acc[a, pl.ds(chip, 1), 0:half, 0:w][0] + ry2[s, 0:half, 0:w]
        zs[s, half:u, 0:w] = acc[a, pl.ds(chip, 1), half:u, 0:w][0] + rx2[s, 0:half, 0:w]

        @pl.when(outer)
        def _():
            view_z1(i).start()

    def stage_z2(i):
        (u, w), s = chunk_shape(i), long_ring(i)

        @pl.when(outer)
        def _():
            view_z1(i).wait_send()

        @pl.when(inner)
        def _():
            view_z1(i).wait_recv()
            zs[s, 0:u, 0:w] += rz1[s, 0:u, 0:w]
            view_z2(i).start()

    def stage_z3(i):
        (u, w), s = chunk_shape(i), long_ring(i)

        @pl.when(inner)
        def _():
            view_z2(i).wait()
            fin[i, 0:u, 0:w] = zs[s, 0:u, 0:w] + rz2[s, 0:u, 0:w]
            view_z3(i).start()

    def out_copy(i):
        u, w = chunk_shape(i)
        rows, cols = pl.ds(0, u), pl.ds(0, w)
        return pltpu.make_async_copy(fin.at[i, rows, cols], out_grads.at[i, rows, cols], osem.at[2 + i])

    def stage_end(i):
        @pl.when(inner)
        def _():
            view_z3(i).wait_send()

        @pl.when(outer)
        def _():
            view_z3(i).wait_recv()

        out_copy(i).start()

    def store_slabs(i, hh, result):
        (u, w), s = chunk_shape(i), small_ring(i)
        for k in range(4):
            c_s[s, pl.ds(2 * hh + k // 2, 1), k % 2, 0:u, 0:w] = (
                result[u * k : u * k + u].astype(BF).reshape(1, u, w)
            )

    def chunk(i, left_of, right):
        def half(hh, carry):
            store_slabs(i, hh, dg(left_of(hh), right(), 0, 0))
            return carry

        lax.fori_loop(0, 2, half, 0)

    def down_chunk(i, j):
        def left_of(hh):
            return jnp.concatenate(
                [g_s[:, aligned((4 * hh + k) * 384 + j * 128, 128, 128)] for k in range(4)], 1
            )

        chunk(i, left_of, lambda: df[...])

    def slope(j):
        cols = pl.ds(D * j, D)

        def slope_step(m, carry):
            rows = aligned(m * 512, 512, 512)
            dz = (dg(df[rows, :], wdn[cols, :], 1, 1) * gp[rows, cols].astype(F32)).astype(BF)
            gp[rows, cols] = dz
            vg[8 + j : 9 + j, :] += jnp.sum(dz.astype(F32), 0, keepdims=True)
            return carry

        lax.fori_loop(0, 2, slope_step, 0)

    def up_chunk(i, j):
        chunk(i, lambda hh: h1b[:, aligned(384 * hh, 384, 128)], lambda: gp[:, pl.ds(D * j, D)])

    def first_step(i, carry):
        rows = aligned(i * 256, 256, 256)
        dh = n2[rows, :] + dg(gp[rows, :], wup[...], 1, 1)
        n = n1[rows, :]
        vg[4:5, :] += jnp.sum(dh * n, 0, keepdims=True)
        vg[5:6, :] += jnp.sum(dh, 0, keepdims=True)
        u = dh * g1
        d = (u - jnp.mean(u, 1, keepdims=True) - n * jnp.mean(u * n, 1, keepdims=True)) * scales[rows, 0:1]
        n2[rows, :] = d
        db = d.astype(BF)
        df[rows, :] = db
        vg[2:3, :] += jnp.sum(db.astype(F32), 0, keepdims=True)
        return carry

    def out_chunk(i):
        chunk(i, lambda hh: ao[:, aligned(384 * hh, 384, 128)], lambda: df[...])

    def mask_place(r, b):
        m = 2 * r + b
        return pl.ds(384 * (m // 3), 384), pl.ds(256 * (m % 3), 256)

    def place_masks():
        segment_columns()
        for r in range(2):
            for b in range(2):
                key_side = lse[pl.ds(r * ROW + 128 * b, 384), 0:1]
                query_side = segf[r : r + 1, 256 * b : 256 * b + 256]
                n1[mask_place(r, b)] = jnp.where(key_side == query_side, 0.0, NEG)

    head = lax.broadcasted_iota(jnp.int32, (D, 128), 0) // HD
    head_lane = lax.broadcasted_iota(jnp.int32, (D, 128), 1)
    one_hot = jnp.where(head_lane == head // 2 + 8 * (head % 2), 1.0, 0.0).astype(BF)

    def mix_step(m, carry):
        rows = aligned(m * 512, 512, 512)
        da = dg(df[rows, :], wo[...], 1, 1).astype(BF)
        high, low = split_two(da.astype(F32) * ao[rows, :].astype(F32))
        dots = dg(high, one_hot, 1, 0) + dg(low, one_hot, 1, 0)
        dot_t[:, rows] = dots.T[0:16]
        ao[rows, :] = da
        return carry

    def mix():
        place_masks()
        lax.fori_loop(0, 2, mix_step, 0)

    def attend_back(r, pair, at):
        grads_k, grads_v = [], []
        for b in range(2):
            kq = aligned(r * ROW + 128 * b, 384, 128)
            qq = aligned(r * ROW + 256 * b, 256, 256)
            k = qkv[kq, aligned(at + 256, 128, 128)]
            v = qkv[kq, aligned(at + 512, 128, 128)]
            q = qkv[qq, aligned(at, 128, 128)]
            da = ao[qq, aligned(pair * 128, 128, 128)]
            scores = dg(both(k), q, 1, 1)
            dp = dg(both(v), da, 1, 1)
            bias = n1[mask_place(r, b)]
            probs, dscores = [], []
            for h in range(2):
                rows = slice(384 * h, 384 * h + 384)
                prob = jnp.exp(scores[rows] + bias - lse_t[pair + 8 * h : pair + 8 * h + 1, qq])
                probs.append(prob.astype(BF))
                dscores.append((prob * (dp[rows] - dot_t[pair + 8 * h : pair + 8 * h + 1, qq])).astype(BF))
            grads_v.append(dg(jnp.concatenate(probs, 1), both(da), 1, 0))
            grads_k.append(dg(jnp.concatenate(dscores, 1), both(q), 1, 0))
            even_q, odd_q = dg(k, dscores[0], 0, 0), dg(k, dscores[1], 0, 0)
            dq = jnp.concatenate([even_q[0:HD], odd_q[HD : 2 * HD]], 0).T
            g_s[qq, aligned(at, 128, 128)] = (dq * 0.125).astype(BF)
        for off, (first, second) in ((256, grads_k), (512, grads_v)):
            cols = aligned(at + off, 128, 128)
            g_s[aligned(r * ROW, 128, 128), cols] = first[0:128].astype(BF)
            g_s[aligned(r * ROW + 128, 256, 128), cols] = (first[128:384] + second[0:256]).astype(BF)
            g_s[aligned(r * ROW + 384, 128, 128), cols] = second[256:384].astype(BF)

    def heads(pair):
        def back_step(r, carry):
            attend_back(r, pair, D * (pair // 2) + 128 * (pair % 2))
            return carry

        lax.fori_loop(0, 2, back_step, 0, unroll=True)

    def group_chunk(i, group):
        def right():
            if group < 2:
                return g_s[:, pl.ds(D * group, D)]
            first = 2 * D + 128 * (group - 2)
            return jnp.concatenate([g_s[:, pl.ds(first + 256 * n, 128)] for n in range(3)], 1)

        chunk(i, lambda hh: x_s[:, aligned(384 * hh, 384, 128)], right)

    def vector_sums():
        for row, off in ((0, 0), (1, 512)):
            for group in range(3):
                vg[row : row + 1, 256 * group : 256 * group + 256] = jnp.sum(
                    g_s[:, pl.ds(D * group + off, 256)].astype(F32), 0, keepdims=True
                )
        v_copy(0).start()

    order = (dev_s, dev_x, dev_y, dev_z1, dev_z2)

    def v_copy(n):
        return remote(vg, vr.at[n], vsend.at[n], vrecv.at[n], order[n])

    def v_step(n):
        v_copy(n).wait()
        vg[...] = vg[...] + vr[n]
        if n + 1 < len(order):
            v_copy(n + 1).start()

    def token_step(i, carry):
        rows = aligned(i * 256, 256, 256)
        h1b[rows, :] = (n2[rows, :] + dg(g_s[rows, pl.ds(0, 3 * D)], wqkv[...], 1, 1)).astype(BF)
        return carry

    dx_copy = pltpu.make_async_copy(h1b, out_dx, osem.at[1])

    numbers = {name: i for i, name in enumerate(CHUNK_NAMES)}
    stages = {
        X1: stage_x1,
        X2: stage_x2,
        Z1: stage_z1,
        Z2: stage_z2,
        Z3: stage_z3,
        END: stage_end,
        SHARE: v_step,
        SLOPE: slope,
        HEADS: heads,
    }
    for kind, n in BACK:
        if kind in stages:
            stages[kind](n)
        elif kind == SEND:
            view_s(n).start()
        elif kind == DOWN:
            down_chunk(numbers[kind, n], n)
        elif kind == UP:
            up_chunk(numbers[kind, n], n)
        elif kind == OUT:
            out_chunk(numbers[kind, n])
        elif kind == GROUP:
            group_chunk(numbers[kind, n], n)
        elif kind == FIRST:
            lax.fori_loop(n, n + 1, first_step, 0)
        elif kind == MIX:
            mix()
        elif kind == SUMS:
            vector_sums()
        elif kind == TOKEN:
            lax.fori_loop(n, n + 1, token_step, 0)
            if n == 3:
                dx_copy.start()

    out_vec[8:16, 0:128] = jnp.zeros((8, 128), F32)
    for k in range(8):

        @pl.when(f == k)
        def _():
            out_vec[0:8, 0:96] = vg[0:8, 96 * k : 96 * k + 96]
            line = jnp.concatenate([vg[8 + n : 9 + n, :] for n in range(4)], 1)
            out_vec[8:9, 0:384] = line[:, 384 * k : 384 * k + 384]

    dx_copy.wait()
    for i in range(NCHUNK):
        out_copy(i).wait()


def finish_kernel(
    raw_y,
    raw_dx,
    raw_grads,
    vec,
    out_y,
    out_dx,
    out_gq,
    out_gk,
    out_gv,
    out_go,
    out_gup,
    out_gdn,
    *rest,
):
    vectors = rest[:9]
    y, dx, grads, gq, gk, gv, go, gup, gdn, sems = rest[9:19]
    rows, small = rest[19:], []
    reads = [(raw_y, y), (raw_dx, dx), (raw_grads, grads)]
    reads = [pltpu.make_async_copy(src, dst, sems.at[i]) for i, (src, dst) in enumerate(reads)]
    writes = [(gq, out_gq), (gk, out_gk), (gv, out_gv), (go, out_go), (gup, out_gup), (gdn, out_gdn)]
    writes = [(y, out_y), (dx, out_dx)] + writes
    writes = [pltpu.make_async_copy(src, dst, sems.at[3 + i]) for i, (src, dst) in enumerate(writes)]
    for copy in reads:
        copy.start()
    for n, row in enumerate((0, 1, 2, 8, 3, 4, 5, 6, 7)):
        if row == 8:
            for k in range(3):
                rows[n][k : k + 1, :] = vec[8:9, 128 * k : 128 * k + 128]
        else:
            rows[n][...] = vec[row : row + 1, 0:96]
        small.append(pltpu.make_async_copy(rows[n], vectors[n], sems.at[11 + n]))
        small[-1].start()
    for n in range(2):
        reads[n].wait()
        writes[n].start()
    reads[2].wait()
    for i, (kind, j) in enumerate(CHUNK_NAMES):
        if kind == DOWN:
            gdn[128 * j : 128 * j + 128, :] = grads[i].astype(F32)
        elif kind == UP:
            gup[:, D * j : D * j + D] = grads[i, 0:96].astype(F32)
        elif kind == OUT:
            go[...] = grads[i, 0:96].astype(F32)
        else:
            first, width = (256 * j, 256) if j < 2 else (512 + 128 * (j - 2), 128)
            for n, ref in enumerate((gq, gk, gv)):
                ref[:, first : first + width] = grads[i, 0:96, width * n : width * n + width].astype(F32)
    for copy in writes[2:]:
        copy.start()
    for copy in writes + small:
        copy.wait()


def finish_call(raw_y, raw_dx, grads, vec):
    shape = jax.ShapeDtypeStruct
    any_ = pl.BlockSpec(memory_space=pl.ANY)
    vmem = pl.BlockSpec(memory_space=pltpu.VMEM)
    shapes = ((1, 96),) * 3 + ((3, 128),) + ((1, 96),) * 5
    weights = ((96, D), (96, D), (96, D), (96, D), (96, FF), (384, D))
    return pl.pallas_call(
        finish_kernel,
        name="write_results",
        out_shape=(shape((T, D), BF), shape((T, D), BF))
        + tuple(shape(dims, F32) for dims in weights)
        + tuple(shape(dims, F32) for dims in shapes),
        in_specs=[any_, any_, any_, vmem],
        out_specs=(any_,) * 17,
        scratch_shapes=[pltpu.VMEM((T, D), BF), pltpu.VMEM((T, D), BF), pltpu.VMEM((NCHUNK, 128, D), BF)]
        + [pltpu.VMEM(dims, F32) for dims in weights]
        + [pltpu.SemaphoreType.DMA((20,))]
        + [pltpu.VMEM(dims, F32) for dims in shapes],
        compiler_params=pltpu.CompilerParams(vmem_limit_bytes=60 * 2**20),
    )(raw_y, raw_dx, grads, vec)


def fused_call(tokens, seg, pairing, vectors, shards):
    vm = lambda shape, dtype: pltpu.VMEM(shape, dtype)
    sem = pltpu.SemaphoreType.DMA
    scratch = [
        vm((T, D), BF),
        vm((D, 3 * D), BF),
        vm((D, D), BF),
        vm((D, FF), BF),
        vm((FF, D), BF),
        vm((8, 16, 128), F32),
        vm((8, D), F32),
        vm((8, FF), F32),
        vm((T, 3 * D), BF),
        vm((T, 128), BF),
        vm((T, 128), BF),
        vm((T, 128), F32),
        vm((16, T), F32),
        vm((16, T), F32),
        vm((T, D), BF),
        vm((T, D), F32),
        vm((T, 128), F32),
        vm((T, D), BF),
        vm((T, FF), BF),
        vm((T, FF), BF),
        vm((T, D), F32),
        vm((T, D), BF),
        vm((16, D), F32),
        vm((8, 512), F32),
        vm((2, 4, 2, 128, D), BF),
        vm((2, 4, 1, 128, D), BF),
        vm((ACCS, 4, 128, D), BF),
        vm((4, 2, 64, D), BF),
        vm((4, 2, 64, D), BF),
        vm((4, 64, D), BF),
        vm((4, 64, D), BF),
        vm((4, 128, D), BF),
        vm((4, 128, D), BF),
        vm((4, 128, D), BF),
        vm((NCHUNK, 128, D), BF),
        vm((16, D), F32),
        vm((5, 16, D), F32),
        sem((GROUPS, 14)),
        sem((GROUPS, 14)),
        sem((13,)),
        sem((7,)),
        sem((7,)),
        sem((22,)),
        sem((22,)),
        sem((4, 9)),
        sem((4, 9)),
        sem((NCHUNK,)),
        sem((NCHUNK,)),
        sem((5,)),
        sem((5,)),
        sem((2 + NCHUNK,)),
    ]
    shape = jax.ShapeDtypeStruct
    any_ = pl.BlockSpec(memory_space=pl.ANY)
    vmem = pl.BlockSpec(memory_space=pltpu.VMEM)
    return pl.pallas_call(
        fused_kernel,
        name="layer_step",
        out_shape=(
            shape((T, D), BF),
            shape((T, D), BF),
            shape((NCHUNK, 128, D), BF),
            shape((16, 384), F32),
        ),
        in_specs=[any_, vmem, vmem] + [vmem] * 9 + [any_] * 6,
        out_specs=(any_,) * 3 + (vmem,),
        scratch_shapes=scratch,
        compiler_params=pltpu.CompilerParams(
            collective_id=0, has_side_effects=True, vmem_limit_bytes=64 * 2**20
        ),
        cost_estimate=pl.CostEstimate(
            flops=60 * 10**9, bytes_accessed=30 * 2**20, transcendentals=10**7
        ),
    )(tokens, seg, pairing, *vectors, *shards[:6])


def local_fused(tokens, segment_ids, pairing, *shards):
    width = tokens.shape[-1]
    (bq, bv, bo, bup, bdn, g1, s1, g2, s2) = shards[6:]
    vectors = [piece.reshape(1, -1) for piece in (bq, bv, bo, bdn, g1, s1, g2, s2)]
    vectors.append(bup.reshape(3, 128))
    raw = fused_call(tokens.reshape(-1, width), segment_ids, pairing.reshape(1, -1), vectors, shards)
    results = finish_call(*raw)
    return (
        (results[0].reshape(tokens.shape), results[1].reshape(tokens.shape))
        + tuple(results[2:8])
        + tuple(piece.reshape(-1) for piece in results[8:])
    )


def norm_piece(residual, gain_vector, shift_vector):
    centre = jnp.mean(residual, -1, keepdims=True)
    offset = residual - centre
    spread = jnp.mean(offset * offset, -1, keepdims=True)
    return offset * lax.rsqrt(spread + 1e-12) * gain_vector + shift_vector


def gelu_exact(argument):
    return jax.nn.gelu(argument, approximate=False)


def pool_texts(layer_out, segments):
    member = (segments[:, None] == jnp.arange(SEGS)[None, :]).astype(jnp.float32)
    totals = jnp.dot(member.T, layer_out, precision=lax.Precision.HIGHEST)
    counts = jnp.sum(member, 0)
    pooled = totals / counts[:, None]
    return pooled * lax.rsqrt(jnp.sum(pooled * pooled, -1, keepdims=True) + 1e-06)


def project(inputs, weight, bias_vector):
    return jnp.dot(inputs, weight, preferred_element_type=jnp.float32) + bias_vector.astype(
        jnp.float32
    )


def head_scores(query_states, key_states, segments):
    row_length = query_states.shape[0]
    scores = jnp.einsum(
        "qhd,khd->hqk",
        query_states.reshape(row_length, H, HD),
        key_states.reshape(row_length, H, HD),
        preferred_element_type=jnp.float32,
    ) * HD ** (-0.5)
    same_text = segments[:, None] == segments[None, :]
    return jnp.where(same_text[None], scores, -1e30)


def attend_forward(pieces):
    query_states, key_states, value_states, segments = pieces
    row_length = query_states.shape[0]
    scores = head_scores(query_states, key_states, segments)
    row_peak = jnp.max(scores, -1, keepdims=True)
    exponent = jnp.exp(scores - row_peak)
    row_total = jnp.sum(exponent, -1, keepdims=True)
    probability = (exponent / row_total).astype(jnp.bfloat16)
    mixture = jnp.einsum(
        "hqk,khd->qhd",
        probability,
        value_states.reshape(row_length, H, HD),
        preferred_element_type=jnp.float32,
    )
    return (mixture.reshape(row_length, H * HD).astype(jnp.bfloat16), row_peak + jnp.log(row_total))


def attend_backward(pieces):
    query_states, key_states, value_states, segments, grad_mixture, log_total = pieces
    row_length = query_states.shape[0]
    query_heads = query_states.reshape(row_length, H, HD)
    key_heads = key_states.reshape(row_length, H, HD)
    value_heads = value_states.reshape(row_length, H, HD)
    grad_heads = grad_mixture.reshape(row_length, H, HD)
    probability = jnp.exp(head_scores(query_states, key_states, segments) - log_total)
    grad_probability = jnp.einsum(
        "qhd,khd->hqk", grad_heads, value_heads, preferred_element_type=jnp.float32
    )
    grad_values = jnp.einsum(
        "hqk,qhd->khd",
        probability.astype(jnp.bfloat16),
        grad_heads,
        preferred_element_type=jnp.float32,
    )
    grad_scores = probability * (
        grad_probability - jnp.sum(probability * grad_probability, -1, keepdims=True)
    )
    grad_scores = grad_scores.astype(jnp.bfloat16)
    score_scale = HD ** (-0.5)
    grad_queries = (
        jnp.einsum("hqk,khd->qhd", grad_scores, key_heads, preferred_element_type=jnp.float32)
        * score_scale
    )
    grad_keys = (
        jnp.einsum("hqk,qhd->khd", grad_scores, query_heads, preferred_element_type=jnp.float32)
        * score_scale
    )
    return (
        grad_queries.reshape(row_length, H * HD).astype(jnp.bfloat16),
        grad_keys.reshape(row_length, H * HD).astype(jnp.bfloat16),
        grad_values.reshape(row_length, H * HD).astype(jnp.bfloat16),
    )


def run_layer(tokens, params, segment_ids):
    (
        query_weight,
        key_weight,
        value_weight,
        out_weight,
        up_weight,
        down_weight,
        query_bias,
        value_bias,
        out_bias,
        up_bias,
        down_bias,
        first_gain,
        first_shift,
        second_gain,
        second_shift,
    ) = params
    row_count, row_length, feature_width = tokens.shape
    flat_tokens = tokens.reshape(row_count * row_length, feature_width)
    query_states = project(flat_tokens, query_weight, query_bias).astype(jnp.bfloat16)
    key_states = jnp.dot(flat_tokens, key_weight, preferred_element_type=jnp.float32).astype(
        jnp.bfloat16
    )
    value_states = project(flat_tokens, value_weight, value_bias).astype(jnp.bfloat16)
    row_shape = (row_count, row_length, feature_width)
    joined, log_total = lax.map(
        attend_forward,
        (
            query_states.reshape(row_shape),
            key_states.reshape(row_shape),
            value_states.reshape(row_shape),
            segment_ids,
        ),
    )
    joined = joined.reshape(row_count * row_length, feature_width)
    resid_one = flat_tokens.astype(jnp.float32) + project(joined, out_weight, out_bias)
    hidden = norm_piece(resid_one, first_gain.astype(jnp.float32), first_shift.astype(jnp.float32))
    expanded = project(hidden.astype(jnp.bfloat16), up_weight, up_bias)
    active = gelu_exact(expanded).astype(jnp.bfloat16)
    resid_two = hidden + project(active, down_weight, down_bias)
    output = norm_piece(
        resid_two, second_gain.astype(jnp.float32), second_shift.astype(jnp.float32)
    )
    return (
        flat_tokens,
        query_states,
        key_states,
        value_states,
        joined,
        log_total,
        resid_one,
        hidden,
        expanded,
        active,
        resid_two,
        output,
    )


def gather_all(shards):
    packed = jnp.concatenate([piece.reshape(-1) for piece in shards])
    gathered = lax.all_gather(packed, "fsdp", axis=0, tiled=True)
    gathered = gathered.reshape(-1, packed.size)
    params, at = [], 0
    for piece in shards:
        part = gathered[:, at : at + piece.size]
        params.append(part.reshape((-1,) + piece.shape[1:]))
        at += piece.size
    return tuple(params)


def reduce_all(grad_params):
    group = lax.axis_size("fsdp")
    packed = jnp.concatenate(
        [piece.astype(jnp.bfloat16).reshape(group, -1) for piece in grad_params], 1
    )
    share = lax.psum_scatter(packed.reshape(-1), "fsdp", scatter_dimension=0, tiled=True)
    total = lax.psum(share, "rep").astype(jnp.float32)
    totals, at = [], 0
    for piece in grad_params:
        count = piece.size // group
        shape = (piece.shape[0] // group,) + piece.shape[1:]
        totals.append(total[at : at + count].reshape(shape))
        at += count
    return tuple(totals)


def local(
    tokens,
    segment_ids,
    pairing,
    query_weight,
    key_weight,
    value_weight,
    out_weight,
    up_weight,
    down_weight,
    query_bias,
    value_bias,
    out_bias,
    up_bias,
    down_bias,
    first_gain,
    first_shift,
    second_gain,
    second_shift,
):
    shards = (
        query_weight,
        key_weight,
        value_weight,
        out_weight,
        up_weight,
        down_weight,
        query_bias,
        value_bias,
        out_bias,
        up_bias,
        down_bias,
        first_gain,
        first_shift,
        second_gain,
        second_shift,
    )
    params = gather_all(shards)
    row_count, row_length, feature_width = tokens.shape
    states = run_layer(tokens, params, segment_ids)
    output = states[11].reshape(row_count, row_length, feature_width)

    def embed_rows(layer_out):
        return jax.vmap(pool_texts)(layer_out, segment_ids)

    embedded, embed_pullback = jax.vjp(embed_rows, output)
    local_count = row_count * SEGS
    local_embed = embedded.reshape(local_count, feature_width).astype(jnp.bfloat16)
    everything = lax.all_gather(local_embed, ("rep", "fsdp"), axis=0, tiled=True)
    text_count = everything.shape[0]
    pair_count = text_count // 2
    local_ids = lax.axis_index(("rep", "fsdp")) * local_count + jnp.arange(
        local_count, dtype=jnp.int32
    )
    matches = pairing[None, :] == local_ids[:, None]
    position = jnp.sum(jnp.where(matches, jnp.arange(text_count, dtype=jnp.int32)[None, :], 0), 1)
    pair_index = position // 2
    query_flag = position % 2 == 0
    passages = everything[pairing[1::2]]
    logits = (
        jnp.einsum("td,pd->tp", local_embed, passages, preferred_element_type=jnp.float32) * 100.0
    )
    row_peak = jnp.max(logits, 1, keepdims=True)
    exponent = jnp.exp(logits - row_peak)
    softmax_rows = exponent / jnp.sum(exponent, 1, keepdims=True)
    pairs = jnp.arange(pair_count, dtype=jnp.int32)[None, :]
    target = (pairs == pair_index[:, None]).astype(jnp.float32)
    queries = everything[pairing[0::2]]
    whole = jnp.einsum("qd,pd->qp", queries, passages, preferred_element_type=jnp.float32) * 100.0
    peak_all = jnp.max(whole, 1)
    total_all = jnp.sum(jnp.exp(whole - peak_all[:, None]), 1)
    cross = jnp.einsum("td,qd->tq", local_embed, queries, preferred_element_type=jnp.float32) * 100.0
    softmax_columns = jnp.exp(cross - peak_all[None, :]) / total_all[None, :]
    scaled_rows = ((softmax_rows - target) * 100.0).astype(jnp.bfloat16)
    scaled_columns = ((softmax_columns - target) * 100.0).astype(jnp.bfloat16)
    grad_query = jnp.einsum("tp,pd->td", scaled_rows, passages, preferred_element_type=jnp.float32)
    grad_passage = jnp.einsum(
        "tq,qd->td", scaled_columns, queries, preferred_element_type=jnp.float32
    )
    grad_embed = jnp.where(query_flag[:, None], grad_query, grad_passage)
    (grad_output,) = embed_pullback(grad_embed.reshape(row_count, SEGS, feature_width))
    flat_tokens, query_states, key_states, value_states, joined, log_total = states[:6]
    resid_one, hidden, expanded, active, resid_two = states[6:11]
    w_query_full, w_key_full, w_value_full, w_out_full, w_up_full, w_down_full = params[:6]
    first_gain_f = params[11].astype(jnp.float32)
    first_shift_f = params[12].astype(jnp.float32)
    second_gain_f = params[13].astype(jnp.float32)
    second_shift_f = params[14].astype(jnp.float32)
    token_total = row_count * row_length
    norm_out, second_pullback = jax.vjp(norm_piece, resid_two, second_gain_f, second_shift_f)
    grad_resid_two, grad_second_gain, grad_second_shift = second_pullback(
        grad_output.reshape(token_total, feature_width)
    )
    grad_feed = grad_resid_two.astype(jnp.bfloat16)
    grad_down_weight = jnp.einsum(
        "nf,nd->fd", active, grad_feed, preferred_element_type=jnp.float32
    )
    grad_down_bias = jnp.sum(grad_feed.astype(jnp.float32), 0)
    grad_active = jnp.einsum(
        "nd,fd->nf", grad_feed, w_down_full, preferred_element_type=jnp.float32
    )
    gelu_out, gelu_pullback = jax.vjp(gelu_exact, expanded)
    grad_expanded = gelu_pullback(grad_active)[0].astype(jnp.bfloat16)
    grad_up_weight = jnp.einsum(
        "nd,nf->df", hidden.astype(jnp.bfloat16), grad_expanded, preferred_element_type=jnp.float32
    )
    grad_up_bias = jnp.sum(grad_expanded.astype(jnp.float32), 0)
    grad_hidden = grad_resid_two + jnp.einsum(
        "nf,df->nd", grad_expanded, w_up_full, preferred_element_type=jnp.float32
    )
    hidden_out, first_pullback = jax.vjp(norm_piece, resid_one, first_gain_f, first_shift_f)
    grad_resid_one, grad_first_gain, grad_first_shift = first_pullback(grad_hidden)
    grad_branch = grad_resid_one.astype(jnp.bfloat16)
    grad_out_weight = jnp.einsum(
        "nd,ne->de", joined, grad_branch, preferred_element_type=jnp.float32
    )
    grad_out_bias = jnp.sum(grad_branch.astype(jnp.float32), 0)
    grad_joined = jnp.einsum(
        "ne,de->nd", grad_branch, w_out_full, preferred_element_type=jnp.float32
    ).astype(jnp.bfloat16)
    row_shape = (row_count, row_length, feature_width)
    grad_queries, grad_keys, grad_values = lax.map(
        attend_backward,
        (
            query_states.reshape(row_shape),
            key_states.reshape(row_shape),
            value_states.reshape(row_shape),
            segment_ids,
            grad_joined.reshape(row_shape),
            log_total,
        ),
    )
    grad_queries = grad_queries.reshape(token_total, feature_width)
    grad_keys = grad_keys.reshape(token_total, feature_width)
    grad_values = grad_values.reshape(token_total, feature_width)
    grad_query_weight = jnp.einsum(
        "nd,ne->de", flat_tokens, grad_queries, preferred_element_type=jnp.float32
    )
    grad_key_weight = jnp.einsum(
        "nd,ne->de", flat_tokens, grad_keys, preferred_element_type=jnp.float32
    )
    grad_value_weight = jnp.einsum(
        "nd,ne->de", flat_tokens, grad_values, preferred_element_type=jnp.float32
    )
    grad_query_bias = jnp.sum(grad_queries.astype(jnp.float32), 0)
    grad_value_bias = jnp.sum(grad_values.astype(jnp.float32), 0)
    grad_inputs = grad_resid_one
    grad_inputs = grad_inputs + jnp.einsum(
        "ne,de->nd", grad_queries, w_query_full, preferred_element_type=jnp.float32
    )
    grad_inputs = grad_inputs + jnp.einsum(
        "ne,de->nd", grad_keys, w_key_full, preferred_element_type=jnp.float32
    )
    grad_inputs = grad_inputs + jnp.einsum(
        "ne,de->nd", grad_values, w_value_full, preferred_element_type=jnp.float32
    )
    grad_params = (
        grad_query_weight,
        grad_key_weight,
        grad_value_weight,
        grad_out_weight,
        grad_up_weight,
        grad_down_weight,
        grad_query_bias,
        grad_value_bias,
        grad_out_bias,
        grad_up_bias,
        grad_down_bias,
        grad_first_gain,
        grad_first_shift,
        grad_second_gain,
        grad_second_shift,
    )
    totals = reduce_all(grad_params)
    return (
        output.astype(jnp.bfloat16),
        grad_inputs.reshape(row_shape).astype(jnp.bfloat16),
    ) + tuple(totals)


def solution(mesh):
    in_specs = (
        P(("rep", "fsdp"), None, None),
        P(("rep", "fsdp"), None),
        P(),
        P("fsdp", None),
        P("fsdp", None),
        P("fsdp", None),
        P("fsdp", None),
        P("fsdp", None),
        P("fsdp", None),
        P("fsdp"),
        P("fsdp"),
        P("fsdp"),
        P("fsdp"),
        P("fsdp"),
        P("fsdp"),
        P("fsdp"),
        P("fsdp"),
        P("fsdp"),
    )
    out_specs = (
        P(("rep", "fsdp"), None, None),
        P(("rep", "fsdp"), None, None),
        P("fsdp", None),
        P("fsdp", None),
        P("fsdp", None),
        P("fsdp", None),
        P("fsdp", None),
        P("fsdp", None),
        P("fsdp"),
        P("fsdp"),
        P("fsdp"),
        P("fsdp"),
        P("fsdp"),
        P("fsdp"),
        P("fsdp"),
        P("fsdp"),
        P("fsdp"),
    )

    def whole(*arrays):
        fits = (
            mesh.shape["fsdp"] == 8
            and mesh.shape["rep"] == 4
            and arrays[0].shape == (64, 512, 768)
            and arrays[7].shape == (768, 3072)
        )
        return jax.shard_map(
            local_fused if fits else local,
            mesh=mesh,
            in_specs=in_specs,
            out_specs=out_specs,
            check_vma=False,
        )(*arrays)

    return whole
```
